32 devices in a mesh: dp: 16 (over z, y, x), tensor: 2 (over core).
Axes of the slice: x: 2, y: 2, z: 4, core: 2. Of those that a mesh axis runs over, the one named last changes fastest.
Arguments:
- inputs: bfloat16 [4096, 2048], P(('dp', 'tensor')), may hold values from -6 to 6
- attention_gain: float32 [2048], replicated, may hold values from 0.5 to 1.5
- query_weight: bfloat16 [2048, 4096], P('dp', 'tensor'), may hold values from -0.125 to 0.125
- key_weight: bfloat16 [2048, 512], P('dp', 'tensor'), may hold values from -0.125 to 0.125
- value_weight: bfloat16 [2048, 512], P('dp', 'tensor'), may hold values from -0.125 to 0.125
- query_gain: float32 [128], replicated, may hold values from 0.5 to 1.5
- key_gain: float32 [128], replicated, may hold values from 0.5 to 1.5
- out_weight: bfloat16 [4096, 2048], P('tensor', 'dp'), may hold values from -0.75 to 0.75
- feedforward_gain: float32 [2048], replicated, may hold values from 0.5 to 1.5
- router_weight: bfloat16 [2048, 32], P('dp'), may hold values from -0.0625 to 0.0625
- gate_weight: bfloat16 [32, 2048, 768], P(('dp', 'tensor')), may hold values from -0.125 to 0.125
- up_weight: bfloat16 [32, 2048, 768], P(('dp', 'tensor')), may hold values from -0.125 to 0.125
- down_weight: bfloat16 [32, 768, 2048], P(('dp', 'tensor')), may hold values from -0.875 to 0.875
- routes: int32 [4096, 8], P(('dp', 'tensor')), may hold values from 0 to 31, all different within a row; in each aligned block of 128 rows (0 to 127, 128 to 255, ...) at most 44 rows name the same one
- cotangent: bfloat16 [4096, 2048], P(('dp', 'tensor')), may hold values from -6 to 6
Outputs:
- output: bfloat16 [4096, 2048], P(('dp', 'tensor'))
- grad_inputs: float32 [4096, 2048], P(('dp', 'tensor'))
- grad_attention_gain: float32 [2048], replicated
- grad_query_weight: float32 [2048, 4096], P('dp', 'tensor')
- grad_key_weight: float32 [2048, 512], P('dp', 'tensor')
- grad_value_weight: float32 [2048, 512], P('dp', 'tensor')
- grad_query_gain: float32 [128], replicated
- grad_key_gain: float32 [128], replicated
- grad_out_weight: float32 [4096, 2048], P('tensor', 'dp')
- grad_feedforward_gain: float32 [2048], replicated
- grad_router_weight: float32 [2048, 32], P('dp')
- grad_gate_weight: float32 [32, 2048, 768], P(('dp', 'tensor'))
- grad_up_weight: float32 [32, 2048, 768], P(('dp', 'tensor'))
- grad_down_weight: float32 [32, 768, 2048], P(('dp', 'tensor'))
The draws below stay inside these ranges and needn't reach their ends.
Inputs may be any that keep to these rules, and one draw needn't show every extreme that they name: `routes`: each row names 8 different experts; among the rows of one device (aligned blocks of 128 rows) no expert is named more than 44 times, and in every draw some expert is named exactly 44 times in some such block.
All inputs are finite; a program needn't handle non-finite values.
Results may differ from the reference program's by a relative error of at most 0.02.
Values may be sent and summed in bfloat16 or wider, within the bound.
No kernel may reach another device: no remote copies, remote signals or barrier semaphores. Data moves between devices by JAX's collectives and lax.ppermute only.
A program may use at most 256 MiB of HBM per device.

```python
import math
import jax
import jax.numpy as jnp
import numpy as np
from jax import lax

D = 2048
H = 32
KV = 4
HD = 128
EF = 768
TOPK = 8
TOK_DEV = 128
EXPERTS = 32
SEQ = 256
TOKENS = 4096
CAP = 44
N_DP = 16
N_TENSOR = 2


def level_of(key, shape, cuts, smallest, largest):
    loudness, own = 1.0, jax.random.fold_in(key, 6)
    for dim, blocks in cuts:
        steps = jnp.exp(jax.random.uniform(jax.random.fold_in(own, dim), (blocks,), jnp.float32, smallest / len(cuts), largest / len(cuts)))
        loudness = loudness * jnp.repeat(steps, shape[dim] // blocks).reshape([-1 if axis == dim else 1 for axis in range(len(shape))])
    return loudness


def shared_out(own_key, own, number, rows, count, top, most, slope):
    order = jax.random.permutation(own_key, count)
    crowded, common = shares(count, rows * top, most, slope, True), shares(count, rows * top, most, slope, False)
    places = jnp.arange(count)

    def named(tallies, rotation):
        used = int((tallies > 0).sum())
        fixed = max(1, used // 4)
        moved = fixed + (places - fixed + rotation * (used - fixed)) % max(1, count - fixed)
        return jnp.zeros((count,), jnp.int32).at[order[jnp.where(places < fixed, places, moved)]].set(jnp.asarray(tallies, jnp.int32))

    tallies = jnp.where(number % 4 == 0, named(crowded, number // 4), named(common, number - number // 4 - 1))
    mixed = jax.random.permutation(jax.random.fold_in(own, 3), count)
    giver, receiver = mixed[0:count // 2 * 2:2], mixed[1:count // 2 * 2:2]
    slack = jnp.minimum(tallies[giver] - 1, most - tallies[receiver]) // 2
    slack = jnp.where((giver == order[0]) | (receiver == order[0]) | (tallies[receiver] == 0), 0, jnp.maximum(slack, 0))
    moved = jax.random.randint(jax.random.fold_in(own, 4), (count // 2,), 0, 1 << 20) % (slack + 1)
    tallies = tallies.at[giver].add(-moved).at[receiver].add(moved)
    labels = jnp.searchsorted(jnp.cumsum(tallies), jnp.arange(rows * top), side="right").astype(jnp.int32)
    listing = labels.reshape(top, rows).T
    listing = listing[jax.random.permutation(jax.random.fold_in(own, 1), rows)]
    rotation = jax.random.randint(jax.random.fold_in(own, 2), (rows, 1), 0, top)
    return jnp.take_along_axis(listing, (jnp.arange(top)[None, :] + rotation) % top, axis=1)


def shares(count, total, bound, lean, full):
    loads = [(1 << 20) // math.isqrt(grade ** lean) + 1 for grade in range(1, count + 1)]
    largest = bound if full else min(bound, max(-(-total // count), total * loads[0] // sum(loads)))
    least = 1 if total - largest >= count - 1 else 0
    holding, rest = [largest] + [least] * (count - 1), total - largest - least * (count - 1)
    while rest > 0:
        free = [i for i in range(1, count) if holding[i] < largest] or [i for i in range(1, count) if holding[i] < bound]
        pool, budget = sum([loads[i] for i in free]), rest
        for i in free:
            extra = min(bound - holding[i], max(1, budget * loads[i] // pool), rest)
            holding[i] = holding[i] + extra
            rest = rest - extra
    return np.array(holding)


def bell_draw(own_key, extent, width, bound, cuts=(), held_as=jnp.bfloat16):
    factor_of = level_of(own_key, extent, cuts, -0.22, 0.18) if cuts else 1.0
    values = jax.random.normal(own_key, extent, jnp.float32) * width * factor_of
    return jnp.minimum(jnp.maximum(values, -bound), bound).astype(held_as)


def setup_inputs(seed: int = 0) -> dict:
    splits = jax.random.split(jax.random.key(seed), 16)
    inputs = bell_draw(splits[0], (TOKENS, D), 1.0, 6.0, ((0, 32),))
    attention_gain = jnp.clip(1.0 + 0.1 * jax.random.normal(splits[1], (D,), jnp.float32), 0.5, 1.5)
    query_weight = bell_draw(splits[2], (D, H * HD), D ** -0.5, 0.125, ((0, 16), (1, 2)))
    key_weight = bell_draw(splits[3], (D, KV * HD), D ** -0.5, 0.125, ((0, 16), (1, 2)))
    value_weight = bell_draw(splits[4], (D, KV * HD), D ** -0.5, 0.125, ((0, 16), (1, 2)))
    query_gain = jnp.clip(1.0 + 0.1 * jax.random.normal(splits[5], (HD,), jnp.float32), 0.5, 1.5)
    key_gain = jnp.clip(1.0 + 0.1 * jax.random.normal(splits[6], (HD,), jnp.float32), 0.5, 1.5)
    out_weight = bell_draw(splits[7], (H * HD, D), (H * HD // 64) ** -0.5, 0.75, ((0, 2), (1, 16)))
    feedforward_gain = jnp.clip(1.0 + 0.1 * jax.random.normal(splits[8], (D,), jnp.float32), 0.5, 1.5)
    router_weight = bell_draw(splits[9], (D, EXPERTS), (4 * D) ** -0.5, 0.0625, ((0, 16),))
    gate_weight = bell_draw(splits[10], (EXPERTS, D, EF), D ** -0.5, 0.125, ((0, 32),))
    up_weight = bell_draw(splits[11], (EXPERTS, D, EF), D ** -0.5, 0.125, ((0, 32),))
    down_weight = bell_draw(splits[12], (EXPERTS, EF, D), (EF // 16) ** -0.5, 0.875, ((0, 32),))
    routes_keys = jax.random.split(jax.random.fold_in(splits[13], 1), TOKENS // TOK_DEV)
    routes_turns = jax.random.permutation(jax.random.fold_in(splits[13], 3), TOKENS // TOK_DEV)
    routes = jax.vmap(lambda own, number: shared_out(jax.random.fold_in(splits[13], 2), own, number, TOK_DEV, EXPERTS, TOPK, CAP, 2))(routes_keys, routes_turns).reshape((TOKENS, TOPK))
    cotangent = bell_draw(splits[14], (TOKENS, D), 1.0, 6.0, ((0, 32),))
    return {"inputs": inputs, "attention_gain": attention_gain, "query_weight": query_weight, "key_weight": key_weight, "value_weight": value_weight, "query_gain": query_gain, "key_gain": key_gain, "out_weight": out_weight, "feedforward_gain": feedforward_gain, "router_weight": router_weight, "gate_weight": gate_weight, "up_weight": up_weight, "down_weight": down_weight, "routes": routes, "cotangent": cotangent}


EPS = 1e-06
THETA = 1000000.0
HIGH = lax.Precision.HIGHEST

@jax.custom_vjp
def low(v):
    return lax.optimization_barrier(v.astype(jnp.bfloat16)).astype(jnp.float32)

@jax.custom_vjp
def low_back(v):
    return v

def low_keep(v):
    return (low(v), None)

def low_pass(kept, grad):
    return (grad,)

def back_keep(v):
    return (v, None)

def back_low(kept, grad):
    return (low(grad),)
low.defvjp(low_keep, low_pass)
low_back.defvjp(back_keep, back_low)

def rms_scale(values, scales):
    inverse = lax.rsqrt(lax.optimization_barrier(jnp.mean(values * values, axis=-1, keepdims=True)) + EPS)
    return values * inverse * scales

def rope_tables(length, columns):
    halfway = columns // 2
    frequency = THETA ** (-(jnp.arange(halfway, dtype=jnp.float32) * 2.0 / columns))
    angles = jnp.arange(length, dtype=jnp.float32)[:, None] * frequency[None, :]
    return (jnp.cos(angles), jnp.sin(angles))

def head_prep(raw_rows, scales, cosine_table, sine_table):
    length = raw_rows.shape[0]
    columns = scales.shape[0]
    shaped = rms_scale(raw_rows.reshape(length, -1, columns), scales)
    halfway = columns // 2
    leading = shaped[..., :halfway]
    second = shaped[..., halfway:]
    cos_part = cosine_table[:, None, :]
    sin_part = sine_table[:, None, :]
    turned = jnp.concatenate([leading * cos_part - second * sin_part, second * cos_part + leading * sin_part], axis=-1)
    return turned.reshape(length, -1)

def attention_sequence(sequence, query_weight, key_weight, value_weight, query_gain, key_gain, out_weight):
    length = sequence.shape[0]
    query_raw = low_back(jnp.dot(sequence, query_weight, precision=HIGH))
    key_raw = low_back(jnp.dot(sequence, key_weight, precision=HIGH))
    value_raw = low_back(jnp.dot(sequence, value_weight, precision=HIGH))
    cosine_table, sine_table = rope_tables(length, HD)
    queries = low(head_prep(query_raw, query_gain, cosine_table, sine_table)).reshape(length, KV, H // KV, HD)
    key_rows = low(head_prep(key_raw, key_gain, cosine_table, sine_table)).reshape(length, KV, HD)
    value_rows = low(value_raw).reshape(length, KV, HD)
    scores = low_back(jnp.einsum('qkgd,ckd->kgqc', queries, key_rows, precision=HIGH) * HD ** (-0.5))
    places = jnp.arange(length, dtype=jnp.int32)
    allowed = places[None, :] <= places[:, None]
    attention_weights = jax.nn.softmax(jnp.where(allowed, scores, -1e+30), axis=-1)
    mixture = jnp.einsum('kgqc,ckd->qkgd', low(attention_weights), value_rows, precision=HIGH)
    attended = low(low_back(mixture.reshape(length, H * HD)))
    return low_back(jnp.dot(attended, out_weight, precision=HIGH))

def experts_sequence(normed_rows, route_rows, router_weight, gate_weight, up_weight, down_weight):
    count_rows = normed_rows.shape[0]
    logits = jnp.dot(normed_rows, router_weight, precision=HIGH)
    chosen = jnp.take_along_axis(logits, route_rows, axis=1)
    gate_values = jax.nn.softmax(chosen, axis=-1)
    flat_routes = route_rows.reshape(-1)
    onehot = (flat_routes[:, None] == jnp.arange(EXPERTS, dtype=jnp.int32)[None, :]).astype(jnp.int32)
    position = lax.optimization_barrier(jnp.sum((jnp.cumsum(onehot, axis=0) - onehot) * onehot, axis=1))
    slot_room = CAP * N_TENSOR
    slots = (flat_routes * slot_room + position).astype(jnp.int32)
    repeated = jnp.repeat(normed_rows, TOPK, axis=0)
    buffer = jnp.zeros((EXPERTS * slot_room, D), jnp.float32).at[slots].set(repeated)
    expert_rows = low_back(buffer).reshape(EXPERTS, slot_room, D)
    gate_pre = low_back(jnp.einsum('erd,edf->erf', expert_rows, gate_weight, precision=HIGH))
    up_pre = low_back(jnp.einsum('erd,edf->erf', expert_rows, up_weight, precision=HIGH))
    activated = low(jax.nn.silu(gate_pre) * up_pre)
    expert_out = low(low_back(jnp.einsum('erf,efd->erd', activated, down_weight, precision=HIGH)))
    picked = expert_out.reshape(EXPERTS * slot_room, D)[slots].reshape(count_rows, TOPK, D)
    return jnp.einsum('tk,tkd->td', gate_values, picked, precision=HIGH)

def reference(inputs, attention_gain, query_weight, key_weight, value_weight, query_gain, key_gain, out_weight, feedforward_gain, router_weight, gate_weight, up_weight, down_weight, routes, cotangent):

    def forward(inputs, attention_gain, query_weight, key_weight, value_weight, query_gain, key_gain, out_weight, feedforward_gain, router_weight, gate_weight, up_weight, down_weight):
        normed = low(rms_scale(inputs, attention_gain)).reshape(N_DP, SEQ, D)

        def attend(sequence):
            return attention_sequence(sequence, query_weight, key_weight, value_weight, query_gain, key_gain, out_weight)
        branch = lax.map(jax.checkpoint(attend), normed).reshape(TOKENS, D)
        hidden = inputs + branch
        moe_in = low(rms_scale(hidden, feedforward_gain)).reshape(N_DP, SEQ, D)

        def mix_experts(sequence_pair):
            return experts_sequence(sequence_pair[0], sequence_pair[1], router_weight, gate_weight, up_weight, down_weight)
        mixture = lax.map(jax.checkpoint(mix_experts), (moe_in, routes.reshape(N_DP, SEQ, TOPK))).reshape(TOKENS, D)
        return hidden + mixture
    floats = (inputs.astype(jnp.float32), attention_gain.astype(jnp.float32), query_weight.astype(jnp.float32), key_weight.astype(jnp.float32), value_weight.astype(jnp.float32), query_gain.astype(jnp.float32), key_gain.astype(jnp.float32), out_weight.astype(jnp.float32), feedforward_gain.astype(jnp.float32), router_weight.astype(jnp.float32), gate_weight.astype(jnp.float32), up_weight.astype(jnp.float32), down_weight.astype(jnp.float32))
    result, backward = jax.vjp(forward, *floats)
    grads = backward(cotangent.astype(jnp.float32))
    return (result.astype(jnp.bfloat16), grads[0], grads[1], grads[2], grads[3], grads[4], grads[5], grads[6], grads[7], grads[8], grads[9], grads[10], grads[11], grads[12])
```

```python
import functools
import math

import jax
import jax.numpy as jnp
from jax import lax
from jax.experimental import pallas as pl
from jax.experimental.pallas import tpu as pltpu
from jax.sharding import PartitionSpec as P

EPS = 1e-06
THETA = 1000000.0
HIGH = lax.Precision.HIGHEST
block_limit = 512


def rms_scale(values, scales):
    inverse = lax.rsqrt(jnp.mean(values * values, axis=-1, keepdims=True) + EPS)
    return values * inverse * scales


def rope_tables(length, columns):
    halfway = columns // 2
    frequency = THETA ** (-(jnp.arange(halfway, dtype=jnp.float32) * 2.0 / columns))
    angles = jnp.arange(length, dtype=jnp.float32)[:, None] * frequency[None, :]
    return (jnp.cos(angles), jnp.sin(angles))


def head_prep(raw_rows, scales, cosine_table, sine_table):
    length = raw_rows.shape[0]
    columns = scales.shape[0]
    shaped = rms_scale(raw_rows.reshape(length, -1, columns), scales)
    halfway = columns // 2
    leading = shaped[..., :halfway]
    second = shaped[..., halfway:]
    cos_part = cosine_table[:, None, :]
    sin_part = sine_table[:, None, :]
    turned = jnp.concatenate(
        [leading * cos_part - second * sin_part, second * cos_part + leading * sin_part], axis=-1
    )
    return turned.reshape(length, -1)


def masked_scores(offset, block_rows, queries, key_rows, score_scale):
    scores = (
        jnp.einsum("qkgd,ckd->kgqc", queries, key_rows, preferred_element_type=jnp.float32)
        * score_scale
    )
    row_places = offset + jnp.arange(block_rows, dtype=jnp.int32)
    key_places = jnp.arange(key_rows.shape[0], dtype=jnp.int32)
    allowed = key_places[None, :] <= row_places[:, None]
    return (queries, jnp.where(allowed, scores, -1e30))


def slot_layout(routes, expert_count, capacity):
    flat_routes = routes.reshape(-1)
    onehot = (flat_routes[:, None] == jnp.arange(expert_count, dtype=jnp.int32)[None, :]).astype(
        jnp.int32
    )
    position = jnp.sum((jnp.cumsum(onehot, axis=0) - onehot) * onehot, axis=1)
    return flat_routes * capacity + position


def route_rows(buffer):
    return lax.all_to_all(buffer, ("dp", "tensor"), split_axis=0, concat_axis=0, tiled=True)


def local_any(
    inputs,
    attention_gain,
    query_weight,
    key_weight,
    value_weight,
    query_gain,
    key_gain,
    out_weight,
    feedforward_gain,
    router_weight,
    gate_weight,
    up_weight,
    down_weight,
    routes,
    cotangent,
):
    tok_rows, model_width = inputs.shape
    head_width = query_gain.shape[0]
    top_count = routes.shape[1]
    expert_count = router_weight.shape[1]
    local_experts = gate_weight.shape[0]
    capacity = tok_rows * top_count * 11 // (expert_count * 8)
    full_query, full_key, full_value, full_out, full_router = (
        lax.all_gather(query_weight, "dp", axis=0, tiled=True),
        lax.all_gather(key_weight, "dp", axis=0, tiled=True),
        lax.all_gather(value_weight, "dp", axis=0, tiled=True),
        lax.all_gather(out_weight, "dp", axis=1, tiled=True),
        lax.all_gather(router_weight, "dp", axis=0, tiled=True),
    )
    inputs_float = inputs.astype(jnp.float32)
    normed_attention, attention_back = jax.vjp(rms_scale, inputs_float, attention_gain)
    sequence = lax.all_gather(normed_attention.astype(jnp.bfloat16), "tensor", axis=0, tiled=True)
    length = sequence.shape[0]
    query_raw = jnp.dot(sequence, full_query, preferred_element_type=jnp.float32)
    key_raw = jnp.dot(sequence, full_key, preferred_element_type=jnp.float32)
    value_raw = jnp.dot(sequence, full_value, preferred_element_type=jnp.float32)
    cosine_table, sine_table = rope_tables(length, head_width)

    def prepare(raw_rows, scales):
        return head_prep(raw_rows, scales, cosine_table, sine_table)

    query_ready, query_back = jax.vjp(prepare, query_raw, query_gain)
    key_ready, key_back = jax.vjp(prepare, key_raw, key_gain)
    kv_heads = key_raw.shape[1] // head_width
    group_size = query_raw.shape[1] // head_width // kv_heads
    queries = query_ready.astype(jnp.bfloat16).reshape(length, kv_heads, group_size, head_width)
    key_rows = key_ready.astype(jnp.bfloat16).reshape(length, kv_heads, head_width)
    value_rows = value_raw.astype(jnp.bfloat16).reshape(length, kv_heads, head_width)
    score_scale = head_width ** (-0.5)
    block_rows = min(block_limit, length)
    block_count = length // block_rows
    offsets = jnp.arange(block_count, dtype=jnp.int32) * block_rows

    def forward_block(offset):
        query_block, masked = masked_scores(offset, block_rows, queries, key_rows, score_scale)
        peak_value = jnp.max(masked, axis=-1, keepdims=True)
        exp_total = jnp.sum(jnp.exp(masked - peak_value), axis=-1, keepdims=True)
        log_total = peak_value + jnp.log(exp_total)
        soft_weights = jnp.exp(masked - log_total).astype(jnp.bfloat16)
        mixture = jnp.einsum(
            "kgqc,ckd->qkgd", soft_weights, value_rows, preferred_element_type=jnp.float32
        )
        return (mixture, log_total)

    mixed_blocks, log_totals = lax.map(forward_block, offsets)
    attended = mixed_blocks.reshape(length, -1).astype(jnp.bfloat16)
    branch = lax.psum_scatter(
        jnp.dot(attended, full_out, preferred_element_type=jnp.float32).astype(jnp.bfloat16),
        "tensor",
        scatter_dimension=0,
        tiled=True,
    ).astype(jnp.float32)
    hidden = inputs_float + branch
    normed_experts, experts_back = jax.vjp(rms_scale, hidden, feedforward_gain)
    moe_in = normed_experts.astype(jnp.bfloat16)
    logits = jnp.dot(moe_in, full_router, preferred_element_type=jnp.float32)
    onehot_routes = (
        routes[:, :, None] == jnp.arange(expert_count, dtype=jnp.int32)[None, None, :]
    ).astype(jnp.float32)
    chosen = jnp.einsum("tke,te->tk", onehot_routes, logits, precision=HIGH)
    gate_values = jax.nn.softmax(chosen, axis=-1)
    slots = slot_layout(routes, expert_count, capacity)
    buffer_shape = (expert_count // local_experts, local_experts, capacity, model_width)
    dispatch = (
        jnp.zeros((expert_count * capacity, model_width), jnp.bfloat16)
        .at[slots]
        .set(jnp.repeat(moe_in, top_count, axis=0))
    )
    received = route_rows(dispatch.reshape(buffer_shape))
    gate_pre = jnp.einsum(
        "secd,edf->secf", received, gate_weight, preferred_element_type=jnp.float32
    )
    up_pre = jnp.einsum("secd,edf->secf", received, up_weight, preferred_element_type=jnp.float32)
    sigmoid_gate = jax.nn.sigmoid(gate_pre)
    silu_gate = gate_pre * sigmoid_gate
    activated = (silu_gate * up_pre).astype(jnp.bfloat16)
    expert_out = jnp.einsum(
        "secf,efd->secd", activated, down_weight, preferred_element_type=jnp.float32
    ).astype(jnp.bfloat16)
    returned = route_rows(expert_out).reshape(expert_count * capacity, model_width)
    picked = returned[slots].reshape(tok_rows, top_count, model_width).astype(jnp.float32)
    mixture_out = jnp.sum(gate_values[:, :, None] * picked, axis=1)
    output = (hidden + mixture_out).astype(jnp.bfloat16)
    grad_output = cotangent.astype(jnp.float32)
    grad_gates = jnp.sum(picked * grad_output[:, None, :], axis=2)
    grad_picks = (
        (gate_values[:, :, None] * grad_output[:, None, :])
        .astype(jnp.bfloat16)
        .reshape(-1, model_width)
    )
    grad_dispatch = (
        jnp.zeros((expert_count * capacity, model_width), jnp.bfloat16).at[slots].set(grad_picks)
    )
    grad_received = route_rows(grad_dispatch.reshape(buffer_shape))
    grad_act = jnp.einsum(
        "secd,efd->secf", grad_received, down_weight, preferred_element_type=jnp.float32
    )
    grad_down = jnp.einsum(
        "secf,secd->efd", activated, grad_received, preferred_element_type=jnp.float32
    )
    grad_gate_pre = (
        grad_act * up_pre * sigmoid_gate * (1.0 + gate_pre * (1.0 - sigmoid_gate))
    ).astype(jnp.bfloat16)
    grad_up_pre = (grad_act * silu_gate).astype(jnp.bfloat16)
    grad_gate = jnp.einsum(
        "secd,secf->edf", received, grad_gate_pre, preferred_element_type=jnp.float32
    )
    grad_up = jnp.einsum(
        "secd,secf->edf", received, grad_up_pre, preferred_element_type=jnp.float32
    )
    grad_sent = jnp.einsum(
        "secf,edf->secd", grad_gate_pre, gate_weight, preferred_element_type=jnp.float32
    )
    grad_sent = (
        grad_sent
        + jnp.einsum("secf,edf->secd", grad_up_pre, up_weight, preferred_element_type=jnp.float32)
    ).astype(jnp.bfloat16)
    grad_back = route_rows(grad_sent).reshape(expert_count * capacity, model_width)
    grad_moe_in = jnp.sum(
        grad_back[slots].reshape(tok_rows, top_count, model_width).astype(jnp.float32), axis=1
    )
    grad_chosen = gate_values * (
        grad_gates - jnp.sum(gate_values * grad_gates, axis=1, keepdims=True)
    )
    grad_logits = jnp.einsum("tk,tke->te", grad_chosen, onehot_routes, precision=HIGH)
    router_float = full_router.astype(jnp.float32)
    grad_moe_in = grad_moe_in + jnp.einsum("te,de->td", grad_logits, router_float, precision=HIGH)
    grad_router = jnp.einsum("td,te->de", moe_in.astype(jnp.float32), grad_logits, precision=HIGH)
    grad_hidden_norm, grad_experts_gain = experts_back(grad_moe_in)
    grad_hidden = grad_output + grad_hidden_norm
    grad_branch = lax.all_gather(grad_hidden.astype(jnp.bfloat16), "tensor", axis=0, tiled=True)
    grad_attended = jnp.einsum(
        "td,ad->ta", grad_branch, full_out, preferred_element_type=jnp.float32
    ).astype(jnp.bfloat16)
    grad_blocks = grad_attended.reshape(block_count, block_rows, kv_heads, group_size, head_width)

    def backward_block(carry, item):
        key_sum, value_sum = carry
        offset, log_total, grad_block = item
        query_block, masked = masked_scores(offset, block_rows, queries, key_rows, score_scale)
        soft_weights = jnp.exp(masked - log_total)
        soft_low = soft_weights.astype(jnp.bfloat16)
        grad_soft = jnp.einsum(
            "qkgd,ckd->kgqc", grad_block, value_rows, preferred_element_type=jnp.float32
        )
        inner_sum = jnp.sum(soft_weights * grad_soft, axis=-1, keepdims=True)
        grad_scores = (soft_weights * (grad_soft - inner_sum)).astype(jnp.bfloat16)
        grad_query_block = (
            jnp.einsum("kgqc,ckd->qkgd", grad_scores, key_rows, preferred_element_type=jnp.float32)
            * score_scale
        )
        key_sum = (
            key_sum
            + jnp.einsum(
                "kgqc,qkgd->ckd", grad_scores, query_block, preferred_element_type=jnp.float32
            )
            * score_scale
        )
        value_sum = value_sum + jnp.einsum(
            "kgqc,qkgd->ckd", soft_low, grad_block, preferred_element_type=jnp.float32
        )
        return ((key_sum, value_sum), grad_query_block)

    zero_rows = jnp.zeros((length, kv_heads, head_width), jnp.float32)
    (key_sum, value_sum), grad_query_blocks = lax.scan(
        backward_block, (zero_rows, zero_rows), (offsets, log_totals, grad_blocks)
    )
    grad_query_raw, grad_query_gain = query_back(grad_query_blocks.reshape(length, -1))
    grad_key_raw, grad_key_gain = key_back(key_sum.reshape(length, -1))
    grad_query_low = grad_query_raw.astype(jnp.bfloat16)
    grad_key_low = grad_key_raw.astype(jnp.bfloat16)
    grad_value_low = value_sum.reshape(length, -1).astype(jnp.bfloat16)
    total = jnp.einsum("tc,dc->td", grad_query_low, full_query, preferred_element_type=jnp.float32)
    total = total + jnp.einsum(
        "tc,dc->td", grad_key_low, full_key, preferred_element_type=jnp.float32
    )
    grad_sequence = lax.psum_scatter(
        (
            total
            + jnp.einsum(
                "tc,dc->td", grad_value_low, full_value, preferred_element_type=jnp.float32
            )
        ).astype(jnp.bfloat16),
        "tensor",
        scatter_dimension=0,
        tiled=True,
    ).astype(jnp.float32)
    grad_inputs_norm, grad_attention_gain = attention_back(grad_sequence)
    grad_inputs = grad_hidden + grad_inputs_norm
    query_cols = grad_query_low.shape[1]
    key_cols = grad_key_low.shape[1]
    grad_raw_all = jnp.concatenate([grad_query_low, grad_key_low, grad_value_low], axis=1)
    inward = jnp.einsum("td,tc->dc", sequence, grad_raw_all, preferred_element_type=jnp.float32)
    outward = jnp.einsum("td,ta->da", grad_branch, attended, preferred_element_type=jnp.float32)
    owned = lax.psum_scatter(
        jnp.concatenate([inward, outward], axis=1), "dp", scatter_dimension=0, tiled=True
    )
    grad_query_weight = owned[:, :query_cols]
    grad_key_weight = owned[:, query_cols : query_cols + key_cols]
    grad_value_weight = owned[:, query_cols + key_cols : query_cols + 2 * key_cols]
    grad_out_weight = owned[:, query_cols + 2 * key_cols :].T
    router_total, attention_total, query_total, key_total, experts_total = lax.psum(
        (grad_router, grad_attention_gain, grad_query_gain, grad_key_gain, grad_experts_gain),
        ("dp", "tensor"),
    )
    router_rows = router_weight.shape[0]
    router_share = lax.dynamic_slice_in_dim(
        router_total, lax.axis_index("dp") * router_rows, router_rows, 0
    )
    return (
        output,
        grad_inputs,
        attention_total,
        grad_query_weight,
        grad_key_weight,
        grad_value_weight,
        query_total,
        key_total,
        grad_out_weight,
        experts_total,
        router_share,
        grad_gate,
        grad_up,
        grad_down,
    )


low, wide = jnp.bfloat16, jnp.float32
Z_RING = tuple((i, (i + 4) % 16) for i in range(16))
Z_PAIR = tuple((i, i ^ 4) for i in range(16))
Z_FAR = tuple((i, i ^ 8) for i in range(16))
Y_PAIR = tuple((i, i ^ 2) for i in range(16))
X_PAIR = tuple((i, i ^ 1) for i in range(16))
BLOCKS = tuple((k, dy, dx) for k in range(4) for dy in range(2) for dx in range(2))
PLANE = tuple((dy, dx) for dy in range(2) for dx in range(2))
OVER_X = (1, 2)
ROOM = 8 * 2**20
WHOLE = 60 * 2**20
TILE = 256
WIDE = 512
HIDDEN_TILE = 768
NT = (((1,), (1,)), ((), ()))
TN = (((0,), (0,)), ((), ()))


def z_next(block):
    return lax.ppermute(block, "dp", Z_RING)


def z_pair(block):
    return lax.ppermute(block, "dp", Z_PAIR)


def z_far(block):
    return lax.ppermute(block, "dp", Z_FAR)


def y_swap(block):
    return lax.ppermute(block, "dp", Y_PAIR)


def x_swap(block):
    return lax.ppermute(block, "dp", X_PAIR)


def core_swap(block):
    return lax.ppermute(block, "tensor", ((0, 1), (1, 0)))


def after(value, *earlier):
    return lax.optimization_barrier((value, *earlier))[0]


def plus(own, *others):
    total = own.astype(wide)
    for other in others:
        total = total + other.astype(wide)
    return total


TOKEN_ROUNDS = (
    (((0, 0, 0), (0, 0, 1), x_swap), ((0, 0, 0), (0, 1, 0), y_swap), ((0, 0, 0), (1, 0, 0), z_next)),
    (((1, 0, 0), (1, 0, 1), x_swap), ((0, 0, 1), (0, 1, 1), y_swap), ((1, 0, 0), (2, 0, 0), z_next)),
    (((2, 0, 0), (2, 0, 1), x_swap), ((1, 0, 0), (1, 1, 0), y_swap), ((2, 0, 0), (3, 0, 0), z_next)),
    (((3, 0, 0), (3, 0, 1), x_swap), ((2, 0, 0), (2, 1, 0), y_swap), ((0, 1, 1), (1, 1, 1), z_next)),
    (((2, 1, 0), (2, 1, 1), x_swap), ((3, 0, 1), (3, 1, 1), y_swap), ((2, 1, 0), (3, 1, 0), z_next)),
)
WEIGHT_ROUNDS = (
    (
        ((0, 0, 0), (0, 0, 1), x_swap),
        ((0, 0, 0), (0, 1, 0), y_swap),
        ((0, 0, 0), (2, 0, 0), z_far, True),
    ),
    (
        ((1, 0, 0), (1, 0, 1), x_swap),
        ((1, 0, 0), (1, 1, 0), y_swap),
        ((1, 0, 0), (3, 0, 0), z_far, True),
        ((0, 0, 1), (0, 1, 1), y_swap),
    ),
    (
        ((2, 0, 0), (2, 0, 1), x_swap),
        ((2, 0, 0), (2, 1, 0), y_swap),
        ((1, 1, 0), (1, 1, 1), x_swap),
    ),
    (
        ((3, 0, 0), (3, 1, 0), y_swap),
        ((3, 0, 0), (3, 0, 1), x_swap),
        ((2, 0, 1), (2, 1, 1), y_swap),
    ),
    (((3, 1, 0), (3, 1, 1), x_swap),),
)
SHORT_ROUNDS = (
    (*WEIGHT_ROUNDS[0][:2],),
    (((0, 0, 0), (2, 0, 0), z_far, True), *WEIGHT_ROUNDS[1][:2], WEIGHT_ROUNDS[1][3]),
    (((1, 0, 0), (3, 0, 0), z_far), *WEIGHT_ROUNDS[2]),
    (*WEIGHT_ROUNDS[3], ((1, 1, 1), (3, 1, 1), z_far)),
)
WEIGHT_RETURNS = (
    (((3, 1, 1), (3, 1, 0), x_swap),),
    (
        ((3, 1, 0), (3, 0, 0), y_swap),
        ((3, 0, 1), (3, 0, 0), x_swap),
        ((2, 1, 1), (2, 0, 1), y_swap),
    ),
    (
        ((3, 0, 0), (1, 0, 0), z_far, True),
        ((2, 0, 1), (2, 0, 0), x_swap),
        ((2, 1, 0), (2, 0, 0), y_swap),
        ((1, 1, 1), (1, 1, 0), x_swap),
    ),
    (
        ((2, 0, 0), (0, 0, 0), z_far, True),
        ((1, 1, 0), (1, 0, 0), y_swap),
        ((1, 0, 1), (1, 0, 0), x_swap),
        ((0, 1, 1), (0, 0, 1), y_swap),
    ),
    (((0, 0, 1), (0, 0, 0), x_swap), ((0, 1, 0), (0, 0, 0), y_swap)),
)


def turned(block):
    k, dy, dx = block
    return (-k) % 4, dy, dx


RETURN_ROUNDS = tuple(
    tuple((turned(end), turned(start), over) for start, end, over in moves)
    for moves in reversed(TOKEN_ROUNDS)
)
OUTPUT_ROUNDS = (
    (((2, 1, 1), (2, 1, 0), x_swap), ((1, 1, 0), (2, 1, 0), z_next)),
    (((1, 1, 1), (1, 0, 1), y_swap), ((2, 0, 1), (2, 0, 0), x_swap), ((3, 1, 1), (0, 1, 1), z_next)),
    (((1, 0, 1), (1, 0, 0), x_swap), ((2, 1, 0), (2, 0, 0), y_swap)),
    (((3, 1, 0), (3, 0, 0), y_swap), ((3, 0, 1), (3, 0, 0), x_swap), ((1, 0, 0), (2, 0, 0), z_next)),
    (((0, 1, 1), (0, 0, 1), y_swap), ((2, 0, 0), (3, 0, 0), z_next)),
    (((0, 0, 1), (0, 0, 0), x_swap), ((0, 1, 0), (0, 0, 0), y_swap), ((3, 0, 0), (0, 0, 0), z_next)),
)


class Chain:
    def __init__(self):
        self.earlier = []
        self.late = []
        self.values = []

    def add(self, *values):
        self.earlier.extend(values)

    def send(self, values, ways, late=()):
        values = lax.optimization_barrier((*values, *self.earlier))[: len(values)]
        self.values = values
        results = [way(value) for value, way in zip(values, ways)]
        self.earlier = self.late + [r for i, r in enumerate(results) if i not in late]
        self.late = [results[i] for i in late]
        return results

    def round(self, values, moves, others):
        late = [i for i, move in enumerate(moves) if len(move) > 3]
        values = values + [value for value, _ in others]
        ways = [move[2] for move in moves] + [way for _, way in others]
        results = self.send(values, ways, late)
        return results[: len(moves)], results[len(moves) :]

    def gather(self, pairs, others=()):
        values = [held[move[0]] for held, moves in pairs for move in moves]
        moves = [move for _, moves in pairs for move in moves]
        results, rest = self.round(values, moves, others)
        for (held, end), result in zip([(h, m[1]) for h, ms in pairs for m in ms], results):
            held[end] = result
        return rest

    def scatter(self, pairs, others=()):
        values = totals([terms[move[0]] for terms, moves in pairs for move in moves])
        moves = [move for _, moves in pairs for move in moves]
        results, rest = self.round(values, moves, others)
        for (terms, end), result in zip([(t, m[1]) for t, ms in pairs for m in ms], results):
            terms[end].append(result)
        return rest


def sum_kernel(counts, *refs):
    outs = refs[sum(counts) :]
    for count, out in zip(counts, outs):
        terms, refs = refs[:count], refs[count:]
        out[...] = plus(*[term[...] for term in terms]).astype(out.dtype)


def totals(lists):
    several = [terms for terms in lists if len(terms) > 1]
    if not several:
        return [terms[0] for terms in lists]
    operands = [term for terms in several for term in terms]
    rows = operands[0].shape[0] // 4
    whole = [(a.shape[0] // 4, a.shape[1]) for a in operands]
    specs = [pl.BlockSpec(block, lambda i: (i, 0)) for block in whole]
    firsts = [terms[0] for terms in several]
    sums = pl.pallas_call(
        functools.partial(sum_kernel, [len(terms) for terms in several]),
        grid=(4,),
        out_shape=[jax.ShapeDtypeStruct(a.shape, low) for a in firsts],
        in_specs=specs,
        out_specs=[pl.BlockSpec((rows, a.shape[1]), lambda i: (i, 0)) for a in firsts],
        name="sums",
        compiler_params=pltpu.CompilerParams(vmem_limit_bytes=2 * ROOM),
    )(*operands)
    sums = list(sums)
    return [sums.pop(0) if len(terms) > 1 else terms[0] for terms in lists]


def dot(left, right, dims=None):
    if dims is None:
        return jnp.dot(left, right, preferred_element_type=wide)
    return lax.dot_general(left, right, dims, preferred_element_type=wide)


def lanes(start, size):
    return pl.ds(pl.multiple_of(start, 128), size)


def spot(ids, i):
    return pl.multiple_of(ids[i] * 128, 128)


def row_copies(ids, blocks, whole, sems):
    return [
        pltpu.make_async_copy(block, whole.at[pl.ds(spot(ids, i), 128), :], sems.at[i])
        for i, block in enumerate(blocks)
    ]


def column_copies(ids, blocks, whole, sems):
    return [
        pltpu.make_async_copy(block, whole.at[:, pl.ds(spot(ids, i), 128)], sems.at[i])
        for i, block in enumerate(blocks)
    ]


def stack_copies(blocks, whole, sems):
    rows = blocks[0].shape[0]
    return [
        pltpu.make_async_copy(block, whole.at[pl.ds(i * rows, rows), :], sems.at[i])
        for i, block in enumerate(blocks)
    ]


def start_all(copies):
    for copy in copies:
        copy.start()


def wait_all(copies):
    for copy in copies:
        copy.wait()


def head_forward(raw, gain, cosine, sine):
    inverse = lax.rsqrt(jnp.mean(raw * raw, axis=-1, keepdims=True) + EPS)
    unit = raw * inverse
    shaped = unit * gain
    return unit, inverse, shaped * cosine + pltpu.roll(shaped, 64, 1) * sine


def head_backward(grad, unit, inverse, gain, cosine, sine):
    back = grad * cosine - pltpu.roll(grad, 64, 1) * sine
    gain_grad = jnp.sum(back * unit, axis=0, keepdims=True)
    scaled = back * gain
    return gain_grad, inverse * (scaled - unit * jnp.mean(scaled * unit, axis=-1, keepdims=True))


def causal(core, length):
    half = length // 2
    rows = lax.broadcasted_iota(jnp.int32, (length, length), 0)
    columns = lax.broadcasted_iota(jnp.int32, (length, length), 1)

    def place(i):
        return jnp.where(i < half, i + core * half, i - half + (1 - core) * half)

    return place(columns) <= place(rows)


def soft(query, key, allowed, scale):
    scores = jnp.where(allowed, dot(query, key, NT) * scale, -1e30)
    raised = jnp.exp(scores - jnp.max(scores, axis=-1, keepdims=True))
    return raised / jnp.sum(raised, axis=-1, keepdims=True)


def raw_kernel(ids, block_ids, *refs):
    seq_blocks, blocks = refs[:4], refs[4:20]
    raw, router, rest, whole, seq, sems = refs[20:]
    copies = stack_copies(seq_blocks, seq, sems.at[pl.ds(16, 4)]) + row_copies(
        ids, blocks, whole, sems
    )
    start_all(copies)
    wait_all(copies)
    width = raw.shape[1]

    @pl.loop(0, width // TILE)
    def _(j):
        span = lanes(j * TILE, TILE)
        raw[:, span] = dot(seq[...], whole[:, span])

    router[...] = whole[:, width:]
    for p in range(16):
        rest[p * 128 : (p + 1) * 128, :] = whole[pl.ds(spot(block_ids, p), 128), width:]


def forward_kernel(head_count, core, raw, cosine, sine, query_gain, key_gain, attended):
    length = raw.shape[0] // 2
    key_start = head_count * 128
    allowed = causal(core[0], length)
    scale = 128 ** (-0.5)
    for s in range(2):
        span = slice(s * length, (s + 1) * length)
        turn = (cosine[...], sine[...])
        key_raw = raw[span, key_start : key_start + 128]
        key = head_forward(key_raw, key_gain[...], *turn)[2].astype(low)
        value = raw[span, key_start + 128 : key_start + 256].astype(low)

        @pl.loop(0, head_count, unroll=2)
        def _(h):
            columns = lanes(h * 128, 128)
            query = head_forward(raw[span, columns], query_gain[...], *turn)[2].astype(low)
            weights = soft(query, key, allowed, scale)
            attended[span, columns] = dot(weights.astype(low), value).astype(low)


def split_rows(product, span, sent, kept):
    rows = product.shape[0] // 4
    kept[:rows, span] = product[:rows]
    sent[:rows, span] = product[rows : 2 * rows].astype(low)
    kept[rows:, span] = product[2 * rows : 3 * rows]
    sent[rows:, span] = product[3 * rows :].astype(low)


def out_kernel(ids, attended, *refs):
    blocks, (sent, kept, whole, sems) = refs[:16], refs[16:]
    copies = column_copies(ids, blocks, whole, sems)
    start_all(copies)
    wait_all(copies)

    @pl.loop(0, whole.shape[1] // WIDE)
    def _(j):
        span = lanes(j * WIDE, WIDE)
        split_rows(dot(attended[...], whole[:, span]), span, sent, kept)


def normed_grad_kernel(ids, grad_raw, gain, *refs):
    seq_blocks, blocks = refs[:4], refs[4:20]
    sent, kept, gain_grad, whole, seq, sems = refs[20:]
    copies = row_copies(ids, blocks, whole, sems) + stack_copies(
        seq_blocks, seq, sems.at[pl.ds(16, 4)]
    )
    start_all(copies)
    wait_all(copies)
    width = grad_raw.shape[1]

    @pl.loop(0, whole.shape[0] // WIDE)
    def _(j):
        span = lanes(j * WIDE, WIDE)
        product = dot(grad_raw[...], whole[span, :width], NT)
        split_rows(product, span, sent, kept)
        unit = seq[:, span].astype(wide) / gain[:, span]
        gain_grad[:, span] = jnp.sum(product * unit, axis=0, keepdims=True)


def attended_grad_kernel(ids, *refs):
    grad_blocks, blocks = refs[:4], refs[4:20]
    grad_attended, grad_branch, whole, sems = refs[20:]
    copies = stack_copies(grad_blocks, grad_branch, sems.at[pl.ds(16, 4)]) + column_copies(
        ids, blocks, whole, sems
    )
    start_all(copies)
    wait_all(copies)

    @pl.loop(0, grad_attended.shape[1] // WIDE)
    def _(j):
        span = lanes(j * WIDE, WIDE)
        grad_attended[:, span] = dot(grad_branch[...], whole[span, :], NT).astype(low)


def map_kernel(capacity, expert_count, experts, named, picks, turned_picks):
    slot_rows = 4 * capacity
    early = lax.broadcasted_iota(jnp.int32, (128, 128), 0)
    late = lax.broadcasted_iota(jnp.int32, (128, 128), 1)
    before = jnp.where(early < late, 1.0, 0.0).astype(low)
    behind = jnp.where(late < early, 1.0, 0.0).astype(low)
    slot_numbers = lax.broadcasted_iota(jnp.int32, (slot_rows, 128), 0)
    slot_lanes = lax.broadcasted_iota(jnp.int32, (128, turned_picks.shape[1]), 1)
    for b in range(16):
        k, i = b // 4, b % 4
        block = named[b * 128 : (b + 1) * 128, :]
        turned_slots = []
        for c in range(2):
            column = experts[c] + expert_count
            own_lane = lax.broadcasted_iota(jnp.int32, (8, 128), 1) == column
            hit = dot(jnp.where(own_lane, 1.0, 0.0).astype(low), block, NT)
            slot = dot(hit.astype(low), before) + float(i * capacity)
            slot = jnp.where(hit > 0.5, slot, -1.0).astype(jnp.int32)
            first = (2 * k + c) * slot_rows
            picks[first : first + slot_rows, i * 128 : (i + 1) * 128] = jnp.where(
                slot_numbers == slot[:1], 1.0, 0.0
            ).astype(low)
            mine = jnp.where(late == column, block.astype(wide), 0.0)
            hit = jnp.sum(mine, axis=1, keepdims=True)
            slot = jnp.sum(dot(behind, mine.astype(low)), axis=1, keepdims=True)
            slot = slot + float(i * capacity + c * slot_rows)
            turned_slots.append(jnp.where(hit > 0.5, slot, -1.0).astype(jnp.int32))
        either = jnp.logical_or(slot_lanes == turned_slots[0], slot_lanes == turned_slots[1])
        turned_picks[b * 128 : (b + 1) * 128, :] = jnp.where(either, 1.0, 0.0).astype(low)


def pick_kernel(k, picks_in, named, *refs):
    tokens, cots, (own, other, picks, rows, sems) = refs[:4], refs[4:8], refs[8:]
    quad_rows, full = rows.shape
    width = tokens[0].shape[1]
    copies = (
        stack_copies(tokens, rows.at[:, pl.ds(0, width)], sems.at[pl.ds(0, 4)])
        + stack_copies(cots, rows.at[:, pl.ds(width + 128, width)], sems.at[pl.ds(4, 4)])
        + [
            pltpu.make_async_copy(
                picks_in.at[pl.ds(k * picks.shape[0], picks.shape[0]), :], picks, sems.at[8]
            ),
            pltpu.make_async_copy(
                named.at[pl.ds(k * quad_rows, quad_rows), :],
                rows.at[:, pl.ds(width, 128)],
                sems.at[9],
            ),
        ]
    )
    start_all(copies)
    wait_all(copies)
    slot_rows = own.shape[0]
    for start in range(0, full, WIDE):
        span = slice(start, min(start + WIDE, full))
        made = dot(picks[...], rows[:, span]).astype(low)
        own[:, span] = made[:slot_rows]
        other[:, span] = made[slot_rows:]


def expert_kernel(expert_count, k, experts, router, *refs):
    sides, weights = refs[:2], refs[2:5]
    refs = refs[5 + (5 if k else 0) :]
    (all_rows, all_act, all_grads, all_gate, all_up, own_out, back_out) = refs[:7]
    (rows, v_gate, v_up, v_down, act, grads, gate_back, up_back) = refs[7:15]
    (gate_pre, up_pre, sig, sems) = refs[15:]
    slot_rows = own_out.shape[0]
    width, hidden = v_gate.shape
    after_width = width + 128
    spans = [slice(c * slot_rows, (c + 1) * slot_rows) for c in range(2)]
    side_copies = stack_copies(sides, rows, sems.at[pl.ds(0, 2)])
    weight_copies = [
        pltpu.make_async_copy(a, b, sems.at[2 + i])
        for i, (a, b) in enumerate(zip(weights, (v_gate, v_up, v_down)))
    ]
    start_all(side_copies + weight_copies)
    kept = []

    def keep(source, target, sem):
        copy = pltpu.make_async_copy(
            source.at[:, pl.ds(0, target.shape[1])],
            target.at[pl.ds(k * 2 * slot_rows, 2 * slot_rows), :],
            sems.at[sem],
        )
        copy.start()
        kept.append(copy)

    wait_all(side_copies)
    keep(rows, all_rows, 5)
    logits = dot(rows[:, :width], router[...])
    numbers = lax.broadcasted_iota(jnp.int32, logits.shape, 1)
    is_named = pltpu.roll(rows[:, width:after_width].astype(wide), 128 - expert_count, 1)
    is_named = jnp.logical_and(is_named > 0.5, numbers < expert_count)
    lifted = jnp.where(is_named, logits, -1e30)
    lifted = jnp.where(
        is_named, jnp.exp(lifted - jnp.max(lifted, axis=1, keepdims=True)), 0.0
    )
    mine = jnp.sum(jnp.where(numbers == experts[0], lifted, 0.0), axis=1, keepdims=True)
    gates = mine / jnp.maximum(jnp.sum(lifted, axis=1, keepdims=True), 1e-30)
    wait_all(weight_copies[:2])
    pre = dot(rows[:, :width], v_gate[...])
    up = dot(rows[:, :width], v_up[...])
    s = jax.nn.sigmoid(pre)
    gate_pre[...] = pre
    up_pre[...] = up
    sig[...] = s
    act[...] = (pre * s * up).astype(low)
    keep(act, all_act, 6)
    wait_all(weight_copies[2:])
    slot_grads = jnp.zeros((2 * slot_rows, 1), wide)
    for j in range(width // WIDE):
        span = slice(j * WIDE, (j + 1) * WIDE)
        later = slice(after_width + j * WIDE, after_width + (j + 1) * WIDE)
        out = dot(act[...], v_down[:, span]).astype(low).astype(wide)
        cot = rows[:, later].astype(wide)
        grads[:, span] = (gates * cot).astype(low)
        scaled = (gates * out).astype(low)
        own_out[:, later] = scaled[spans[0]]
        back_out[:, later] = scaled[spans[1]]
        slot_grads = slot_grads + jnp.sum(cot * out, axis=1, keepdims=True)
    keep(grads, all_grads, 7)
    back = dot(grads[...], v_down[...], NT)
    pre, s = gate_pre[...], sig[...]
    gate_back[...] = (back * up_pre[...] * s * (1.0 + pre * (1.0 - s))).astype(low)
    up_back[...] = (back * (pre * s)).astype(low)
    keep(gate_back, all_gate, 8)
    keep(up_back, all_up, 9)
    for j in range(width // WIDE):
        span = slice(j * WIDE, (j + 1) * WIDE)
        back = dot(gate_back[...], v_gate[span, :], NT) + dot(up_back[...], v_up[span, :], NT)
        back = back.astype(low)
        own_out[:, span] = back[spans[0]]
        back_out[:, span] = back[spans[1]]
    high = slot_grads.astype(low).astype(wide)
    rest = jnp.where(numbers == experts[0] + expert_count, slot_grads - high, 0.0)
    parts = jnp.where(numbers == experts[0], high, rest).astype(low)
    own_out[:, width:after_width] = parts[spans[0]]
    back_out[:, width:after_width] = parts[spans[1]]
    wait_all(kept)


def token_sum_kernel(k, turned_picks, *refs):
    sides, blocks, outputs, (picks, rows, out_rows, sems) = refs[:2], refs[2:6], refs[6:10], refs[10:]
    quad_rows, width = out_rows.shape
    copies = stack_copies(sides, rows, sems.at[pl.ds(0, 2)]) + [
        pltpu.make_async_copy(
            turned_picks.at[pl.ds(k * quad_rows, quad_rows), :], picks, sems.at[2]
        )
    ]
    start_all(copies)
    wait_all(copies)
    slots = rows.shape[0]
    size, first = blocks[0].shape
    for j in range(0, width, WIDE):
        span = slice(j, j + WIDE)
        out_rows[:, span] = dot(picks[:, :slots], rows[:, first + j : first + j + WIDE]).astype(low)
    copies = [
        pltpu.make_async_copy(out_rows.at[pl.ds(i * size, size), :], output, sems.at[3 + i])
        for i, output in enumerate(outputs)
    ]
    start_all(copies)
    for j in range(0, first, WIDE):
        span = slice(j, min(j + WIDE, first))
        made = dot(picks[:, :slots], rows[:, span]).astype(low)
        for i, block in enumerate(blocks):
            block[:, span] = made[i * size : (i + 1) * size]
    wait_all(copies)


def backward_kernel(head_count, core, raw, grad_attended, *refs):
    cosine, sine, query_gain, key_gain = refs[:4]
    grad_raw, query_gain_grad, key_gain_grad, key_sum, value_sum = refs[4:]
    length = raw.shape[0] // 2
    key_start = head_count * 128
    allowed = causal(core[0], length)
    scale = 128 ** (-0.5)
    turn = (cosine[...], sine[...])
    query_gain_grad[...] = jnp.zeros_like(query_gain_grad)
    key_gain_grad[...] = jnp.zeros_like(key_gain_grad)
    for s in range(2):
        span = slice(s * length, (s + 1) * length)
        key_raw = raw[span, key_start : key_start + 128]
        key_unit, key_inverse, key = head_forward(key_raw, key_gain[...], *turn)
        key = key.astype(low)
        value = raw[span, key_start + 128 : key_start + 256].astype(low)
        key_sum[...] = jnp.zeros_like(key_sum)
        value_sum[...] = jnp.zeros_like(value_sum)

        @pl.loop(0, head_count, unroll=2)
        def _(h):
            columns = lanes(h * 128, 128)
            unit, inverse, query = head_forward(raw[span, columns], query_gain[...], *turn)
            query = query.astype(low)
            weights = soft(query, key, allowed, scale)
            grad = grad_attended[span, columns]
            grad_soft = dot(grad, value, NT)
            inner = jnp.sum(weights * grad_soft, axis=-1, keepdims=True)
            grad_scores = (weights * (grad_soft - inner)).astype(low)
            value_sum[...] += dot(weights.astype(low), grad, TN)
            key_sum[...] += dot(grad_scores, query, TN) * scale
            grad_query = dot(grad_scores, key) * scale
            gain_grad, back = head_backward(grad_query, unit, inverse, query_gain[...], *turn)
            query_gain_grad[...] += gain_grad
            grad_raw[span, columns] = back.astype(low)

        gain_grad, back = head_backward(
            key_sum[...], key_unit, key_inverse, key_gain[...], *turn
        )
        key_gain_grad[...] += gain_grad
        grad_raw[span, key_start : key_start + 128] = back.astype(low)
        grad_raw[span, key_start + 128 : key_start + 256] = value_sum[...].astype(low)


def block_product_kernel(with_rest, ids, right, *refs):
    left_blocks, refs = refs[:4], refs[4:]
    rest, refs = (refs[0], refs[1:]) if with_rest else (None, refs)
    outs, (left, sems) = refs[:16], refs[16:]
    copies = stack_copies(left_blocks, left, sems)
    start_all(copies)
    wait_all(copies)
    width = right.shape[1]
    for i, out in enumerate(outs):
        part = left[:, pl.ds(spot(ids, i), 128)]
        out[:, :width] = dot(part, right[...], TN).astype(low)
        if with_rest:
            out[:, width:] = jnp.transpose(rest[:, pl.ds(spot(ids, i), 128)]).astype(low)


SMEM = pl.BlockSpec(memory_space=pltpu.SMEM)
VMEM = pl.BlockSpec(memory_space=pltpu.VMEM)
FAR = pl.BlockSpec(memory_space=pl.ANY)
HBM = pl.BlockSpec(memory_space=pltpu.HBM)


def call(kernel, name, ins, outs, scratch, flops, specs=None, aliases=None, alone=False):
    operands = [value for value, _ in ins]
    moved = sum(a.size * a.dtype.itemsize for a in operands + outs)
    placed = [value for value, spec in ins if spec is VMEM] + scratch
    placed += [out for out, spec in zip(outs, specs or [VMEM] * len(outs)) if spec is VMEM]
    held = sum(
        math.prod(a.shape) * jnp.dtype(a.dtype).itemsize
        for a in placed
        if jnp.issubdtype(a.dtype, jnp.floating)
    )
    return pl.pallas_call(
        kernel,
        out_shape=outs,
        in_specs=[spec for _, spec in ins],
        out_specs=specs or [VMEM] * len(outs),
        scratch_shapes=scratch,
        name=name,
        input_output_aliases=aliases or {},
        compiler_params=pltpu.CompilerParams(vmem_limit_bytes=WHOLE if alone else ROOM + held),
        cost_estimate=pl.CostEstimate(flops=flops, bytes_accessed=moved, transcendentals=0),
    )(*operands)


def shape(rows, columns, dtype):
    return jax.ShapeDtypeStruct((rows, columns), dtype)


def copies_sem(count):
    return pltpu.SemaphoreType.DMA((count,))


def local_sixteen(
    inputs,
    attention_gain,
    query_weight,
    key_weight,
    value_weight,
    query_gain,
    key_gain,
    out_weight,
    feedforward_gain,
    router_weight,
    gate_weight,
    up_weight,
    down_weight,
    routes,
    cotangent,
):
    tok_rows, model_width = inputs.shape
    head_width = query_gain.shape[0]
    top_count = routes.shape[1]
    expert_count = router_weight.shape[1]
    hidden_width = gate_weight.shape[2]
    capacity = tok_rows * top_count * 11 // (expert_count * 8)
    query_cols, key_cols = query_weight.shape[1] // 2, key_weight.shape[1] // 2
    raw_cols = query_cols + 2 * key_cols
    head_count = query_cols // head_width
    place = lax.axis_index("dp")
    core = lax.axis_index("tensor")
    z, y, x = place // 4, (place // 2) % 2, place % 2
    even = z % 2 == 0
    core_id = core.astype(jnp.int32)[None]
    block_ids = jnp.stack(
        [((z - k) % 4) * 4 + (y ^ dy) * 2 + (x ^ dx) for k, dy, dx in BLOCKS]
    ).astype(jnp.int32)
    weight_ids = jnp.stack(
        [(z ^ w) * 4 + (y ^ dy) * 2 + (x ^ dx) for w, dy, dx in BLOCKS]
    ).astype(jnp.int32)

    def halves(values, axis):
        first, second = jnp.split(values, 2, axis=axis)
        return jnp.where(even, first, second), jnp.where(even, second, first)

    def in_order(mine, theirs, axis):
        return jnp.where(
            even,
            jnp.concatenate([mine, theirs], axis=axis),
            jnp.concatenate([theirs, mine], axis=axis),
        )

    chain = Chain()
    numbers = jnp.arange(expert_count, dtype=jnp.int32)
    own_named = jnp.any(routes[:, :, None] == numbers, axis=1)
    splits = [halves(w, 1) for w in (query_weight, key_weight, value_weight)]
    rest = [
        router_weight,
        own_named.astype(low),
        jnp.zeros((tok_rows, 128 - 2 * expert_count), low),
    ]
    mine = jnp.concatenate([s[0] for s in splits] + rest, axis=1)
    theirs = jnp.concatenate([s[1] for s in splits] + rest, axis=1)
    held = {(0, 0, 0): mine}
    (held[1, 0, 0],) = chain.gather([(held, WEIGHT_ROUNDS[0])], [(theirs, z_pair)])
    inputs_float = inputs.astype(wide)
    normed_attention, attention_back = jax.vjp(rms_scale, inputs_float, attention_gain)
    normed = normed_attention.astype(low)
    chain.add(normed)
    chain.gather([(held, WEIGHT_ROUNDS[1])])
    chain.gather([(held, WEIGHT_ROUNDS[2])])
    far, swapped = chain.gather(
        [(held, WEIGHT_ROUNDS[3])], [(normed, z_pair), (normed, core_swap)]
    )
    out_mine, out_theirs = halves(out_weight, 0)
    out_held = {(0, 0, 0): out_mine}
    cot_held = {(0, 0, 0): cotangent}
    far_swapped, out_held[1, 0, 0] = chain.gather(
        [(held, WEIGHT_ROUNDS[4]), (out_held, SHORT_ROUNDS[0])],
        [(far, core_swap), (out_theirs, z_pair)],
    )
    sequence = [normed, swapped, far, far_swapped]
    blocks = [held[b] for b in BLOCKS]
    chain.gather([(out_held, SHORT_ROUNDS[1])])
    grad_output = cotangent.astype(wide)
    length = 2 * tok_rows
    own_places = jnp.arange(tok_rows, dtype=jnp.int32)
    places = jnp.concatenate([own_places + core * tok_rows, own_places + (1 - core) * tok_rows])
    halfway = head_width // 2
    frequency = THETA ** (-(jnp.arange(halfway, dtype=wide) * 2.0 / head_width))
    angles = places.astype(wide)[:, None] * frequency[None, :]
    cosine, sine = jnp.cos(angles), jnp.sin(angles)
    turns = [
        (jnp.concatenate([cosine, cosine], axis=1), VMEM),
        (jnp.concatenate([-sine, sine], axis=1), VMEM),
        (query_gain[None, :], VMEM),
        (key_gain[None, :], VMEM),
    ]
    both = 2 * length
    raw, router_rows, rest_rows = call(
        raw_kernel,
        "attention_raw",
        [(weight_ids, SMEM), (block_ids, SMEM)]
        + [(b, FAR) for b in sequence]
        + [(b, HBM) for b in blocks],
        [
            shape(both, raw_cols, wide),
            shape(model_width, 128, low),
            shape(model_width, 128, low),
        ],
        [
            pltpu.VMEM((model_width, raw_cols + 128), low),
            pltpu.VMEM((both, model_width), low),
            copies_sem(20),
        ],
        2 * both * model_width * raw_cols,
        alone=True,
    )
    chain.add(raw)
    chain.gather([(out_held, SHORT_ROUNDS[2])])
    (attended,) = call(
        functools.partial(forward_kernel, head_count),
        "attention_forward",
        [(core_id, SMEM), (raw, VMEM)] + turns,
        [shape(both, query_cols, low)],
        [],
        4 * both * length * query_cols,
    )
    chain.add(attended)
    chain.gather([(out_held, SHORT_ROUNDS[3])])
    out_blocks = [out_held[b] for b in BLOCKS]
    chain.gather([(cot_held, TOKEN_ROUNDS[0])])
    sent, kept = call(
        out_kernel,
        "attention_out",
        [(weight_ids, SMEM), (attended, VMEM)] + [(b, HBM) for b in out_blocks],
        [shape(length, model_width, low), shape(length, model_width, wide)],
        [pltpu.VMEM((query_cols, model_width), low), copies_sem(16)],
        2 * both * model_width * query_cols,
    )

    pair_total = kept + core_swap(sent).astype(wide)
    leaving = pair_total[tok_rows:].astype(low)
    from_pair = z_pair(leaving)
    chain.add(leaving)
    chain.gather([(cot_held, TOKEN_ROUNDS[1])])
    chain.gather([(cot_held, TOKEN_ROUNDS[2])])
    hidden = inputs_float + pair_total[:tok_rows] + from_pair.astype(wide)
    normed_experts, experts_back = jax.vjp(rms_scale, hidden, feedforward_gain)
    moe_in = normed_experts.astype(low)
    chain.add(moe_in)

    token_held = {(0, 0, 0): moe_in}
    chain.gather([(token_held, TOKEN_ROUNDS[0])])
    chain.gather([(token_held, TOKEN_ROUNDS[1])])
    slot_rows = 4 * capacity
    quad_rows = 4 * tok_rows
    rows_of = 2 * slot_rows
    all_slots = 4 * rows_of
    experts = jnp.stack([place * 2 + core, place * 2 + 1 - core]).astype(jnp.int32)
    w_gate, w_up, w_down = gate_weight[0], up_weight[0], down_weight[0]
    turned_width = -(-rows_of // 128) * 128
    picks, turned_picks = call(
        functools.partial(map_kernel, capacity, expert_count),
        "pick_maps",
        [(experts, SMEM), (rest_rows, VMEM)],
        [shape(all_slots, quad_rows, low), shape(model_width, turned_width, low)],
        [],
        2 * 128 * 128 * model_width,
    )

    logits = jnp.dot(moe_in, router_rows, preferred_element_type=wide)[:, :expert_count]
    lifted = jnp.where(own_named, logits, -1e30)
    lifted = jnp.where(own_named, jnp.exp(lifted - jnp.max(lifted, axis=1, keepdims=True)), 0.0)
    gate_dense = lifted / jnp.sum(lifted, axis=1, keepdims=True)

    full = 2 * model_width + 128

    def pick_tokens(k, *earlier):
        return call(
            functools.partial(pick_kernel, k),
            "picks",
            [(after(picks, *earlier), FAR), (rest_rows, FAR)]
            + [(token_held[k, dy, dx], FAR) for dy, dx in PLANE]
            + [(cot_held[k, dy, dx], HBM) for dy, dx in PLANE],
            [shape(slot_rows, full, low)] * 2,
            [
                pltpu.VMEM((rows_of, quad_rows), low),
                pltpu.VMEM((quad_rows, full), low),
                copies_sem(10),
            ],
            2 * rows_of * quad_rows * full,
            alone=k == 0,
        )

    stores = []

    def run_experts(k, own, back):
        ins = (
            [(experts, SMEM), (router_rows, VMEM), (own, FAR), (back, FAR)]
            + [(w, HBM) for w in (w_gate, w_up, w_down)]
        )
        made = call(
            functools.partial(expert_kernel, expert_count, k),
            "experts",
            ins + [(store, HBM) for store in stores],
            [
                shape(all_slots, model_width, low),
                shape(all_slots, hidden_width, low),
                shape(all_slots, model_width, low),
                shape(all_slots, hidden_width, low),
                shape(all_slots, hidden_width, low),
                shape(slot_rows, full, low),
                shape(slot_rows, full, low),
            ],
            [
                pltpu.VMEM((rows_of, full), low),
                pltpu.VMEM((model_width, hidden_width), low),
                pltpu.VMEM((model_width, hidden_width), low),
                pltpu.VMEM((hidden_width, model_width), low),
                pltpu.VMEM((rows_of, hidden_width), low),
                pltpu.VMEM((rows_of, model_width), low),
                pltpu.VMEM((rows_of, hidden_width), low),
                pltpu.VMEM((rows_of, hidden_width), low),
                pltpu.VMEM((rows_of, hidden_width), wide),
                pltpu.VMEM((rows_of, hidden_width), wide),
                pltpu.VMEM((rows_of, hidden_width), wide),
                copies_sem(10),
            ],
            12 * rows_of * model_width * hidden_width,
            [HBM] * 5 + [VMEM] * 2,
            {len(ins) + i: i for i in range(len(stores))},
        )
        stores[:] = made[:5]
        return made[5:]

    terms, y_terms = {}, {}

    def sum_tokens(k, own, back):
        made = call(
            functools.partial(token_sum_kernel, k),
            "token_sums",
            [(turned_picks, FAR), (own, FAR), (back, FAR)],
            [shape(tok_rows, model_width + 128, low)] * 4 + [shape(tok_rows, model_width, low)] * 4,
            [
                pltpu.VMEM((quad_rows, turned_width), low),
                pltpu.VMEM((rows_of, full), low),
                pltpu.VMEM((quad_rows, model_width), low),
                copies_sem(7),
            ],
            2 * rows_of * quad_rows * full,
            [VMEM] * 4 + [HBM] * 4,
        )
        for i, p in enumerate(PLANE):
            terms[(k, *p)] = [made[i]]
            y_terms[(k, *p)] = [made[4 + i]]
        return made[0]

    def row_product(left, right, *earlier):
        return lax.dot_general(after(left, *earlier), right, TN, preferred_element_type=wide)[None]

    own, other = pick_tokens(0)
    chain.add(other)
    (back,) = chain.gather([(token_held, TOKEN_ROUNDS[2])], [(other, core_swap)])
    own, sent = run_experts(0, own, back)
    chain.add(sent)
    (back,) = chain.gather([(token_held, TOKEN_ROUNDS[3])], [(sent, core_swap)])
    summed = sum_tokens(0, own, back)
    chain.gather([(cot_held, TOKEN_ROUNDS[3])])
    own, other = pick_tokens(1, summed)
    (back,) = chain.gather([(token_held, TOKEN_ROUNDS[4])], [(other, core_swap)])
    own, sent = run_experts(1, own, back)
    chain.add(own)
    chain.gather([(cot_held, TOKEN_ROUNDS[4])])
    own_two, other_two = pick_tokens(2, sent)
    back, back_two = chain.send([sent, other_two], [core_swap] * 2)
    first_own, first_back = own, back
    own, sent = run_experts(2, own_two, back_two)
    own_three, other_three = pick_tokens(3, sent)
    back, back_three = chain.send([sent, other_three], [core_swap] * 2)
    sum_tokens(1, after(first_own, sent), first_back)
    sum_tokens(2, own, back)
    chain.scatter([(terms, RETURN_ROUNDS[0]), (y_terms, OUTPUT_ROUNDS[0])])
    own, sent = run_experts(3, own_three, back_three)
    all_rows, all_act, all_grads, all_gate, all_up = stores
    (back,) = chain.send([sent], [core_swap])
    sum_tokens(3, own, back)
    weight_grads = []
    for moves, pair in zip(
        RETURN_ROUNDS[1:], ((all_act, all_grads), (all_rows, all_gate), (all_rows, all_up), None)
    ):
        chain.scatter([(terms, moves)])
        if pair:
            weight_grads.append(row_product(*pair, *chain.values))
            chain.add(weight_grads[-1])
    grad_down, grad_gate, grad_up = weight_grads

    summed = plus(*terms[0, 0, 0])
    gate_parts = summed[:, model_width:]
    grad_gates = gate_parts[:, :expert_count] + gate_parts[:, expert_count : 2 * expert_count]
    grad_logits = gate_dense * (
        grad_gates - jnp.sum(gate_dense * grad_gates, axis=1, keepdims=True)
    )
    router_wide = router_rows[:, :expert_count].astype(wide)
    grad_moe_in = summed[:, :model_width] + jnp.einsum(
        "te,de->td", grad_logits, router_wide, precision=HIGH
    )

    grad_hidden_norm, grad_feed_gain = experts_back(grad_moe_in)
    grad_hidden = grad_output + grad_hidden_norm
    grad_own = grad_hidden.astype(low)
    chain.scatter([(y_terms, OUTPUT_ROUNDS[1])])
    chain.add(grad_own)
    far, swapped = chain.scatter(
        [(y_terms, OUTPUT_ROUNDS[2])], [(grad_own, z_pair), (grad_own, core_swap)]
    )

    grad_router = jnp.einsum(
        "td,te->ed", moe_in.astype(wide), after(grad_logits, grad_own), precision=HIGH
    )
    (far_swapped,) = chain.scatter([(y_terms, OUTPUT_ROUNDS[3])], [(far, core_swap)])
    grad_branch = [grad_own, swapped, far, far_swapped]

    def block_products(left_blocks, right, rest, name):
        width = right.shape[1] + (0 if rest is None else 128)
        return call(
            functools.partial(block_product_kernel, rest is not None),
            name,
            [(weight_ids, SMEM), (right, VMEM)]
            + [(b, FAR) for b in left_blocks]
            + ([] if rest is None else [(rest, VMEM)]),
            [shape(tok_rows, width, low)] * 16,
            [pltpu.VMEM((both, model_width), low), copies_sem(4)],
            2 * both * model_width * right.shape[1],
        )

    out_products = block_products(grad_branch, attended, None, "out_weight_grad")
    out_terms = {b: [block] for b, block in zip(BLOCKS, out_products)}
    chain.add(out_products[0])
    (router_part,) = chain.scatter(
        [(y_terms, OUTPUT_ROUNDS[4]), (out_terms, WEIGHT_RETURNS[0])], [(grad_router, core_swap)]
    )
    grad_router = grad_router + router_part
    (grad_attended,) = call(
        attended_grad_kernel,
        "attended_grad",
        [(weight_ids, SMEM)]
        + [(b, FAR) for b in (after(grad_branch[0], out_products[0]), *grad_branch[1:])]
        + [(b, HBM) for b in out_blocks],
        [shape(both, query_cols, low)],
        [
            pltpu.VMEM((both, model_width), low),
            pltpu.VMEM((query_cols, model_width), low),
            copies_sem(20),
        ],
        2 * both * model_width * query_cols,
    )
    chain.add(grad_attended)
    (router_part,) = chain.scatter([(out_terms, WEIGHT_RETURNS[1])], [(grad_router, z_pair)])
    grad_rest = jnp.pad(grad_router + router_part, ((0, 128 - expert_count), (0, 0)))
    grad_raw, query_gain_grad, key_gain_grad = call(
        functools.partial(backward_kernel, head_count),
        "attention_backward",
        [(core_id, SMEM), (raw, VMEM), (after(grad_attended, *chain.values), VMEM)] + turns,
        [shape(both, raw_cols, low), shape(1, head_width, wide), shape(1, head_width, wide)],
        [pltpu.VMEM((length, head_width), wide), pltpu.VMEM((length, head_width), wide)],
        10 * both * length * query_cols,
    )
    chain.add(grad_raw)
    chain.scatter([(out_terms, WEIGHT_RETURNS[2])])
    raw_products = block_products(
        sequence, after(grad_raw, *chain.values), grad_rest, "raw_weight_grad"
    )
    raw_terms = {b: [block] for b, block in zip(BLOCKS, raw_products)}
    chain.add(raw_products[0])
    chain.scatter([(raw_terms, WEIGHT_RETURNS[0]), (y_terms, OUTPUT_ROUNDS[5])])
    sent, kept, attention_part = call(
        normed_grad_kernel,
        "normed_grad",
        [
            (weight_ids, SMEM),
            (after(grad_raw, *chain.values), VMEM),
            (attention_gain[None, :], VMEM),
        ]
        + [(b, FAR) for b in sequence]
        + [(b, HBM) for b in blocks],
        [
            shape(length, model_width, low),
            shape(length, model_width, wide),
            shape(1, model_width, wide),
        ],
        [
            pltpu.VMEM((model_width, raw_cols + 128), low),
            pltpu.VMEM((both, model_width), low),
            copies_sem(20),
        ],
        2 * both * model_width * raw_cols,
    )
    chain.add(kept)
    gains = jnp.concatenate(
        [attention_part[0], grad_feed_gain, query_gain_grad[0], key_gain_grad[0]]
    ).reshape(-1, head_width)
    from_core, gain_part = chain.scatter(
        [(out_terms, WEIGHT_RETURNS[3])], [(sent, core_swap), (gains, core_swap)]
    )
    pair_total = kept + from_core.astype(wide)
    gains = gains + gain_part
    from_pair, gain_part = chain.scatter(
        [(raw_terms, WEIGHT_RETURNS[1])],
        [(pair_total[tok_rows:].astype(low), z_pair), (gains, x_swap)],
    )
    gains = gains + gain_part
    chain.scatter([(raw_terms, WEIGHT_RETURNS[2]), (out_terms, WEIGHT_RETURNS[4])])
    grad_normed = pair_total[:tok_rows] + from_pair.astype(wide)
    grad_inputs_norm, _ = attention_back(grad_normed)
    grad_inputs = grad_hidden + grad_inputs_norm
    gains = gains + y_swap(after(gains, *chain.values))
    chain.add(grad_inputs, gains)
    out_theirs = plus(*out_terms[1, 0, 0]).astype(low)
    out_theirs, gain_part = chain.scatter(
        [(raw_terms, WEIGHT_RETURNS[3])], [(out_theirs, z_pair), (gains, z_pair)]
    )
    gains = gains + gain_part
    raw_theirs = plus(*raw_terms[1, 0, 0]).astype(low)
    raw_theirs, gain_part = chain.scatter(
        [(raw_terms, WEIGHT_RETURNS[4])], [(raw_theirs, z_pair), (gains, z_far)]
    )
    gains = (gains + gain_part).reshape(-1)
    output = (hidden + plus(*y_terms[0, 0, 0])).astype(low)
    grad_out_weight = in_order(plus(*out_terms[0, 0, 0]), out_theirs.astype(wide), 1).T
    mine, theirs = plus(*raw_terms[0, 0, 0]), raw_theirs.astype(wide)
    spans = ((0, query_cols), (query_cols, query_cols + key_cols), (query_cols + key_cols, raw_cols))
    grad_query_weight, grad_key_weight, grad_value_weight = [
        in_order(mine[:, a:b], theirs[:, a:b], 1) for a, b in spans
    ]
    router_share = mine[:, raw_cols : raw_cols + expert_count]
    return (
        output,
        grad_inputs,
        gains[:model_width],
        grad_query_weight,
        grad_key_weight,
        grad_value_weight,
        gains[2 * model_width : 2 * model_width + head_width],
        gains[2 * model_width + head_width :],
        grad_out_weight,
        gains[model_width : 2 * model_width],
        router_share,
        grad_gate,
        grad_up,
        grad_down,
    )


def solution(mesh):
    in_specs = (
        P(("dp", "tensor"), None),
        P(),
        P("dp", "tensor"),
        P("dp", "tensor"),
        P("dp", "tensor"),
        P(),
        P(),
        P("tensor", "dp"),
        P(),
        P("dp", None),
        P(("dp", "tensor"), None, None),
        P(("dp", "tensor"), None, None),
        P(("dp", "tensor"), None, None),
        P(("dp", "tensor"), None),
        P(("dp", "tensor"), None),
    )
    out_specs = (
        P(("dp", "tensor"), None),
        P(("dp", "tensor"), None),
        P(),
        P("dp", "tensor"),
        P("dp", "tensor"),
        P("dp", "tensor"),
        P(),
        P(),
        P("tensor", "dp"),
        P(),
        P("dp", None),
        P(("dp", "tensor"), None, None),
        P(("dp", "tensor"), None, None),
        P(("dp", "tensor"), None, None),
    )
    fits = mesh.shape["dp"] == 16 and mesh.shape["tensor"] == 2
    local = local_sixteen if fits else local_any
    return jax.shard_map(local, mesh=mesh, in_specs=in_specs, out_specs=out_specs, check_vma=False)
```

```python
import functools
import math

import jax
import jax.numpy as jnp
from jax import lax
from jax.experimental import pallas as pl
from jax.experimental.pallas import tpu as pltpu
from jax.sharding import PartitionSpec as P

EPS = 1e-06
THETA = 1000000.0
HIGH = lax.Precision.HIGHEST
block_limit = 512


def rms_scale(values, scales):
    inverse = lax.rsqrt(jnp.mean(values * values, axis=-1, keepdims=True) + EPS)
    return values * inverse * scales


def rope_tables(length, columns):
    halfway = columns // 2
    frequency = THETA ** (-(jnp.arange(halfway, dtype=jnp.float32) * 2.0 / columns))
    angles = jnp.arange(length, dtype=jnp.float32)[:, None] * frequency[None, :]
    return (jnp.cos(angles), jnp.sin(angles))


def head_prep(raw_rows, scales, cosine_table, sine_table):
    length = raw_rows.shape[0]
    columns = scales.shape[0]
    shaped = rms_scale(raw_rows.reshape(length, -1, columns), scales)
    halfway = columns // 2
    leading = shaped[..., :halfway]
    second = shaped[..., halfway:]
    cos_part = cosine_table[:, None, :]
    sin_part = sine_table[:, None, :]
    turned = jnp.concatenate(
        [leading * cos_part - second * sin_part, second * cos_part + leading * sin_part], axis=-1
    )
    return turned.reshape(length, -1)


def masked_scores(offset, block_rows, queries, key_rows, score_scale):
    scores = (
        jnp.einsum("qkgd,ckd->kgqc", queries, key_rows, preferred_element_type=jnp.float32)
        * score_scale
    )
    row_places = offset + jnp.arange(block_rows, dtype=jnp.int32)
    key_places = jnp.arange(key_rows.shape[0], dtype=jnp.int32)
    allowed = key_places[None, :] <= row_places[:, None]
    return (queries, jnp.where(allowed, scores, -1e30))


def slot_layout(routes, expert_count, capacity):
    flat_routes = routes.reshape(-1)
    onehot = (flat_routes[:, None] == jnp.arange(expert_count, dtype=jnp.int32)[None, :]).astype(
        jnp.int32
    )
    position = jnp.sum((jnp.cumsum(onehot, axis=0) - onehot) * onehot, axis=1)
    return flat_routes * capacity + position


def route_rows(buffer):
    return lax.all_to_all(buffer, ("dp", "tensor"), split_axis=0, concat_axis=0, tiled=True)


def local_any(
    inputs,
    attention_gain,
    query_weight,
    key_weight,
    value_weight,
    query_gain,
    key_gain,
    out_weight,
    feedforward_gain,
    router_weight,
    gate_weight,
    up_weight,
    down_weight,
    routes,
    cotangent,
):
    tok_rows, model_width = inputs.shape
    head_width = query_gain.shape[0]
    top_count = routes.shape[1]
    expert_count = router_weight.shape[1]
    local_experts = gate_weight.shape[0]
    capacity = tok_rows * top_count * 11 // (expert_count * 8)
    full_query, full_key, full_value, full_out, full_router = (
        lax.all_gather(query_weight, "dp", axis=0, tiled=True),
        lax.all_gather(key_weight, "dp", axis=0, tiled=True),
        lax.all_gather(value_weight, "dp", axis=0, tiled=True),
        lax.all_gather(out_weight, "dp", axis=1, tiled=True),
        lax.all_gather(router_weight, "dp", axis=0, tiled=True),
    )
    inputs_float = inputs.astype(jnp.float32)
    normed_attention, attention_back = jax.vjp(rms_scale, inputs_float, attention_gain)
    sequence = lax.all_gather(normed_attention.astype(jnp.bfloat16), "tensor", axis=0, tiled=True)
    length = sequence.shape[0]
    query_raw = jnp.dot(sequence, full_query, preferred_element_type=jnp.float32)
    key_raw = jnp.dot(sequence, full_key, preferred_element_type=jnp.float32)
    value_raw = jnp.dot(sequence, full_value, preferred_element_type=jnp.float32)
    cosine_table, sine_table = rope_tables(length, head_width)

    def prepare(raw_rows, scales):
        return head_prep(raw_rows, scales, cosine_table, sine_table)

    query_ready, query_back = jax.vjp(prepare, query_raw, query_gain)
    key_ready, key_back = jax.vjp(prepare, key_raw, key_gain)
    kv_heads = key_raw.shape[1] // head_width
    group_size = query_raw.shape[1] // head_width // kv_heads
    queries = query_ready.astype(jnp.bfloat16).reshape(length, kv_heads, group_size, head_width)
    key_rows = key_ready.astype(jnp.bfloat16).reshape(length, kv_heads, head_width)
    value_rows = value_raw.astype(jnp.bfloat16).reshape(length, kv_heads, head_width)
    score_scale = head_width ** (-0.5)
    block_rows = min(block_limit, length)
    block_count = length // block_rows
    offsets = jnp.arange(block_count, dtype=jnp.int32) * block_rows

    def forward_block(offset):
        query_block, masked = masked_scores(offset, block_rows, queries, key_rows, score_scale)
        peak_value = jnp.max(masked, axis=-1, keepdims=True)
        exp_total = jnp.sum(jnp.exp(masked - peak_value), axis=-1, keepdims=True)
        log_total = peak_value + jnp.log(exp_total)
        soft_weights = jnp.exp(masked - log_total).astype(jnp.bfloat16)
        mixture = jnp.einsum(
            "kgqc,ckd->qkgd", soft_weights, value_rows, preferred_element_type=jnp.float32
        )
        return (mixture, log_total)

    mixed_blocks, log_totals = lax.map(forward_block, offsets)
    attended = mixed_blocks.reshape(length, -1).astype(jnp.bfloat16)
    branch = lax.psum_scatter(
        jnp.dot(attended, full_out, preferred_element_type=jnp.float32).astype(jnp.bfloat16),
        "tensor",
        scatter_dimension=0,
        tiled=True,
    ).astype(jnp.float32)
    hidden = inputs_float + branch
    normed_experts, experts_back = jax.vjp(rms_scale, hidden, feedforward_gain)
    moe_in = normed_experts.astype(jnp.bfloat16)
    logits = jnp.dot(moe_in, full_router, preferred_element_type=jnp.float32)
    onehot_routes = (
        routes[:, :, None] == jnp.arange(expert_count, dtype=jnp.int32)[None, None, :]
    ).astype(jnp.float32)
    chosen = jnp.einsum("tke,te->tk", onehot_routes, logits, precision=HIGH)
    gate_values = jax.nn.softmax(chosen, axis=-1)
    slots = slot_layout(routes, expert_count, capacity)
    buffer_shape = (expert_count // local_experts, local_experts, capacity, model_width)
    dispatch = (
        jnp.zeros((expert_count * capacity, model_width), jnp.bfloat16)
        .at[slots]
        .set(jnp.repeat(moe_in, top_count, axis=0))
    )
    received = route_rows(dispatch.reshape(buffer_shape))
    gate_pre = jnp.einsum(
        "secd,edf->secf", received, gate_weight, preferred_element_type=jnp.float32
    )
    up_pre = jnp.einsum("secd,edf->secf", received, up_weight, preferred_element_type=jnp.float32)
    sigmoid_gate = jax.nn.sigmoid(gate_pre)
    silu_gate = gate_pre * sigmoid_gate
    activated = (silu_gate * up_pre).astype(jnp.bfloat16)
    expert_out = jnp.einsum(
        "secf,efd->secd", activated, down_weight, preferred_element_type=jnp.float32
    ).astype(jnp.bfloat16)
    returned = route_rows(expert_out).reshape(expert_count * capacity, model_width)
    picked = returned[slots].reshape(tok_rows, top_count, model_width).astype(jnp.float32)
    mixture_out = jnp.sum(gate_values[:, :, None] * picked, axis=1)
    output = (hidden + mixture_out).astype(jnp.bfloat16)
    grad_output = cotangent.astype(jnp.float32)
    grad_gates = jnp.sum(picked * grad_output[:, None, :], axis=2)
    grad_picks = (
        (gate_values[:, :, None] * grad_output[:, None, :])
        .astype(jnp.bfloat16)
        .reshape(-1, model_width)
    )
    grad_dispatch = (
        jnp.zeros((expert_count * capacity, model_width), jnp.bfloat16).at[slots].set(grad_picks)
    )
    grad_received = route_rows(grad_dispatch.reshape(buffer_shape))
    grad_act = jnp.einsum(
        "secd,efd->secf", grad_received, down_weight, preferred_element_type=jnp.float32
    )
    grad_down = jnp.einsum(
        "secf,secd->efd", activated, grad_received, preferred_element_type=jnp.float32
    )
    grad_gate_pre = (
        grad_act * up_pre * sigmoid_gate * (1.0 + gate_pre * (1.0 - sigmoid_gate))
    ).astype(jnp.bfloat16)
    grad_up_pre = (grad_act * silu_gate).astype(jnp.bfloat16)
    grad_gate = jnp.einsum(
        "secd,secf->edf", received, grad_gate_pre, preferred_element_type=jnp.float32
    )
    grad_up = jnp.einsum(
        "secd,secf->edf", received, grad_up_pre, preferred_element_type=jnp.float32
    )
    grad_sent = jnp.einsum(
        "secf,edf->secd", grad_gate_pre, gate_weight, preferred_element_type=jnp.float32
    )
    grad_sent = (
        grad_sent
        + jnp.einsum("secf,edf->secd", grad_up_pre, up_weight, preferred_element_type=jnp.float32)
    ).astype(jnp.bfloat16)
    grad_back = route_rows(grad_sent).reshape(expert_count * capacity, model_width)
    grad_moe_in = jnp.sum(
        grad_back[slots].reshape(tok_rows, top_count, model_width).astype(jnp.float32), axis=1
    )
    grad_chosen = gate_values * (
        grad_gates - jnp.sum(gate_values * grad_gates, axis=1, keepdims=True)
    )
    grad_logits = jnp.einsum("tk,tke->te", grad_chosen, onehot_routes, precision=HIGH)
    router_float = full_router.astype(jnp.float32)
    grad_moe_in = grad_moe_in + jnp.einsum("te,de->td", grad_logits, router_float, precision=HIGH)
    grad_router = jnp.einsum("td,te->de", moe_in.astype(jnp.float32), grad_logits, precision=HIGH)
    grad_hidden_norm, grad_experts_gain = experts_back(grad_moe_in)
    grad_hidden = grad_output + grad_hidden_norm
    grad_branch = lax.all_gather(grad_hidden.astype(jnp.bfloat16), "tensor", axis=0, tiled=True)
    grad_attended = jnp.einsum(
        "td,ad->ta", grad_branch, full_out, preferred_element_type=jnp.float32
    ).astype(jnp.bfloat16)
    grad_blocks = grad_attended.reshape(block_count, block_rows, kv_heads, group_size, head_width)

    def backward_block(carry, item):
        key_sum, value_sum = carry
        offset, log_total, grad_block = item
        query_block, masked = masked_scores(offset, block_rows, queries, key_rows, score_scale)
        soft_weights = jnp.exp(masked - log_total)
        soft_low = soft_weights.astype(jnp.bfloat16)
        grad_soft = jnp.einsum(
            "qkgd,ckd->kgqc", grad_block, value_rows, preferred_element_type=jnp.float32
        )
        inner_sum = jnp.sum(soft_weights * grad_soft, axis=-1, keepdims=True)
        grad_scores = (soft_weights * (grad_soft - inner_sum)).astype(jnp.bfloat16)
        grad_query_block = (
            jnp.einsum("kgqc,ckd->qkgd", grad_scores, key_rows, preferred_element_type=jnp.float32)
            * score_scale
        )
        key_sum = (
            key_sum
            + jnp.einsum(
                "kgqc,qkgd->ckd", grad_scores, query_block, preferred_element_type=jnp.float32
            )
            * score_scale
        )
        value_sum = value_sum + jnp.einsum(
            "kgqc,qkgd->ckd", soft_low, grad_block, preferred_element_type=jnp.float32
        )
        return ((key_sum, value_sum), grad_query_block)

    zero_rows = jnp.zeros((length, kv_heads, head_width), jnp.float32)
    (key_sum, value_sum), grad_query_blocks = lax.scan(
        backward_block, (zero_rows, zero_rows), (offsets, log_totals, grad_blocks)
    )
    grad_query_raw, grad_query_gain = query_back(grad_query_blocks.reshape(length, -1))
    grad_key_raw, grad_key_gain = key_back(key_sum.reshape(length, -1))
    grad_query_low = grad_query_raw.astype(jnp.bfloat16)
    grad_key_low = grad_key_raw.astype(jnp.bfloat16)
    grad_value_low = value_sum.reshape(length, -1).astype(jnp.bfloat16)
    total = jnp.einsum("tc,dc->td", grad_query_low, full_query, preferred_element_type=jnp.float32)
    total = total + jnp.einsum(
        "tc,dc->td", grad_key_low, full_key, preferred_element_type=jnp.float32
    )
    grad_sequence = lax.psum_scatter(
        (
            total
            + jnp.einsum(
                "tc,dc->td", grad_value_low, full_value, preferred_element_type=jnp.float32
            )
        ).astype(jnp.bfloat16),
        "tensor",
        scatter_dimension=0,
        tiled=True,
    ).astype(jnp.float32)
    grad_inputs_norm, grad_attention_gain = attention_back(grad_sequence)
    grad_inputs = grad_hidden + grad_inputs_norm
    query_cols = grad_query_low.shape[1]
    key_cols = grad_key_low.shape[1]
    grad_raw_all = jnp.concatenate([grad_query_low, grad_key_low, grad_value_low], axis=1)
    inward = jnp.einsum("td,tc->dc", sequence, grad_raw_all, preferred_element_type=jnp.float32)
    outward = jnp.einsum("td,ta->da", grad_branch, attended, preferred_element_type=jnp.float32)
    owned = lax.psum_scatter(
        jnp.concatenate([inward, outward], axis=1), "dp", scatter_dimension=0, tiled=True
    )
    grad_query_weight = owned[:, :query_cols]
    grad_key_weight = owned[:, query_cols : query_cols + key_cols]
    grad_value_weight = owned[:, query_cols + key_cols : query_cols + 2 * key_cols]
    grad_out_weight = owned[:, query_cols + 2 * key_cols :].T
    router_total, attention_total, query_total, key_total, experts_total = lax.psum(
        (grad_router, grad_attention_gain, grad_query_gain, grad_key_gain, grad_experts_gain),
        ("dp", "tensor"),
    )
    router_rows = router_weight.shape[0]
    router_share = lax.dynamic_slice_in_dim(
        router_total, lax.axis_index("dp") * router_rows, router_rows, 0
    )
    return (
        output,
        grad_inputs,
        attention_total,
        grad_query_weight,
        grad_key_weight,
        grad_value_weight,
        query_total,
        key_total,
        grad_out_weight,
        experts_total,
        router_share,
        grad_gate,
        grad_up,
        grad_down,
    )


low, wide = jnp.bfloat16, jnp.float32
Z_RING = tuple((i, (i + 4) % 16) for i in range(16))
Z_PAIR = tuple((i, i ^ 4) for i in range(16))
Z_FAR = tuple((i, i ^ 8) for i in range(16))
Y_PAIR = tuple((i, i ^ 2) for i in range(16))
X_PAIR = tuple((i, i ^ 1) for i in range(16))
BLOCKS = tuple((k, dy, dx) for k in range(4) for dy in range(2) for dx in range(2))
PLANE = tuple((dy, dx) for dy in range(2) for dx in range(2))
OVER_X = (1, 2)
ROOM = 8 * 2**20
WHOLE = 60 * 2**20
TILE = 256
WIDE = 512
HIDDEN_TILE = 768
NT = (((1,), (1,)), ((), ()))
TN = (((0,), (0,)), ((), ()))


def z_next(block):
    return lax.ppermute(block, "dp", Z_RING)


def z_pair(block):
    return lax.ppermute(block, "dp", Z_PAIR)


def z_far(block):
    return lax.ppermute(block, "dp", Z_FAR)


def y_swap(block):
    return lax.ppermute(block, "dp", Y_PAIR)


def x_swap(block):
    return lax.ppermute(block, "dp", X_PAIR)


def core_swap(block):
    return lax.ppermute(block, "tensor", ((0, 1), (1, 0)))


def after(value, *earlier):
    return lax.optimization_barrier((value, *earlier))[0]


def plus(own, *others):
    total = own.astype(wide)
    for other in others:
        total = total + other.astype(wide)
    return total


TOKEN_ROUNDS = (
    (((0, 0, 0), (0, 0, 1), x_swap), ((0, 0, 0), (0, 1, 0), y_swap), ((0, 0, 0), (1, 0, 0), z_next)),
    (((1, 0, 0), (1, 0, 1), x_swap), ((0, 0, 1), (0, 1, 1), y_swap), ((1, 0, 0), (2, 0, 0), z_next)),
    (((2, 0, 0), (2, 0, 1), x_swap), ((1, 0, 0), (1, 1, 0), y_swap), ((2, 0, 0), (3, 0, 0), z_next)),
    (((3, 0, 0), (3, 0, 1), x_swap), ((2, 0, 0), (2, 1, 0), y_swap), ((0, 1, 1), (1, 1, 1), z_next)),
    (((2, 1, 0), (2, 1, 1), x_swap), ((3, 0, 1), (3, 1, 1), y_swap), ((2, 1, 0), (3, 1, 0), z_next)),
)
WEIGHT_ROUNDS = (
    (
        ((0, 0, 0), (0, 0, 1), x_swap),
        ((0, 0, 0), (0, 1, 0), y_swap),
        ((0, 0, 0), (2, 0, 0), z_far, True),
    ),
    (
        ((1, 0, 0), (1, 0, 1), x_swap),
        ((1, 0, 0), (1, 1, 0), y_swap),
        ((1, 0, 0), (3, 0, 0), z_far, True),
        ((0, 0, 1), (0, 1, 1), y_swap),
    ),
    (
        ((2, 0, 0), (2, 0, 1), x_swap),
        ((2, 0, 0), (2, 1, 0), y_swap),
        ((1, 1, 0), (1, 1, 1), x_swap),
    ),
    (
        ((3, 0, 0), (3, 1, 0), y_swap),
        ((3, 0, 0), (3, 0, 1), x_swap),
        ((2, 0, 1), (2, 1, 1), y_swap),
    ),
    (((3, 1, 0), (3, 1, 1), x_swap),),
)
SHORT_ROUNDS = (
    (*WEIGHT_ROUNDS[0][:2],),
    (((0, 0, 0), (2, 0, 0), z_far, True), *WEIGHT_ROUNDS[1][:2], WEIGHT_ROUNDS[1][3]),
    (((1, 0, 0), (3, 0, 0), z_far), *WEIGHT_ROUNDS[2]),
    (*WEIGHT_ROUNDS[3], ((1, 1, 1), (3, 1, 1), z_far)),
)
WEIGHT_RETURNS = (
    (((3, 1, 1), (3, 1, 0), x_swap),),
    (
        ((3, 1, 0), (3, 0, 0), y_swap),
        ((3, 0, 1), (3, 0, 0), x_swap),
        ((2, 1, 1), (2, 0, 1), y_swap),
    ),
    (
        ((3, 0, 0), (1, 0, 0), z_far),
        ((2, 0, 1), (2, 0, 0), x_swap),
        ((2, 1, 0), (2, 0, 0), y_swap),
        ((1, 1, 1), (1, 1, 0), x_swap),
    ),
    (
        ((2, 0, 0), (0, 0, 0), z_far),
        ((1, 1, 0), (1, 0, 0), y_swap),
        ((1, 0, 1), (1, 0, 0), x_swap),
        ((0, 1, 1), (0, 0, 1), y_swap),
    ),
    (((0, 0, 1), (0, 0, 0), x_swap), ((0, 1, 0), (0, 0, 0), y_swap)),
)


RETURN_ROUNDS = (
    (((1, 1, 1), (1, 0, 1), y_swap), ((0, 1, 1), (0, 1, 0), x_swap), ((1, 1, 0), (2, 1, 0), z_next)),
    (((1, 0, 1), (1, 0, 0), x_swap), ((2, 1, 1), (2, 0, 1), y_swap), ((2, 1, 0), (2, 0, 0), y_swap)),
    (((2, 0, 1), (2, 0, 0), x_swap), ((3, 1, 1), (3, 0, 1), y_swap), ((1, 0, 0), (2, 0, 0), z_next)),
    (((3, 0, 1), (3, 0, 0), x_swap), ((3, 1, 0), (3, 0, 0), y_swap), ((2, 0, 0), (3, 0, 0), z_next)),
    (((0, 0, 1), (0, 0, 0), x_swap), ((0, 1, 0), (0, 0, 0), y_swap), ((3, 0, 0), (0, 0, 0), z_next)),
)
OUTPUT_ROUNDS = (
    (((3, 1, 1), (3, 1, 0), x_swap), ((1, 1, 1), (1, 0, 1), y_swap), ((1, 1, 0), (2, 1, 0), z_next)),
    (((1, 0, 1), (1, 0, 0), x_swap), ((2, 1, 1), (2, 0, 1), y_swap)),
    (((2, 0, 1), (2, 0, 0), x_swap), ((2, 1, 0), (2, 0, 0), y_swap), ((1, 0, 0), (2, 0, 0), z_next)),
    (((3, 0, 1), (3, 0, 0), x_swap), ((3, 1, 0), (3, 0, 0), y_swap), ((2, 0, 0), (3, 0, 0), z_next)),
    (((0, 1, 1), (0, 1, 0), x_swap),),
    (((0, 0, 1), (0, 0, 0), x_swap), ((0, 1, 0), (0, 0, 0), y_swap), ((3, 0, 0), (0, 0, 0), z_next)),
)


class Chain:
    def __init__(self):
        self.earlier = []
        self.late = []
        self.values = []

    def add(self, *values):
        self.earlier.extend(values)

    def send(self, values, ways, late=()):
        values = lax.optimization_barrier((*values, *self.earlier))[: len(values)]
        self.values = values
        results = [way(value) for value, way in zip(values, ways)]
        self.earlier = self.late + [r for i, r in enumerate(results) if i not in late]
        self.late = [results[i] for i in late]
        return results

    def round(self, values, moves, others):
        late = [i for i, move in enumerate(moves) if len(move) > 3]
        values = values + [value for value, _ in others]
        ways = [move[2] for move in moves] + [way for _, way in others]
        results = self.send(values, ways, late)
        return results[: len(moves)], results[len(moves) :]

    def gather(self, pairs, others=()):
        values = [held[move[0]] for held, moves in pairs for move in moves]
        moves = [move for _, moves in pairs for move in moves]
        results, rest = self.round(values, moves, others)
        for (held, end), result in zip([(h, m[1]) for h, ms in pairs for m in ms], results):
            held[end] = result
        return rest

    def scatter(self, pairs, others=(), later=None):
        if later is not None:
            for terms, moves in pairs:
                for move in moves:
                    terms[move[0]][-1] = after(terms[move[0]][-1], later)
        values = totals([terms[move[0]] for terms, moves in pairs for move in moves])
        moves = [move for _, moves in pairs for move in moves]
        results, rest = self.round(values, moves, others)
        for (terms, end), result in zip([(t, m[1]) for t, ms in pairs for m in ms], results):
            terms[end].append(result)
        return rest


def sum_kernel(counts, *refs):
    outs = refs[sum(counts) :]
    for count, out in zip(counts, outs):
        terms, refs = refs[:count], refs[count:]
        out[...] = plus(*[term[...] for term in terms]).astype(out.dtype)


def totals(lists):
    several = [terms for terms in lists if len(terms) > 1]
    if not several:
        return [terms[0] for terms in lists]
    operands = [term for terms in several for term in terms]
    rows = operands[0].shape[0] // 4
    whole = [(a.shape[0] // 4, a.shape[1]) for a in operands]
    specs = [pl.BlockSpec(block, lambda i: (i, 0)) for block in whole]
    firsts = [terms[0] for terms in several]
    sums = pl.pallas_call(
        functools.partial(sum_kernel, [len(terms) for terms in several]),
        grid=(4,),
        out_shape=[jax.ShapeDtypeStruct(a.shape, low) for a in firsts],
        in_specs=specs,
        out_specs=[pl.BlockSpec((rows, a.shape[1]), lambda i: (i, 0)) for a in firsts],
        name="sums",
        compiler_params=pltpu.CompilerParams(vmem_limit_bytes=2 * ROOM),
    )(*operands)
    sums = list(sums)
    return [sums.pop(0) if len(terms) > 1 else terms[0] for terms in lists]


def dot(left, right, dims=None):
    if dims is None:
        return jnp.dot(left, right, preferred_element_type=wide)
    return lax.dot_general(left, right, dims, preferred_element_type=wide)


def lanes(start, size):
    return pl.ds(pl.multiple_of(start, 128), size)


def spot(ids, i):
    return pl.multiple_of(ids[i] * 128, 128)


def row_copies(ids, blocks, whole, sems):
    return [
        pltpu.make_async_copy(block, whole.at[pl.ds(spot(ids, i), 128), :], sems.at[i])
        for i, block in enumerate(blocks)
    ]


def column_copies(ids, blocks, whole, sems):
    return [
        pltpu.make_async_copy(block, whole.at[:, pl.ds(spot(ids, i), 128)], sems.at[i])
        for i, block in enumerate(blocks)
    ]


def stack_copies(blocks, whole, sems):
    rows = blocks[0].shape[0]
    return [
        pltpu.make_async_copy(block, whole.at[pl.ds(i * rows, rows), :], sems.at[i])
        for i, block in enumerate(blocks)
    ]


def start_all(copies):
    for copy in copies:
        copy.start()


def wait_all(copies):
    for copy in copies:
        copy.wait()


def head_forward(raw, gain, cosine, sine):
    inverse = lax.rsqrt(jnp.mean(raw * raw, axis=-1, keepdims=True) + EPS)
    unit = raw * inverse
    shaped = unit * gain
    return unit, inverse, shaped * cosine + pltpu.roll(shaped, 64, 1) * sine


def head_backward(grad, unit, inverse, gain, cosine, sine):
    back = grad * cosine - pltpu.roll(grad, 64, 1) * sine
    gain_grad = jnp.sum(back * unit, axis=0, keepdims=True)
    scaled = back * gain
    return gain_grad, inverse * (scaled - unit * jnp.mean(scaled * unit, axis=-1, keepdims=True))


def causal(core, length):
    half = length // 2
    rows = lax.broadcasted_iota(jnp.int32, (length, length), 0)
    columns = lax.broadcasted_iota(jnp.int32, (length, length), 1)

    def place(i):
        return jnp.where(i < half, i + core * half, i - half + (1 - core) * half)

    return place(columns) <= place(rows)


def soft(query, key, allowed, scale):
    scores = jnp.where(allowed, dot(query, key, NT) * scale, -1e30)
    raised = jnp.exp(scores - jnp.max(scores, axis=-1, keepdims=True))
    return raised / jnp.sum(raised, axis=-1, keepdims=True)


def raw_kernel(ids, block_ids, *refs):
    seq_blocks, blocks = refs[:4], refs[4:20]
    raw, router, rest, whole, seq, sems = refs[20:]
    copies = stack_copies(seq_blocks, seq, sems.at[pl.ds(16, 4)]) + row_copies(
        ids, blocks, whole, sems
    )
    start_all(copies)
    wait_all(copies)
    width = raw.shape[1]

    @pl.loop(0, width // TILE)
    def _(j):
        span = lanes(j * TILE, TILE)
        raw[:, span] = dot(seq[...], whole[:, span])

    router[...] = whole[:, width:]
    for p in range(16):
        rest[p * 128 : (p + 1) * 128, :] = whole[pl.ds(spot(block_ids, p), 128), width:]


def forward_kernel(head_count, core, raw, cosine, sine, query_gain, key_gain, attended):
    length = raw.shape[0] // 2
    key_start = head_count * 128
    allowed = causal(core[0], length)
    scale = 128 ** (-0.5)
    for s in range(2):
        span = slice(s * length, (s + 1) * length)
        turn = (cosine[...], sine[...])
        key_raw = raw[span, key_start : key_start + 128]
        key = head_forward(key_raw, key_gain[...], *turn)[2].astype(low)
        value = raw[span, key_start + 128 : key_start + 256].astype(low)

        @pl.loop(0, head_count, unroll=2)
        def _(h):
            columns = lanes(h * 128, 128)
            query = head_forward(raw[span, columns], query_gain[...], *turn)[2].astype(low)
            weights = soft(query, key, allowed, scale)
            attended[span, columns] = dot(weights.astype(low), value).astype(low)


def split_rows(product, span, sent, kept):
    rows = product.shape[0] // 4
    kept[:rows, span] = product[:rows]
    sent[:rows, span] = product[rows : 2 * rows].astype(low)
    kept[rows:, span] = product[2 * rows : 3 * rows]
    sent[rows:, span] = product[3 * rows :].astype(low)


def out_kernel(ids, attended, *refs):
    blocks, (sent, kept, whole, sems) = refs[:16], refs[16:]
    copies = column_copies(ids, blocks, whole, sems)
    start_all(copies)
    wait_all(copies)

    @pl.loop(0, whole.shape[1] // WIDE)
    def _(j):
        span = lanes(j * WIDE, WIDE)
        split_rows(dot(attended[...], whole[:, span]), span, sent, kept)


def normed_grad_kernel(ids, grad_raw, gain, *refs):
    seq_blocks, blocks = refs[:4], refs[4:20]
    sent, kept, gain_grad, whole, seq, sems = refs[20:]
    copies = row_copies(ids, blocks, whole, sems) + stack_copies(
        seq_blocks, seq, sems.at[pl.ds(16, 4)]
    )
    start_all(copies)
    wait_all(copies)
    width = grad_raw.shape[1]

    @pl.loop(0, whole.shape[0] // WIDE)
    def _(j):
        span = lanes(j * WIDE, WIDE)
        product = dot(grad_raw[...], whole[span, :width], NT)
        split_rows(product, span, sent, kept)
        unit = seq[:, span].astype(wide) / gain[:, span]
        gain_grad[:, span] = jnp.sum(product * unit, axis=0, keepdims=True)


def attended_grad_kernel(ids, *refs):
    grad_blocks, blocks = refs[:4], refs[4:20]
    grad_attended, grad_branch, whole, sems = refs[20:]
    copies = stack_copies(grad_blocks, grad_branch, sems.at[pl.ds(16, 4)]) + column_copies(
        ids, blocks, whole, sems
    )
    start_all(copies)
    wait_all(copies)

    @pl.loop(0, grad_attended.shape[1] // WIDE)
    def _(j):
        span = lanes(j * WIDE, WIDE)
        grad_attended[:, span] = dot(grad_branch[...], whole[span, :], NT).astype(low)


def map_kernel(capacity, expert_count, experts, named, picks, turned_picks):
    slot_rows = 4 * capacity
    early = lax.broadcasted_iota(jnp.int32, (128, 128), 0)
    late = lax.broadcasted_iota(jnp.int32, (128, 128), 1)
    before = jnp.where(early < late, 1.0, 0.0).astype(low)
    behind = jnp.where(late < early, 1.0, 0.0).astype(low)
    slot_numbers = lax.broadcasted_iota(jnp.int32, (slot_rows, 128), 0)
    slot_lanes = lax.broadcasted_iota(jnp.int32, (128, turned_picks.shape[1]), 1)
    for b in range(16):
        k, i = b // 4, b % 4
        block = named[b * 128 : (b + 1) * 128, :]
        turned_slots = []
        for c in range(2):
            column = experts[c] + expert_count
            own_lane = lax.broadcasted_iota(jnp.int32, (8, 128), 1) == column
            hit = dot(jnp.where(own_lane, 1.0, 0.0).astype(low), block, NT)
            slot = dot(hit.astype(low), before) + float(i * capacity)
            slot = jnp.where(hit > 0.5, slot, -1.0).astype(jnp.int32)
            first = (2 * k + c) * slot_rows
            picks[first : first + slot_rows, i * 128 : (i + 1) * 128] = jnp.where(
                slot_numbers == slot[:1], 1.0, 0.0
            ).astype(low)
            mine = jnp.where(late == column, block.astype(wide), 0.0)
            hit = jnp.sum(mine, axis=1, keepdims=True)
            slot = jnp.sum(dot(behind, mine.astype(low)), axis=1, keepdims=True)
            slot = slot + float(i * capacity + c * slot_rows)
            turned_slots.append(jnp.where(hit > 0.5, slot, -1.0).astype(jnp.int32))
        either = jnp.logical_or(slot_lanes == turned_slots[0], slot_lanes == turned_slots[1])
        turned_picks[b * 128 : (b + 1) * 128, :] = jnp.where(either, 1.0, 0.0).astype(low)


def pick_kernel(k, picks_in, named, *refs):
    tokens, cots, (own, other, picks, rows, sems) = refs[:4], refs[4:8], refs[8:]
    quad_rows, full = rows.shape
    width = tokens[0].shape[1]
    copies = (
        stack_copies(tokens, rows.at[:, pl.ds(0, width)], sems.at[pl.ds(0, 4)])
        + stack_copies(cots, rows.at[:, pl.ds(width + 128, width)], sems.at[pl.ds(4, 4)])
        + [
            pltpu.make_async_copy(
                picks_in.at[pl.ds(k * picks.shape[0], picks.shape[0]), :], picks, sems.at[8]
            ),
            pltpu.make_async_copy(
                named.at[pl.ds(k * quad_rows, quad_rows), :],
                rows.at[:, pl.ds(width, 128)],
                sems.at[9],
            ),
        ]
    )
    start_all(copies)
    wait_all(copies)
    slot_rows = own.shape[0]
    for start in range(0, full, WIDE):
        span = slice(start, min(start + WIDE, full))
        made = dot(picks[...], rows[:, span]).astype(low)
        own[:, span] = made[:slot_rows]
        other[:, span] = made[slot_rows:]


def expert_kernel(expert_count, k, experts, router, *refs):
    sides, weights = refs[:2], refs[2:5]
    refs = refs[5 + (5 if k else 0) :]
    (all_rows, all_act, all_grads, all_gate, all_up, own_out, back_out) = refs[:7]
    (rows, v_gate, v_up, v_down, act, grads, gate_back, up_back) = refs[7:15]
    (gate_pre, up_pre, sig, sems) = refs[15:]
    slot_rows = own_out.shape[0]
    width, hidden = v_gate.shape
    after_width = width + 128
    spans = [slice(c * slot_rows, (c + 1) * slot_rows) for c in range(2)]
    side_copies = stack_copies(sides, rows, sems.at[pl.ds(0, 2)])
    weight_copies = [
        pltpu.make_async_copy(a, b, sems.at[2 + i])
        for i, (a, b) in enumerate(zip(weights, (v_gate, v_up, v_down)))
    ]
    start_all(side_copies + weight_copies)
    kept = []

    def keep(source, target, sem):
        copy = pltpu.make_async_copy(
            source.at[:, pl.ds(0, target.shape[1])],
            target.at[pl.ds(k * 2 * slot_rows, 2 * slot_rows), :],
            sems.at[sem],
        )
        copy.start()
        kept.append(copy)

    wait_all(side_copies)
    keep(rows, all_rows, 5)
    logits = dot(rows[:, :width], router[...])
    numbers = lax.broadcasted_iota(jnp.int32, logits.shape, 1)
    is_named = pltpu.roll(rows[:, width:after_width].astype(wide), 128 - expert_count, 1)
    is_named = jnp.logical_and(is_named > 0.5, numbers < expert_count)
    lifted = jnp.where(is_named, logits, -1e30)
    lifted = jnp.where(
        is_named, jnp.exp(lifted - jnp.max(lifted, axis=1, keepdims=True)), 0.0
    )
    mine = jnp.sum(jnp.where(numbers == experts[0], lifted, 0.0), axis=1, keepdims=True)
    gates = mine / jnp.maximum(jnp.sum(lifted, axis=1, keepdims=True), 1e-30)
    wait_all(weight_copies[:2])
    pre = dot(rows[:, :width], v_gate[...])
    up = dot(rows[:, :width], v_up[...])
    s = jax.nn.sigmoid(pre)
    gate_pre[...] = pre
    up_pre[...] = up
    sig[...] = s
    act[...] = (pre * s * up).astype(low)
    keep(act, all_act, 6)
    wait_all(weight_copies[2:])
    slot_grads = jnp.zeros((2 * slot_rows, 1), wide)
    for j in range(width // WIDE):
        span = slice(j * WIDE, (j + 1) * WIDE)
        later = slice(after_width + j * WIDE, after_width + (j + 1) * WIDE)
        out = dot(act[...], v_down[:, span]).astype(low).astype(wide)
        cot = rows[:, later].astype(wide)
        grads[:, span] = (gates * cot).astype(low)
        scaled = (gates * out).astype(low)
        own_out[:, later] = scaled[spans[0]]
        back_out[:, later] = scaled[spans[1]]
        slot_grads = slot_grads + jnp.sum(cot * out, axis=1, keepdims=True)
    keep(grads, all_grads, 7)
    back = dot(grads[...], v_down[...], NT)
    pre, s = gate_pre[...], sig[...]
    gate_back[...] = (back * up_pre[...] * s * (1.0 + pre * (1.0 - s))).astype(low)
    up_back[...] = (back * (pre * s)).astype(low)
    keep(gate_back, all_gate, 8)
    keep(up_back, all_up, 9)
    for j in range(width // WIDE):
        span = slice(j * WIDE, (j + 1) * WIDE)
        back = dot(gate_back[...], v_gate[span, :], NT) + dot(up_back[...], v_up[span, :], NT)
        back = back.astype(low)
        own_out[:, span] = back[spans[0]]
        back_out[:, span] = back[spans[1]]
    high = slot_grads.astype(low).astype(wide)
    rest = jnp.where(numbers == experts[0] + expert_count, slot_grads - high, 0.0)
    parts = jnp.where(numbers == experts[0], high, rest).astype(low)
    own_out[:, width:after_width] = parts[spans[0]]
    back_out[:, width:after_width] = parts[spans[1]]
    wait_all(kept)


def token_sum_kernel(k, turned_picks, *refs):
    sides, blocks, outputs, (picks, rows, out_rows, sems) = refs[:2], refs[2:6], refs[6:10], refs[10:]
    quad_rows, width = out_rows.shape
    copies = stack_copies(sides, rows, sems.at[pl.ds(0, 2)]) + [
        pltpu.make_async_copy(
            turned_picks.at[pl.ds(k * quad_rows, quad_rows), :], picks, sems.at[2]
        )
    ]
    start_all(copies)
    wait_all(copies)
    slots = rows.shape[0]
    size, first = blocks[0].shape
    for j in range(0, width, WIDE):
        span = slice(j, j + WIDE)
        out_rows[:, span] = dot(picks[:, :slots], rows[:, first + j : first + j + WIDE]).astype(low)
    copies = [
        pltpu.make_async_copy(out_rows.at[pl.ds(i * size, size), :], output, sems.at[3 + i])
        for i, output in enumerate(outputs)
    ]
    start_all(copies)
    for j in range(0, first, WIDE):
        span = slice(j, min(j + WIDE, first))
        made = dot(picks[:, :slots], rows[:, span]).astype(low)
        for i, block in enumerate(blocks):
            block[:, span] = made[i * size : (i + 1) * size]
    wait_all(copies)


def backward_kernel(head_count, core, raw, grad_attended, *refs):
    cosine, sine, query_gain, key_gain = refs[:4]
    grad_raw, query_gain_grad, key_gain_grad, key_sum, value_sum = refs[4:]
    length = raw.shape[0] // 2
    key_start = head_count * 128
    allowed = causal(core[0], length)
    scale = 128 ** (-0.5)
    turn = (cosine[...], sine[...])
    query_gain_grad[...] = jnp.zeros_like(query_gain_grad)
    key_gain_grad[...] = jnp.zeros_like(key_gain_grad)
    for s in range(2):
        span = slice(s * length, (s + 1) * length)
        key_raw = raw[span, key_start : key_start + 128]
        key_unit, key_inverse, key = head_forward(key_raw, key_gain[...], *turn)
        key = key.astype(low)
        value = raw[span, key_start + 128 : key_start + 256].astype(low)
        key_sum[...] = jnp.zeros_like(key_sum)
        value_sum[...] = jnp.zeros_like(value_sum)

        @pl.loop(0, head_count, unroll=2)
        def _(h):
            columns = lanes(h * 128, 128)
            unit, inverse, query = head_forward(raw[span, columns], query_gain[...], *turn)
            query = query.astype(low)
            weights = soft(query, key, allowed, scale)
            grad = grad_attended[span, columns]
            grad_soft = dot(grad, value, NT)
            inner = jnp.sum(weights * grad_soft, axis=-1, keepdims=True)
            grad_scores = (weights * (grad_soft - inner)).astype(low)
            value_sum[...] += dot(weights.astype(low), grad, TN)
            key_sum[...] += dot(grad_scores, query, TN) * scale
            grad_query = dot(grad_scores, key) * scale
            gain_grad, back = head_backward(grad_query, unit, inverse, query_gain[...], *turn)
            query_gain_grad[...] += gain_grad
            grad_raw[span, columns] = back.astype(low)

        gain_grad, back = head_backward(
            key_sum[...], key_unit, key_inverse, key_gain[...], *turn
        )
        key_gain_grad[...] += gain_grad
        grad_raw[span, key_start : key_start + 128] = back.astype(low)
        grad_raw[span, key_start + 128 : key_start + 256] = value_sum[...].astype(low)


def block_product_kernel(with_rest, ids, right, *refs):
    left_blocks, refs = refs[:4], refs[4:]
    rest, refs = (refs[0], refs[1:]) if with_rest else (None, refs)
    outs, (left, sems) = refs[:16], refs[16:]
    copies = stack_copies(left_blocks, left, sems)
    start_all(copies)
    wait_all(copies)
    width = right.shape[1]
    for i, out in enumerate(outs):
        part = left[:, pl.ds(spot(ids, i), 128)]
        out[:, :width] = dot(part, right[...], TN).astype(low)
        if with_rest:
            out[:, width:] = jnp.transpose(rest[:, pl.ds(spot(ids, i), 128)]).astype(low)


SMEM = pl.BlockSpec(memory_space=pltpu.SMEM)
VMEM = pl.BlockSpec(memory_space=pltpu.VMEM)
FAR = pl.BlockSpec(memory_space=pl.ANY)
HBM = pl.BlockSpec(memory_space=pltpu.HBM)


def call(kernel, name, ins, outs, scratch, flops, specs=None, aliases=None, alone=False):
    operands = [value for value, _ in ins]
    moved = sum(a.size * a.dtype.itemsize for a in operands + outs)
    placed = [value for value, spec in ins if spec is VMEM] + scratch
    placed += [out for out, spec in zip(outs, specs or [VMEM] * len(outs)) if spec is VMEM]
    held = sum(
        math.prod(a.shape) * jnp.dtype(a.dtype).itemsize
        for a in placed
        if jnp.issubdtype(a.dtype, jnp.floating)
    )
    return pl.pallas_call(
        kernel,
        out_shape=outs,
        in_specs=[spec for _, spec in ins],
        out_specs=specs or [VMEM] * len(outs),
        scratch_shapes=scratch,
        name=name,
        input_output_aliases=aliases or {},
        compiler_params=pltpu.CompilerParams(vmem_limit_bytes=WHOLE if alone else ROOM + held),
        cost_estimate=pl.CostEstimate(flops=flops, bytes_accessed=moved, transcendentals=0),
    )(*operands)


def shape(rows, columns, dtype):
    return jax.ShapeDtypeStruct((rows, columns), dtype)


def copies_sem(count):
    return pltpu.SemaphoreType.DMA((count,))


def local_sixteen(
    inputs,
    attention_gain,
    query_weight,
    key_weight,
    value_weight,
    query_gain,
    key_gain,
    out_weight,
    feedforward_gain,
    router_weight,
    gate_weight,
    up_weight,
    down_weight,
    routes,
    cotangent,
):
    tok_rows, model_width = inputs.shape
    head_width = query_gain.shape[0]
    top_count = routes.shape[1]
    expert_count = router_weight.shape[1]
    hidden_width = gate_weight.shape[2]
    capacity = tok_rows * top_count * 11 // (expert_count * 8)
    query_cols, key_cols = query_weight.shape[1] // 2, key_weight.shape[1] // 2
    raw_cols = query_cols + 2 * key_cols
    head_count = query_cols // head_width
    place = lax.axis_index("dp")
    core = lax.axis_index("tensor")
    z, y, x = place // 4, (place // 2) % 2, place % 2
    even = z % 2 == 0
    core_id = core.astype(jnp.int32)[None]
    block_ids = jnp.stack(
        [((z - k) % 4) * 4 + (y ^ dy) * 2 + (x ^ dx) for k, dy, dx in BLOCKS]
    ).astype(jnp.int32)
    weight_ids = jnp.stack(
        [(z ^ w) * 4 + (y ^ dy) * 2 + (x ^ dx) for w, dy, dx in BLOCKS]
    ).astype(jnp.int32)

    def halves(values, axis):
        first, second = jnp.split(values, 2, axis=axis)
        return jnp.where(even, first, second), jnp.where(even, second, first)

    def in_order(mine, theirs, axis):
        return jnp.where(
            even,
            jnp.concatenate([mine, theirs], axis=axis),
            jnp.concatenate([theirs, mine], axis=axis),
        )

    chain = Chain()
    numbers = jnp.arange(expert_count, dtype=jnp.int32)
    own_named = jnp.any(routes[:, :, None] == numbers, axis=1)
    splits = [halves(w, 1) for w in (query_weight, key_weight, value_weight)]
    rest = [
        router_weight,
        own_named.astype(low),
        jnp.zeros((tok_rows, 128 - 2 * expert_count), low),
    ]
    mine = jnp.concatenate([s[0] for s in splits] + rest, axis=1)
    theirs = jnp.concatenate([s[1] for s in splits] + rest, axis=1)
    held = {(0, 0, 0): mine}
    (held[1, 0, 0],) = chain.gather([(held, WEIGHT_ROUNDS[0])], [(theirs, z_pair)])
    inputs_float = inputs.astype(wide)
    normed_attention, attention_back = jax.vjp(rms_scale, inputs_float, attention_gain)
    normed = normed_attention.astype(low)
    chain.add(normed)
    chain.gather([(held, WEIGHT_ROUNDS[1])])
    chain.gather([(held, WEIGHT_ROUNDS[2])])
    far, swapped = chain.gather(
        [(held, WEIGHT_ROUNDS[3])], [(normed, z_pair), (normed, core_swap)]
    )
    out_mine, out_theirs = halves(out_weight, 0)
    out_held = {(0, 0, 0): out_mine}
    cot_held = {(0, 0, 0): cotangent}
    far_swapped, out_held[1, 0, 0] = chain.gather(
        [(held, WEIGHT_ROUNDS[4]), (out_held, SHORT_ROUNDS[0])],
        [(far, core_swap), (out_theirs, z_pair)],
    )
    sequence = [normed, swapped, far, far_swapped]
    blocks = [held[b] for b in BLOCKS]
    chain.gather([(out_held, SHORT_ROUNDS[1])])
    grad_output = cotangent.astype(wide)
    length = 2 * tok_rows
    own_places = jnp.arange(tok_rows, dtype=jnp.int32)
    places = jnp.concatenate([own_places + core * tok_rows, own_places + (1 - core) * tok_rows])
    halfway = head_width // 2
    frequency = THETA ** (-(jnp.arange(halfway, dtype=wide) * 2.0 / head_width))
    angles = places.astype(wide)[:, None] * frequency[None, :]
    cosine, sine = jnp.cos(angles), jnp.sin(angles)
    turns = [
        (jnp.concatenate([cosine, cosine], axis=1), VMEM),
        (jnp.concatenate([-sine, sine], axis=1), VMEM),
        (query_gain[None, :], VMEM),
        (key_gain[None, :], VMEM),
    ]
    both = 2 * length
    raw, router_rows, rest_rows = call(
        raw_kernel,
        "attention_raw",
        [(weight_ids, SMEM), (block_ids, SMEM)]
        + [(b, FAR) for b in sequence]
        + [(b, HBM) for b in blocks],
        [
            shape(both, raw_cols, wide),
            shape(model_width, 128, low),
            shape(model_width, 128, low),
        ],
        [
            pltpu.VMEM((model_width, raw_cols + 128), low),
            pltpu.VMEM((both, model_width), low),
            copies_sem(20),
        ],
        2 * both * model_width * raw_cols,
        alone=True,
    )
    chain.add(raw)
    chain.gather([(out_held, SHORT_ROUNDS[2])])
    (attended,) = call(
        functools.partial(forward_kernel, head_count),
        "attention_forward",
        [(core_id, SMEM), (raw, VMEM)] + turns,
        [shape(both, query_cols, low)],
        [],
        4 * both * length * query_cols,
    )
    chain.add(attended)
    chain.gather([(out_held, SHORT_ROUNDS[3])])
    out_blocks = [out_held[b] for b in BLOCKS]
    chain.gather([(cot_held, TOKEN_ROUNDS[0])])
    sent, kept = call(
        out_kernel,
        "attention_out",
        [(weight_ids, SMEM), (attended, VMEM)] + [(b, HBM) for b in out_blocks],
        [shape(length, model_width, low), shape(length, model_width, wide)],
        [pltpu.VMEM((query_cols, model_width), low), copies_sem(16)],
        2 * both * model_width * query_cols,
    )

    pair_total = kept + core_swap(sent).astype(wide)
    leaving = pair_total[tok_rows:].astype(low)
    from_pair = z_pair(leaving)
    chain.add(leaving)
    chain.gather([(cot_held, TOKEN_ROUNDS[1])])
    chain.gather([(cot_held, TOKEN_ROUNDS[2])])
    hidden = inputs_float + pair_total[:tok_rows] + from_pair.astype(wide)
    normed_experts, experts_back = jax.vjp(rms_scale, hidden, feedforward_gain)
    moe_in = normed_experts.astype(low)
    chain.add(moe_in)

    token_held = {(0, 0, 0): moe_in}
    chain.gather([(token_held, TOKEN_ROUNDS[0])])
    chain.gather([(token_held, TOKEN_ROUNDS[1])])
    slot_rows = 4 * capacity
    quad_rows = 4 * tok_rows
    rows_of = 2 * slot_rows
    all_slots = 4 * rows_of
    experts = jnp.stack([place * 2 + core, place * 2 + 1 - core]).astype(jnp.int32)
    w_gate, w_up, w_down = gate_weight[0], up_weight[0], down_weight[0]
    turned_width = -(-rows_of // 128) * 128
    picks, turned_picks = call(
        functools.partial(map_kernel, capacity, expert_count),
        "pick_maps",
        [(experts, SMEM), (rest_rows, VMEM)],
        [shape(all_slots, quad_rows, low), shape(model_width, turned_width, low)],
        [],
        2 * 128 * 128 * model_width,
    )

    logits = jnp.dot(moe_in, router_rows, preferred_element_type=wide)[:, :expert_count]
    lifted = jnp.where(own_named, logits, -1e30)
    lifted = jnp.where(own_named, jnp.exp(lifted - jnp.max(lifted, axis=1, keepdims=True)), 0.0)
    gate_dense = lifted / jnp.sum(lifted, axis=1, keepdims=True)

    full = 2 * model_width + 128

    def pick_tokens(k, *earlier):
        return call(
            functools.partial(pick_kernel, k),
            "picks",
            [(after(picks, *earlier), FAR), (rest_rows, FAR)]
            + [(token_held[k, dy, dx], FAR) for dy, dx in PLANE]
            + [(cot_held[k, dy, dx], HBM) for dy, dx in PLANE],
            [shape(slot_rows, full, low)] * 2,
            [
                pltpu.VMEM((rows_of, quad_rows), low),
                pltpu.VMEM((quad_rows, full), low),
                copies_sem(10),
            ],
            2 * rows_of * quad_rows * full,
            alone=k == 0,
        )

    stores = []

    def run_experts(k, own, back):
        ins = (
            [(experts, SMEM), (router_rows, VMEM), (own, FAR), (back, FAR)]
            + [(w, HBM) for w in (w_gate, w_up, w_down)]
        )
        made = call(
            functools.partial(expert_kernel, expert_count, k),
            "experts",
            ins + [(store, HBM) for store in stores],
            [
                shape(all_slots, model_width, low),
                shape(all_slots, hidden_width, low),
                shape(all_slots, model_width, low),
                shape(all_slots, hidden_width, low),
                shape(all_slots, hidden_width, low),
                shape(slot_rows, full, low),
                shape(slot_rows, full, low),
            ],
            [
                pltpu.VMEM((rows_of, full), low),
                pltpu.VMEM((model_width, hidden_width), low),
                pltpu.VMEM((model_width, hidden_width), low),
                pltpu.VMEM((hidden_width, model_width), low),
                pltpu.VMEM((rows_of, hidden_width), low),
                pltpu.VMEM((rows_of, model_width), low),
                pltpu.VMEM((rows_of, hidden_width), low),
                pltpu.VMEM((rows_of, hidden_width), low),
                pltpu.VMEM((rows_of, hidden_width), wide),
                pltpu.VMEM((rows_of, hidden_width), wide),
                pltpu.VMEM((rows_of, hidden_width), wide),
                copies_sem(10),
            ],
            12 * rows_of * model_width * hidden_width,
            [HBM] * 5 + [VMEM] * 2,
            {len(ins) + i: i for i in range(len(stores))},
        )
        stores[:] = made[:5]
        return made[5:]

    terms, y_terms = {b: [] for b in BLOCKS}, {}

    def sum_tokens(k, own, back):
        made = call(
            functools.partial(token_sum_kernel, k),
            "token_sums",
            [(turned_picks, FAR), (own, FAR), (back, FAR)],
            [shape(tok_rows, model_width + 128, low)] * 4 + [shape(tok_rows, model_width, low)] * 4,
            [
                pltpu.VMEM((quad_rows, turned_width), low),
                pltpu.VMEM((rows_of, full), low),
                pltpu.VMEM((quad_rows, model_width), low),
                copies_sem(7),
            ],
            2 * rows_of * quad_rows * full,
            [VMEM] * 4 + [HBM] * 4,
        )
        for i, p in enumerate(PLANE):
            terms[(k, *p)].append(made[i])
            y_terms[(k, *p)] = [made[4 + i]]
        return made[0]

    def row_product(left, right, *earlier):
        return lax.dot_general(after(left, *earlier), right, TN, preferred_element_type=wide)[None]

    own, other = pick_tokens(0)
    chain.add(other)
    (back,) = chain.gather([(token_held, TOKEN_ROUNDS[2])], [(other, core_swap)])
    own, sent = run_experts(0, own, back)
    chain.add(sent)
    (back,) = chain.gather([(token_held, TOKEN_ROUNDS[3])], [(sent, core_swap)])
    summed = sum_tokens(0, own, back)
    chain.gather([(cot_held, TOKEN_ROUNDS[3])])
    own, other = pick_tokens(1, summed)
    (back,) = chain.gather([(token_held, TOKEN_ROUNDS[4])], [(other, core_swap)])
    own, sent = run_experts(1, own, back)
    chain.add(own)
    chain.gather([(cot_held, TOKEN_ROUNDS[4])])
    own_two, other_two = pick_tokens(2, sent)
    back, back_two = chain.send([sent, other_two], [core_swap] * 2)
    sum_tokens(1, own, back)
    chain.scatter([(terms, RETURN_ROUNDS[0])])
    own, sent = run_experts(2, own_two, after(back_two, *chain.values))
    own_three, other_three = pick_tokens(3, sent)
    back, back_three = chain.send([sent, other_three], [core_swap] * 2)
    sum_tokens(2, own, back)
    chain.scatter([(terms, RETURN_ROUNDS[1])])
    own, sent = run_experts(3, own_three, back_three)
    all_rows, all_act, all_grads, all_gate, all_up = stores
    (back,) = chain.send([sent], [core_swap])
    sum_tokens(3, own, back)
    weight_grads = []
    for moves, pair in zip(
        RETURN_ROUNDS[2:], ((all_act, all_grads), (all_rows, all_gate), (all_rows, all_up))
    ):
        chain.scatter([(terms, moves)])
        weight_grads.append(row_product(*pair, *chain.values))
        chain.add(weight_grads[-1])
    grad_down, grad_gate, grad_up = weight_grads

    summed = plus(*terms[0, 0, 0])
    gate_parts = summed[:, model_width:]
    grad_gates = gate_parts[:, :expert_count] + gate_parts[:, expert_count : 2 * expert_count]
    grad_logits = gate_dense * (
        grad_gates - jnp.sum(gate_dense * grad_gates, axis=1, keepdims=True)
    )
    router_wide = router_rows[:, :expert_count].astype(wide)
    grad_moe_in = summed[:, :model_width] + jnp.einsum(
        "te,de->td", grad_logits, router_wide, precision=HIGH
    )

    grad_hidden_norm, grad_feed_gain = experts_back(grad_moe_in)
    grad_hidden = grad_output + grad_hidden_norm
    grad_own = grad_hidden.astype(low)
    chain.scatter([(y_terms, OUTPUT_ROUNDS[0])])
    chain.add(grad_own)
    far, swapped = chain.scatter(
        [(y_terms, OUTPUT_ROUNDS[1])], [(grad_own, z_pair), (grad_own, core_swap)]
    )

    grad_router = jnp.einsum(
        "td,te->ed", moe_in.astype(wide), after(grad_logits, grad_own), precision=HIGH
    )
    (far_swapped,) = chain.scatter([(y_terms, OUTPUT_ROUNDS[2])], [(far, core_swap)])
    grad_branch = [grad_own, swapped, far, far_swapped]

    def block_products(left_blocks, right, rest, name):
        width = right.shape[1] + (0 if rest is None else 128)
        return call(
            functools.partial(block_product_kernel, rest is not None),
            name,
            [(weight_ids, SMEM), (right, VMEM)]
            + [(b, FAR) for b in left_blocks]
            + ([] if rest is None else [(rest, VMEM)]),
            [shape(tok_rows, width, low)] * 16,
            [pltpu.VMEM((both, model_width), low), copies_sem(4)],
            2 * both * model_width * right.shape[1],
        )

    out_products = block_products(grad_branch, attended, None, "out_weight_grad")
    out_terms = {b: [block] for b, block in zip(BLOCKS, out_products)}
    chain.add(out_products[0])
    (router_part,) = chain.scatter(
        [(y_terms, OUTPUT_ROUNDS[3]), (out_terms, WEIGHT_RETURNS[0])],
        [(grad_router, core_swap)],
        out_products[0],
    )
    grad_router = grad_router + router_part
    (grad_attended,) = call(
        attended_grad_kernel,
        "attended_grad",
        [(weight_ids, SMEM)]
        + [(b, FAR) for b in (after(grad_branch[0], out_products[0]), *grad_branch[1:])]
        + [(b, HBM) for b in out_blocks],
        [shape(both, query_cols, low)],
        [
            pltpu.VMEM((both, model_width), low),
            pltpu.VMEM((query_cols, model_width), low),
            copies_sem(20),
        ],
        2 * both * model_width * query_cols,
    )
    chain.add(grad_attended)
    (router_part,) = chain.scatter(
        [(out_terms, WEIGHT_RETURNS[1]), (y_terms, OUTPUT_ROUNDS[4])], [(grad_router, z_pair)]
    )
    grad_rest = jnp.pad(grad_router + router_part, ((0, 128 - expert_count), (0, 0)))
    grad_raw, query_gain_grad, key_gain_grad = call(
        functools.partial(backward_kernel, head_count),
        "attention_backward",
        [(core_id, SMEM), (raw, VMEM), (after(grad_attended, *chain.values), VMEM)] + turns,
        [shape(both, raw_cols, low), shape(1, head_width, wide), shape(1, head_width, wide)],
        [pltpu.VMEM((length, head_width), wide), pltpu.VMEM((length, head_width), wide)],
        10 * both * length * query_cols,
    )
    chain.add(grad_raw)
    chain.scatter([(out_terms, WEIGHT_RETURNS[2])])
    raw_products = block_products(
        sequence, after(grad_raw, *chain.values), grad_rest, "raw_weight_grad"
    )
    raw_terms = {b: [block] for b, block in zip(BLOCKS, raw_products)}
    chain.add(raw_products[0])
    chain.scatter([(raw_terms, WEIGHT_RETURNS[0]), (y_terms, OUTPUT_ROUNDS[5])])
    sent, kept, attention_part = call(
        normed_grad_kernel,
        "normed_grad",
        [
            (weight_ids, SMEM),
            (after(grad_raw, *chain.values), VMEM),
            (attention_gain[None, :], VMEM),
        ]
        + [(b, FAR) for b in sequence]
        + [(b, HBM) for b in blocks],
        [
            shape(length, model_width, low),
            shape(length, model_width, wide),
            shape(1, model_width, wide),
        ],
        [
            pltpu.VMEM((model_width, raw_cols + 128), low),
            pltpu.VMEM((both, model_width), low),
            copies_sem(20),
        ],
        2 * both * model_width * raw_cols,
    )
    chain.add(kept)
    gains = jnp.concatenate(
        [attention_part[0], grad_feed_gain, query_gain_grad[0], key_gain_grad[0]]
    ).reshape(-1, head_width)
    gains = gains + core_swap(gains)
    (from_core,) = chain.scatter([(out_terms, WEIGHT_RETURNS[3])], [(sent, core_swap)])
    pair_total = kept + from_core.astype(wide)
    from_pair, gain_part = chain.scatter(
        [(raw_terms, WEIGHT_RETURNS[1])],
        [(pair_total[tok_rows:].astype(low), z_pair), (gains, x_swap)],
    )
    gains = gains + gain_part
    (gain_part,) = chain.scatter([(raw_terms, WEIGHT_RETURNS[2])], [(gains, y_swap)])
    grad_normed = pair_total[:tok_rows] + from_pair.astype(wide)
    grad_inputs_norm, _ = attention_back(grad_normed)
    grad_inputs = grad_hidden + grad_inputs_norm
    chain.add(grad_inputs)
    gains = gains + gain_part
    (gain_part,) = chain.scatter([(raw_terms, WEIGHT_RETURNS[3])], [(gains, z_pair)])
    gains = gains + gain_part
    theirs = jnp.concatenate([plus(*t[1, 0, 0]).astype(low) for t in (out_terms, raw_terms)], axis=1)
    theirs, gain_part = chain.scatter(
        [(raw_terms, WEIGHT_RETURNS[4]), (out_terms, WEIGHT_RETURNS[4])],
        [(theirs, z_pair), (gains, z_far)],
    )
    out_theirs, raw_theirs = theirs[:, :query_cols], theirs[:, query_cols:]
    gains = (gains + gain_part).reshape(-1)
    output = (hidden + plus(*y_terms[0, 0, 0])).astype(low)
    grad_out_weight = in_order(plus(*out_terms[0, 0, 0]), out_theirs.astype(wide), 1).T
    mine, theirs = plus(*raw_terms[0, 0, 0]), raw_theirs.astype(wide)
    spans = ((0, query_cols), (query_cols, query_cols + key_cols), (query_cols + key_cols, raw_cols))
    grad_query_weight, grad_key_weight, grad_value_weight = [
        in_order(mine[:, a:b], theirs[:, a:b], 1) for a, b in spans
    ]
    router_share = mine[:, raw_cols : raw_cols + expert_count]
    return (
        output,
        grad_inputs,
        gains[:model_width],
        grad_query_weight,
        grad_key_weight,
        grad_value_weight,
        gains[2 * model_width : 2 * model_width + head_width],
        gains[2 * model_width + head_width :],
        grad_out_weight,
        gains[model_width : 2 * model_width],
        router_share,
        grad_gate,
        grad_up,
        grad_down,
    )


def solution(mesh):
    in_specs = (
        P(("dp", "tensor"), None),
        P(),
        P("dp", "tensor"),
        P("dp", "tensor"),
        P("dp", "tensor"),
        P(),
        P(),
        P("tensor", "dp"),
        P(),
        P("dp", None),
        P(("dp", "tensor"), None, None),
        P(("dp", "tensor"), None, None),
        P(("dp", "tensor"), None, None),
        P(("dp", "tensor"), None),
        P(("dp", "tensor"), None),
    )
    out_specs = (
        P(("dp", "tensor"), None),
        P(("dp", "tensor"), None),
        P(),
        P("dp", "tensor"),
        P("dp", "tensor"),
        P("dp", "tensor"),
        P(),
        P(),
        P("tensor", "dp"),
        P(),
        P("dp", None),
        P(("dp", "tensor"), None, None),
        P(("dp", "tensor"), None, None),
        P(("dp", "tensor"), None, None),
    )
    fits = mesh.shape["dp"] == 16 and mesh.shape["tensor"] == 2
    local = local_sixteen if fits else local_any
    return jax.shard_map(local, mesh=mesh, in_specs=in_specs, out_specs=out_specs, check_vma=False)
```

```python
import functools
import math

import jax
import jax.numpy as jnp
from jax import lax
from jax.experimental import pallas as pl
from jax.experimental.pallas import tpu as pltpu
from jax.sharding import PartitionSpec as P

EPS = 1e-06
THETA = 1000000.0
HIGH = lax.Precision.HIGHEST
block_limit = 512


def rms_scale(values, scales):
    inverse = lax.rsqrt(jnp.mean(values * values, axis=-1, keepdims=True) + EPS)
    return values * inverse * scales


def rope_tables(length, columns):
    halfway = columns // 2
    frequency = THETA ** (-(jnp.arange(halfway, dtype=jnp.float32) * 2.0 / columns))
    angles = jnp.arange(length, dtype=jnp.float32)[:, None] * frequency[None, :]
    return (jnp.cos(angles), jnp.sin(angles))


def head_prep(raw_rows, scales, cosine_table, sine_table):
    length = raw_rows.shape[0]
    columns = scales.shape[0]
    shaped = rms_scale(raw_rows.reshape(length, -1, columns), scales)
    halfway = columns // 2
    leading = shaped[..., :halfway]
    second = shaped[..., halfway:]
    cos_part = cosine_table[:, None, :]
    sin_part = sine_table[:, None, :]
    turned = jnp.concatenate(
        [leading * cos_part - second * sin_part, second * cos_part + leading * sin_part], axis=-1
    )
    return turned.reshape(length, -1)


def masked_scores(offset, block_rows, queries, key_rows, score_scale):
    scores = (
        jnp.einsum("qkgd,ckd->kgqc", queries, key_rows, preferred_element_type=jnp.float32)
        * score_scale
    )
    row_places = offset + jnp.arange(block_rows, dtype=jnp.int32)
    key_places = jnp.arange(key_rows.shape[0], dtype=jnp.int32)
    allowed = key_places[None, :] <= row_places[:, None]
    return (queries, jnp.where(allowed, scores, -1e30))


def slot_layout(routes, expert_count, capacity):
    flat_routes = routes.reshape(-1)
    onehot = (flat_routes[:, None] == jnp.arange(expert_count, dtype=jnp.int32)[None, :]).astype(
        jnp.int32
    )
    position = jnp.sum((jnp.cumsum(onehot, axis=0) - onehot) * onehot, axis=1)
    return flat_routes * capacity + position


def route_rows(buffer):
    return lax.all_to_all(buffer, ("dp", "tensor"), split_axis=0, concat_axis=0, tiled=True)


def local_any(
    inputs,
    attention_gain,
    query_weight,
    key_weight,
    value_weight,
    query_gain,
    key_gain,
    out_weight,
    feedforward_gain,
    router_weight,
    gate_weight,
    up_weight,
    down_weight,
    routes,
    cotangent,
):
    tok_rows, model_width = inputs.shape
    head_width = query_gain.shape[0]
    top_count = routes.shape[1]
    expert_count = router_weight.shape[1]
    local_experts = gate_weight.shape[0]
    capacity = tok_rows * top_count * 11 // (expert_count * 8)
    full_query, full_key, full_value, full_out, full_router = (
        lax.all_gather(query_weight, "dp", axis=0, tiled=True),
        lax.all_gather(key_weight, "dp", axis=0, tiled=True),
        lax.all_gather(value_weight, "dp", axis=0, tiled=True),
        lax.all_gather(out_weight, "dp", axis=1, tiled=True),
        lax.all_gather(router_weight, "dp", axis=0, tiled=True),
    )
    inputs_float = inputs.astype(jnp.float32)
    normed_attention, attention_back = jax.vjp(rms_scale, inputs_float, attention_gain)
    sequence = lax.all_gather(normed_attention.astype(jnp.bfloat16), "tensor", axis=0, tiled=True)
    length = sequence.shape[0]
    query_raw = jnp.dot(sequence, full_query, preferred_element_type=jnp.float32)
    key_raw = jnp.dot(sequence, full_key, preferred_element_type=jnp.float32)
    value_raw = jnp.dot(sequence, full_value, preferred_element_type=jnp.float32)
    cosine_table, sine_table = rope_tables(length, head_width)

    def prepare(raw_rows, scales):
        return head_prep(raw_rows, scales, cosine_table, sine_table)

    query_ready, query_back = jax.vjp(prepare, query_raw, query_gain)
    key_ready, key_back = jax.vjp(prepare, key_raw, key_gain)
    kv_heads = key_raw.shape[1] // head_width
    group_size = query_raw.shape[1] // head_width // kv_heads
    queries = query_ready.astype(jnp.bfloat16).reshape(length, kv_heads, group_size, head_width)
    key_rows = key_ready.astype(jnp.bfloat16).reshape(length, kv_heads, head_width)
    value_rows = value_raw.astype(jnp.bfloat16).reshape(length, kv_heads, head_width)
    score_scale = head_width ** (-0.5)
    block_rows = min(block_limit, length)
    block_count = length // block_rows
    offsets = jnp.arange(block_count, dtype=jnp.int32) * block_rows

    def forward_block(offset):
        query_block, masked = masked_scores(offset, block_rows, queries, key_rows, score_scale)
        peak_value = jnp.max(masked, axis=-1, keepdims=True)
        exp_total = jnp.sum(jnp.exp(masked - peak_value), axis=-1, keepdims=True)
        log_total = peak_value + jnp.log(exp_total)
        soft_weights = jnp.exp(masked - log_total).astype(jnp.bfloat16)
        mixture = jnp.einsum(
            "kgqc,ckd->qkgd", soft_weights, value_rows, preferred_element_type=jnp.float32
        )
        return (mixture, log_total)

    mixed_blocks, log_totals = lax.map(forward_block, offsets)
    attended = mixed_blocks.reshape(length, -1).astype(jnp.bfloat16)
    branch = lax.psum_scatter(
        jnp.dot(attended, full_out, preferred_element_type=jnp.float32).astype(jnp.bfloat16),
        "tensor",
        scatter_dimension=0,
        tiled=True,
    ).astype(jnp.float32)
    hidden = inputs_float + branch
    normed_experts, experts_back = jax.vjp(rms_scale, hidden, feedforward_gain)
    moe_in = normed_experts.astype(jnp.bfloat16)
    logits = jnp.dot(moe_in, full_router, preferred_element_type=jnp.float32)
    onehot_routes = (
        routes[:, :, None] == jnp.arange(expert_count, dtype=jnp.int32)[None, None, :]
    ).astype(jnp.float32)
    chosen = jnp.einsum("tke,te->tk", onehot_routes, logits, precision=HIGH)
    gate_values = jax.nn.softmax(chosen, axis=-1)
    slots = slot_layout(routes, expert_count, capacity)
    buffer_shape = (expert_count // local_experts, local_experts, capacity, model_width)
    dispatch = (
        jnp.zeros((expert_count * capacity, model_width), jnp.bfloat16)
        .at[slots]
        .set(jnp.repeat(moe_in, top_count, axis=0))
    )
    received = route_rows(dispatch.reshape(buffer_shape))
    gate_pre = jnp.einsum(
        "secd,edf->secf", received, gate_weight, preferred_element_type=jnp.float32
    )
    up_pre = jnp.einsum("secd,edf->secf", received, up_weight, preferred_element_type=jnp.float32)
    sigmoid_gate = jax.nn.sigmoid(gate_pre)
    silu_gate = gate_pre * sigmoid_gate
    activated = (silu_gate * up_pre).astype(jnp.bfloat16)
    expert_out = jnp.einsum(
        "secf,efd->secd", activated, down_weight, preferred_element_type=jnp.float32
    ).astype(jnp.bfloat16)
    returned = route_rows(expert_out).reshape(expert_count * capacity, model_width)
    picked = returned[slots].reshape(tok_rows, top_count, model_width).astype(jnp.float32)
    mixture_out = jnp.sum(gate_values[:, :, None] * picked, axis=1)
    output = (hidden + mixture_out).astype(jnp.bfloat16)
    grad_output = cotangent.astype(jnp.float32)
    grad_gates = jnp.sum(picked * grad_output[:, None, :], axis=2)
    grad_picks = (
        (gate_values[:, :, None] * grad_output[:, None, :])
        .astype(jnp.bfloat16)
        .reshape(-1, model_width)
    )
    grad_dispatch = (
        jnp.zeros((expert_count * capacity, model_width), jnp.bfloat16).at[slots].set(grad_picks)
    )
    grad_received = route_rows(grad_dispatch.reshape(buffer_shape))
    grad_act = jnp.einsum(
        "secd,efd->secf", grad_received, down_weight, preferred_element_type=jnp.float32
    )
    grad_down = jnp.einsum(
        "secf,secd->efd", activated, grad_received, preferred_element_type=jnp.float32
    )
    grad_gate_pre = (
        grad_act * up_pre * sigmoid_gate * (1.0 + gate_pre * (1.0 - sigmoid_gate))
    ).astype(jnp.bfloat16)
    grad_up_pre = (grad_act * silu_gate).astype(jnp.bfloat16)
    grad_gate = jnp.einsum(
        "secd,secf->edf", received, grad_gate_pre, preferred_element_type=jnp.float32
    )
    grad_up = jnp.einsum(
        "secd,secf->edf", received, grad_up_pre, preferred_element_type=jnp.float32
    )
    grad_sent = jnp.einsum(
        "secf,edf->secd", grad_gate_pre, gate_weight, preferred_element_type=jnp.float32
    )
    grad_sent = (
        grad_sent
        + jnp.einsum("secf,edf->secd", grad_up_pre, up_weight, preferred_element_type=jnp.float32)
    ).astype(jnp.bfloat16)
    grad_back = route_rows(grad_sent).reshape(expert_count * capacity, model_width)
    grad_moe_in = jnp.sum(
        grad_back[slots].reshape(tok_rows, top_count, model_width).astype(jnp.float32), axis=1
    )
    grad_chosen = gate_values * (
        grad_gates - jnp.sum(gate_values * grad_gates, axis=1, keepdims=True)
    )
    grad_logits = jnp.einsum("tk,tke->te", grad_chosen, onehot_routes, precision=HIGH)
    router_float = full_router.astype(jnp.float32)
    grad_moe_in = grad_moe_in + jnp.einsum("te,de->td", grad_logits, router_float, precision=HIGH)
    grad_router = jnp.einsum("td,te->de", moe_in.astype(jnp.float32), grad_logits, precision=HIGH)
    grad_hidden_norm, grad_experts_gain = experts_back(grad_moe_in)
    grad_hidden = grad_output + grad_hidden_norm
    grad_branch = lax.all_gather(grad_hidden.astype(jnp.bfloat16), "tensor", axis=0, tiled=True)
    grad_attended = jnp.einsum(
        "td,ad->ta", grad_branch, full_out, preferred_element_type=jnp.float32
    ).astype(jnp.bfloat16)
    grad_blocks = grad_attended.reshape(block_count, block_rows, kv_heads, group_size, head_width)

    def backward_block(carry, item):
        key_sum, value_sum = carry
        offset, log_total, grad_block = item
        query_block, masked = masked_scores(offset, block_rows, queries, key_rows, score_scale)
        soft_weights = jnp.exp(masked - log_total)
        soft_low = soft_weights.astype(jnp.bfloat16)
        grad_soft = jnp.einsum(
            "qkgd,ckd->kgqc", grad_block, value_rows, preferred_element_type=jnp.float32
        )
        inner_sum = jnp.sum(soft_weights * grad_soft, axis=-1, keepdims=True)
        grad_scores = (soft_weights * (grad_soft - inner_sum)).astype(jnp.bfloat16)
        grad_query_block = (
            jnp.einsum("kgqc,ckd->qkgd", grad_scores, key_rows, preferred_element_type=jnp.float32)
            * score_scale
        )
        key_sum = (
            key_sum
            + jnp.einsum(
                "kgqc,qkgd->ckd", grad_scores, query_block, preferred_element_type=jnp.float32
            )
            * score_scale
        )
        value_sum = value_sum + jnp.einsum(
            "kgqc,qkgd->ckd", soft_low, grad_block, preferred_element_type=jnp.float32
        )
        return ((key_sum, value_sum), grad_query_block)

    zero_rows = jnp.zeros((length, kv_heads, head_width), jnp.float32)
    (key_sum, value_sum), grad_query_blocks = lax.scan(
        backward_block, (zero_rows, zero_rows), (offsets, log_totals, grad_blocks)
    )
    grad_query_raw, grad_query_gain = query_back(grad_query_blocks.reshape(length, -1))
    grad_key_raw, grad_key_gain = key_back(key_sum.reshape(length, -1))
    grad_query_low = grad_query_raw.astype(jnp.bfloat16)
    grad_key_low = grad_key_raw.astype(jnp.bfloat16)
    grad_value_low = value_sum.reshape(length, -1).astype(jnp.bfloat16)
    total = jnp.einsum("tc,dc->td", grad_query_low, full_query, preferred_element_type=jnp.float32)
    total = total + jnp.einsum(
        "tc,dc->td", grad_key_low, full_key, preferred_element_type=jnp.float32
    )
    grad_sequence = lax.psum_scatter(
        (
            total
            + jnp.einsum(
                "tc,dc->td", grad_value_low, full_value, preferred_element_type=jnp.float32
            )
        ).astype(jnp.bfloat16),
        "tensor",
        scatter_dimension=0,
        tiled=True,
    ).astype(jnp.float32)
    grad_inputs_norm, grad_attention_gain = attention_back(grad_sequence)
    grad_inputs = grad_hidden + grad_inputs_norm
    query_cols = grad_query_low.shape[1]
    key_cols = grad_key_low.shape[1]
    grad_raw_all = jnp.concatenate([grad_query_low, grad_key_low, grad_value_low], axis=1)
    inward = jnp.einsum("td,tc->dc", sequence, grad_raw_all, preferred_element_type=jnp.float32)
    outward = jnp.einsum("td,ta->da", grad_branch, attended, preferred_element_type=jnp.float32)
    owned = lax.psum_scatter(
        jnp.concatenate([inward, outward], axis=1), "dp", scatter_dimension=0, tiled=True
    )
    grad_query_weight = owned[:, :query_cols]
    grad_key_weight = owned[:, query_cols : query_cols + key_cols]
    grad_value_weight = owned[:, query_cols + key_cols : query_cols + 2 * key_cols]
    grad_out_weight = owned[:, query_cols + 2 * key_cols :].T
    router_total, attention_total, query_total, key_total, experts_total = lax.psum(
        (grad_router, grad_attention_gain, grad_query_gain, grad_key_gain, grad_experts_gain),
        ("dp", "tensor"),
    )
    router_rows = router_weight.shape[0]
    router_share = lax.dynamic_slice_in_dim(
        router_total, lax.axis_index("dp") * router_rows, router_rows, 0
    )
    return (
        output,
        grad_inputs,
        attention_total,
        grad_query_weight,
        grad_key_weight,
        grad_value_weight,
        query_total,
        key_total,
        grad_out_weight,
        experts_total,
        router_share,
        grad_gate,
        grad_up,
        grad_down,
    )


low, wide = jnp.bfloat16, jnp.float32
Z_RING = tuple((i, (i + 4) % 16) for i in range(16))
Z_PAIR = tuple((i, i ^ 4) for i in range(16))
Z_FAR = tuple((i, i ^ 8) for i in range(16))
Y_PAIR = tuple((i, i ^ 2) for i in range(16))
X_PAIR = tuple((i, i ^ 1) for i in range(16))
BLOCKS = tuple((k, dy, dx) for k in range(4) for dy in range(2) for dx in range(2))
PLANE = tuple((dy, dx) for dy in range(2) for dx in range(2))
OVER_X = (1, 2)
ROOM = 8 * 2**20
WHOLE = 60 * 2**20
TILE = 256
WIDE = 512
HIDDEN_TILE = 768
NT = (((1,), (1,)), ((), ()))
TN = (((0,), (0,)), ((), ()))


def z_next(block):
    return lax.ppermute(block, "dp", Z_RING)


def z_pair(block):
    return lax.ppermute(block, "dp", Z_PAIR)


def z_far(block):
    return lax.ppermute(block, "dp", Z_FAR)


def y_swap(block):
    return lax.ppermute(block, "dp", Y_PAIR)


def x_swap(block):
    return lax.ppermute(block, "dp", X_PAIR)


def core_swap(block):
    return lax.ppermute(block, "tensor", ((0, 1), (1, 0)))


def after(value, *earlier):
    return lax.optimization_barrier((value, *earlier))[0]


def plus(own, *others):
    total = own.astype(wide)
    for other in others:
        total = total + other.astype(wide)
    return total


TOKEN_ROUNDS = (
    (((0, 0, 0), (0, 0, 1), x_swap), ((0, 0, 0), (0, 1, 0), y_swap), ((0, 0, 0), (1, 0, 0), z_next)),
    (((1, 0, 0), (1, 0, 1), x_swap), ((0, 0, 1), (0, 1, 1), y_swap), ((1, 0, 0), (2, 0, 0), z_next)),
    (((2, 0, 0), (2, 0, 1), x_swap), ((1, 0, 0), (1, 1, 0), y_swap), ((2, 0, 0), (3, 0, 0), z_next)),
    (((3, 0, 0), (3, 0, 1), x_swap), ((2, 0, 0), (2, 1, 0), y_swap), ((0, 1, 1), (1, 1, 1), z_next)),
    (((2, 1, 0), (2, 1, 1), x_swap), ((3, 0, 1), (3, 1, 1), y_swap), ((2, 1, 0), (3, 1, 0), z_next)),
)
WEIGHT_ROUNDS = (
    (
        ((0, 0, 0), (0, 0, 1), x_swap),
        ((0, 0, 0), (0, 1, 0), y_swap),
        ((0, 0, 0), (2, 0, 0), z_far, True),
    ),
    (
        ((1, 0, 0), (1, 0, 1), x_swap),
        ((1, 0, 0), (1, 1, 0), y_swap),
        ((1, 0, 0), (3, 0, 0), z_far, True),
        ((0, 0, 1), (0, 1, 1), y_swap),
    ),
    (
        ((2, 0, 0), (2, 0, 1), x_swap),
        ((2, 0, 0), (2, 1, 0), y_swap),
        ((1, 1, 0), (1, 1, 1), x_swap),
    ),
    (
        ((3, 0, 0), (3, 1, 0), y_swap),
        ((3, 0, 0), (3, 0, 1), x_swap),
        ((2, 0, 1), (2, 1, 1), y_swap),
    ),
    (((3, 1, 0), (3, 1, 1), x_swap),),
)
SHORT_ROUNDS = (
    (*WEIGHT_ROUNDS[0][:2],),
    (((0, 0, 0), (2, 0, 0), z_far, True), *WEIGHT_ROUNDS[1][:2], WEIGHT_ROUNDS[1][3]),
    (((1, 0, 0), (3, 0, 0), z_far), *WEIGHT_ROUNDS[2]),
    (*WEIGHT_ROUNDS[3], ((1, 1, 1), (3, 1, 1), z_far)),
)
WEIGHT_RETURNS = (
    (((3, 1, 1), (3, 1, 0), x_swap),),
    (
        ((3, 1, 0), (3, 0, 0), y_swap),
        ((3, 0, 1), (3, 0, 0), x_swap),
        ((2, 1, 1), (2, 0, 1), y_swap),
    ),
    (
        ((3, 0, 0), (1, 0, 0), z_far),
        ((2, 0, 1), (2, 0, 0), x_swap),
        ((2, 1, 0), (2, 0, 0), y_swap),
        ((1, 1, 1), (1, 1, 0), x_swap),
    ),
    (
        ((2, 0, 0), (0, 0, 0), z_far),
        ((1, 1, 0), (1, 0, 0), y_swap),
        ((1, 0, 1), (1, 0, 0), x_swap),
        ((0, 1, 1), (0, 0, 1), y_swap),
    ),
    (((0, 0, 1), (0, 0, 0), x_swap), ((0, 1, 0), (0, 0, 0), y_swap)),
)


RETURN_ROUNDS = (
    (((1, 1, 1), (1, 0, 1), y_swap), ((0, 1, 1), (0, 1, 0), x_swap), ((1, 1, 0), (2, 1, 0), z_next)),
    (((1, 0, 1), (1, 0, 0), x_swap), ((2, 1, 1), (2, 0, 1), y_swap), ((2, 1, 0), (3, 1, 0), z_next)),
    (((2, 0, 1), (2, 0, 0), x_swap), ((3, 1, 1), (3, 0, 1), y_swap), ((1, 0, 0), (2, 0, 0), z_next)),
    (((3, 0, 1), (3, 0, 0), x_swap), ((3, 1, 0), (3, 0, 0), y_swap), ((2, 0, 0), (3, 0, 0), z_next)),
    (((0, 0, 1), (0, 0, 0), x_swap), ((0, 1, 0), (0, 0, 0), y_swap), ((3, 0, 0), (0, 0, 0), z_next)),
)
OUTPUT_ROUNDS = (
    (((3, 1, 1), (3, 1, 0), x_swap), ((1, 1, 1), (1, 0, 1), y_swap), ((1, 1, 0), (2, 1, 0), z_next)),
    (((1, 0, 1), (1, 0, 0), x_swap), ((2, 1, 1), (2, 0, 1), y_swap)),
    (((2, 0, 1), (2, 0, 0), x_swap), ((2, 1, 0), (2, 0, 0), y_swap), ((1, 0, 0), (2, 0, 0), z_next)),
    (((3, 0, 1), (3, 0, 0), x_swap), ((3, 1, 0), (3, 0, 0), y_swap), ((2, 0, 0), (3, 0, 0), z_next)),
    (((0, 1, 1), (0, 1, 0), x_swap),),
    (((0, 0, 1), (0, 0, 0), x_swap), ((0, 1, 0), (0, 0, 0), y_swap), ((3, 0, 0), (0, 0, 0), z_next)),
)


class Chain:
    def __init__(self):
        self.earlier = []
        self.late = []
        self.values = []

    def add(self, *values):
        self.earlier.extend(values)

    def send(self, values, ways, late=()):
        values = lax.optimization_barrier((*values, *self.earlier))[: len(values)]
        self.values = values
        results = [way(value) for value, way in zip(values, ways)]
        self.earlier = self.late + [r for i, r in enumerate(results) if i not in late]
        self.late = [results[i] for i in late]
        return results

    def round(self, values, moves, others):
        late = [i for i, move in enumerate(moves) if len(move) > 3]
        values = values + [value for value, _ in others]
        ways = [move[2] for move in moves] + [way for _, way in others]
        results = self.send(values, ways, late)
        return results[: len(moves)], results[len(moves) :]

    def gather(self, pairs, others=()):
        values = [held[move[0]] for held, moves in pairs for move in moves]
        moves = [move for _, moves in pairs for move in moves]
        results, rest = self.round(values, moves, others)
        for (held, end), result in zip([(h, m[1]) for h, ms in pairs for m in ms], results):
            held[end] = result
        return rest

    def scatter(self, pairs, others=(), later=None):
        if later is not None:
            for terms, moves in pairs:
                for move in moves:
                    terms[move[0]][-1] = after(terms[move[0]][-1], later)
        values = totals([terms[move[0]] for terms, moves in pairs for move in moves])
        moves = [move for _, moves in pairs for move in moves]
        results, rest = self.round(values, moves, others)
        for (terms, end), result in zip([(t, m[1]) for t, ms in pairs for m in ms], results):
            terms[end].append(result)
        return rest


def sum_kernel(counts, *refs):
    outs = refs[sum(counts) :]
    for count, out in zip(counts, outs):
        terms, refs = refs[:count], refs[count:]
        out[...] = plus(*[term[...] for term in terms]).astype(out.dtype)


def totals(lists):
    several = [terms for terms in lists if len(terms) > 1]
    if not several:
        return [terms[0] for terms in lists]
    operands = [term for terms in several for term in terms]
    rows = operands[0].shape[0] // 4
    whole = [(a.shape[0] // 4, a.shape[1]) for a in operands]
    specs = [pl.BlockSpec(block, lambda i: (i, 0)) for block in whole]
    firsts = [terms[0] for terms in several]
    sums = pl.pallas_call(
        functools.partial(sum_kernel, [len(terms) for terms in several]),
        grid=(4,),
        out_shape=[jax.ShapeDtypeStruct(a.shape, low) for a in firsts],
        in_specs=specs,
        out_specs=[pl.BlockSpec((rows, a.shape[1]), lambda i: (i, 0)) for a in firsts],
        name="sums",
        compiler_params=pltpu.CompilerParams(vmem_limit_bytes=2 * ROOM),
    )(*operands)
    sums = list(sums)
    return [sums.pop(0) if len(terms) > 1 else terms[0] for terms in lists]


def dot(left, right, dims=None):
    if dims is None:
        return jnp.dot(left, right, preferred_element_type=wide)
    return lax.dot_general(left, right, dims, preferred_element_type=wide)


def lanes(start, size):
    return pl.ds(pl.multiple_of(start, 128), size)


def spot(ids, i):
    return pl.multiple_of(ids[i] * 128, 128)


def row_copies(ids, blocks, whole, sems):
    return [
        pltpu.make_async_copy(block, whole.at[pl.ds(spot(ids, i), 128), :], sems.at[i])
        for i, block in enumerate(blocks)
    ]


def column_copies(ids, blocks, whole, sems):
    return [
        pltpu.make_async_copy(block, whole.at[:, pl.ds(spot(ids, i), 128)], sems.at[i])
        for i, block in enumerate(blocks)
    ]


def stack_copies(blocks, whole, sems):
    rows = blocks[0].shape[0]
    return [
        pltpu.make_async_copy(block, whole.at[pl.ds(i * rows, rows), :], sems.at[i])
        for i, block in enumerate(blocks)
    ]


def start_all(copies):
    for copy in copies:
        copy.start()


def wait_all(copies):
    for copy in copies:
        copy.wait()


def head_forward(raw, gain, cosine, sine):
    inverse = lax.rsqrt(jnp.mean(raw * raw, axis=-1, keepdims=True) + EPS)
    unit = raw * inverse
    shaped = unit * gain
    return unit, inverse, shaped * cosine + pltpu.roll(shaped, 64, 1) * sine


def head_backward(grad, unit, inverse, gain, cosine, sine):
    back = grad * cosine - pltpu.roll(grad, 64, 1) * sine
    gain_grad = jnp.sum(back * unit, axis=0, keepdims=True)
    scaled = back * gain
    return gain_grad, inverse * (scaled - unit * jnp.mean(scaled * unit, axis=-1, keepdims=True))


def causal(core, length):
    half = length // 2
    rows = lax.broadcasted_iota(jnp.int32, (length, length), 0)
    columns = lax.broadcasted_iota(jnp.int32, (length, length), 1)

    def place(i):
        return jnp.where(i < half, i + core * half, i - half + (1 - core) * half)

    return place(columns) <= place(rows)


def soft(query, key, allowed, scale):
    scores = jnp.where(allowed, dot(query, key, NT) * scale, -1e30)
    raised = jnp.exp(scores - jnp.max(scores, axis=-1, keepdims=True))
    return raised / jnp.sum(raised, axis=-1, keepdims=True)


def raw_kernel(ids, block_ids, *refs):
    seq_blocks, blocks = refs[:4], refs[4:20]
    raw, router, rest, whole, seq, sems = refs[20:]
    copies = stack_copies(seq_blocks, seq, sems.at[pl.ds(16, 4)]) + row_copies(
        ids, blocks, whole, sems
    )
    start_all(copies)
    wait_all(copies)
    width = raw.shape[1]

    @pl.loop(0, width // TILE)
    def _(j):
        span = lanes(j * TILE, TILE)
        raw[:, span] = dot(seq[...], whole[:, span])

    router[...] = whole[:, width:]
    for p in range(16):
        rest[p * 128 : (p + 1) * 128, :] = whole[pl.ds(spot(block_ids, p), 128), width:]


def forward_kernel(head_count, core, raw, cosine, sine, query_gain, key_gain, attended):
    length = raw.shape[0] // 2
    key_start = head_count * 128
    allowed = causal(core[0], length)
    scale = 128 ** (-0.5)
    for s in range(2):
        span = slice(s * length, (s + 1) * length)
        turn = (cosine[...], sine[...])
        key_raw = raw[span, key_start : key_start + 128]
        key = head_forward(key_raw, key_gain[...], *turn)[2].astype(low)
        value = raw[span, key_start + 128 : key_start + 256].astype(low)

        @pl.loop(0, head_count, unroll=2)
        def _(h):
            columns = lanes(h * 128, 128)
            query = head_forward(raw[span, columns], query_gain[...], *turn)[2].astype(low)
            weights = soft(query, key, allowed, scale)
            attended[span, columns] = dot(weights.astype(low), value).astype(low)


def split_rows(product, span, sent, kept):
    rows = product.shape[0] // 4
    kept[:rows, span] = product[:rows]
    sent[:rows, span] = product[rows : 2 * rows].astype(low)
    kept[rows:, span] = product[2 * rows : 3 * rows]
    sent[rows:, span] = product[3 * rows :].astype(low)


def out_kernel(ids, attended, *refs):
    blocks, (sent, kept, whole, sems) = refs[:16], refs[16:]
    copies = column_copies(ids, blocks, whole, sems)
    start_all(copies)
    wait_all(copies)

    @pl.loop(0, whole.shape[1] // WIDE)
    def _(j):
        span = lanes(j * WIDE, WIDE)
        split_rows(dot(attended[...], whole[:, span]), span, sent, kept)


def normed_grad_kernel(ids, grad_raw, gain, *refs):
    seq_blocks, blocks = refs[:4], refs[4:20]
    sent, kept, gain_grad, whole, seq, sems = refs[20:]
    copies = row_copies(ids, blocks, whole, sems) + stack_copies(
        seq_blocks, seq, sems.at[pl.ds(16, 4)]
    )
    start_all(copies)
    wait_all(copies)
    width = grad_raw.shape[1]

    @pl.loop(0, whole.shape[0] // WIDE)
    def _(j):
        span = lanes(j * WIDE, WIDE)
        product = dot(grad_raw[...], whole[span, :width], NT)
        split_rows(product, span, sent, kept)
        unit = seq[:, span].astype(wide) / gain[:, span]
        gain_grad[:, span] = jnp.sum(product * unit, axis=0, keepdims=True)


def attended_grad_kernel(ids, *refs):
    grad_blocks, blocks = refs[:4], refs[4:20]
    grad_attended, grad_branch, whole, sems = refs[20:]
    copies = stack_copies(grad_blocks, grad_branch, sems.at[pl.ds(16, 4)]) + column_copies(
        ids, blocks, whole, sems
    )
    start_all(copies)
    wait_all(copies)

    @pl.loop(0, grad_attended.shape[1] // WIDE)
    def _(j):
        span = lanes(j * WIDE, WIDE)
        grad_attended[:, span] = dot(grad_branch[...], whole[span, :], NT).astype(low)


def map_kernel(capacity, expert_count, experts, named, picks, turned_picks):
    slot_rows = 4 * capacity
    early = lax.broadcasted_iota(jnp.int32, (128, 128), 0)
    late = lax.broadcasted_iota(jnp.int32, (128, 128), 1)
    before = jnp.where(early < late, 1.0, 0.0).astype(low)
    behind = jnp.where(late < early, 1.0, 0.0).astype(low)
    slot_numbers = lax.broadcasted_iota(jnp.int32, (slot_rows, 128), 0)
    slot_lanes = lax.broadcasted_iota(jnp.int32, (128, turned_picks.shape[1]), 1)
    for b in range(16):
        k, i = b // 4, b % 4
        block = named[b * 128 : (b + 1) * 128, :]
        turned_slots = []
        for c in range(2):
            column = experts[c] + expert_count
            own_lane = lax.broadcasted_iota(jnp.int32, (8, 128), 1) == column
            hit = dot(jnp.where(own_lane, 1.0, 0.0).astype(low), block, NT)
            slot = dot(hit.astype(low), before) + float(i * capacity)
            slot = jnp.where(hit > 0.5, slot, -1.0).astype(jnp.int32)
            first = (2 * k + c) * slot_rows
            picks[first : first + slot_rows, i * 128 : (i + 1) * 128] = jnp.where(
                slot_numbers == slot[:1], 1.0, 0.0
            ).astype(low)
            mine = jnp.where(late == column, block.astype(wide), 0.0)
            hit = jnp.sum(mine, axis=1, keepdims=True)
            slot = jnp.sum(dot(behind, mine.astype(low)), axis=1, keepdims=True)
            slot = slot + float(i * capacity + c * slot_rows)
            turned_slots.append(jnp.where(hit > 0.5, slot, -1.0).astype(jnp.int32))
        either = jnp.logical_or(slot_lanes == turned_slots[0], slot_lanes == turned_slots[1])
        turned_picks[b * 128 : (b + 1) * 128, :] = jnp.where(either, 1.0, 0.0).astype(low)


def pick_kernel(k, picks_in, named, *refs):
    tokens, cots, (own, other, picks, rows, sems) = refs[:4], refs[4:8], refs[8:]
    quad_rows, full = rows.shape
    width = tokens[0].shape[1]
    copies = (
        stack_copies(tokens, rows.at[:, pl.ds(0, width)], sems.at[pl.ds(0, 4)])
        + stack_copies(cots, rows.at[:, pl.ds(width + 128, width)], sems.at[pl.ds(4, 4)])
        + [
            pltpu.make_async_copy(
                picks_in.at[pl.ds(k * picks.shape[0], picks.shape[0]), :], picks, sems.at[8]
            ),
            pltpu.make_async_copy(
                named.at[pl.ds(k * quad_rows, quad_rows), :],
                rows.at[:, pl.ds(width, 128)],
                sems.at[9],
            ),
        ]
    )
    start_all(copies)
    wait_all(copies)
    slot_rows = own.shape[0]
    for start in range(0, full, WIDE):
        span = slice(start, min(start + WIDE, full))
        made = dot(picks[...], rows[:, span]).astype(low)
        own[:, span] = made[:slot_rows]
        other[:, span] = made[slot_rows:]


def expert_kernel(expert_count, k, experts, router, *refs):
    sides, weights = refs[:2], refs[2:5]
    refs = refs[5 + (5 if k else 0) :]
    (all_rows, all_act, all_grads, all_gate, all_up, own_out, back_out) = refs[:7]
    (rows, v_gate, v_up, v_down, act, grads, gate_back, up_back) = refs[7:15]
    (gate_pre, up_pre, sig, sems) = refs[15:]
    slot_rows = own_out.shape[0]
    width, hidden = v_gate.shape
    after_width = width + 128
    spans = [slice(c * slot_rows, (c + 1) * slot_rows) for c in range(2)]
    side_copies = stack_copies(sides, rows, sems.at[pl.ds(0, 2)])
    weight_copies = [
        pltpu.make_async_copy(a, b, sems.at[2 + i])
        for i, (a, b) in enumerate(zip(weights, (v_gate, v_up, v_down)))
    ]
    start_all(side_copies + weight_copies)
    kept = []

    def keep(source, target, sem):
        copy = pltpu.make_async_copy(
            source.at[:, pl.ds(0, target.shape[1])],
            target.at[pl.ds(k * 2 * slot_rows, 2 * slot_rows), :],
            sems.at[sem],
        )
        copy.start()
        kept.append(copy)

    wait_all(side_copies)
    keep(rows, all_rows, 5)
    logits = dot(rows[:, :width], router[...])
    numbers = lax.broadcasted_iota(jnp.int32, logits.shape, 1)
    is_named = pltpu.roll(rows[:, width:after_width].astype(wide), 128 - expert_count, 1)
    is_named = jnp.logical_and(is_named > 0.5, numbers < expert_count)
    lifted = jnp.where(is_named, logits, -1e30)
    lifted = jnp.where(
        is_named, jnp.exp(lifted - jnp.max(lifted, axis=1, keepdims=True)), 0.0
    )
    mine = jnp.sum(jnp.where(numbers == experts[0], lifted, 0.0), axis=1, keepdims=True)
    gates = mine / jnp.maximum(jnp.sum(lifted, axis=1, keepdims=True), 1e-30)
    wait_all(weight_copies[:2])
    pre = dot(rows[:, :width], v_gate[...])
    up = dot(rows[:, :width], v_up[...])
    s = jax.nn.sigmoid(pre)
    gate_pre[...] = pre
    up_pre[...] = up
    sig[...] = s
    act[...] = (pre * s * up).astype(low)
    keep(act, all_act, 6)
    wait_all(weight_copies[2:])
    slot_grads = jnp.zeros((2 * slot_rows, 1), wide)
    for j in range(width // WIDE):
        span = slice(j * WIDE, (j + 1) * WIDE)
        later = slice(after_width + j * WIDE, after_width + (j + 1) * WIDE)
        out = dot(act[...], v_down[:, span]).astype(low).astype(wide)
        cot = rows[:, later].astype(wide)
        grads[:, span] = (gates * cot).astype(low)
        scaled = (gates * out).astype(low)
        own_out[:, later] = scaled[spans[0]]
        back_out[:, later] = scaled[spans[1]]
        slot_grads = slot_grads + jnp.sum(cot * out, axis=1, keepdims=True)
    keep(grads, all_grads, 7)
    back = dot(grads[...], v_down[...], NT)
    pre, s = gate_pre[...], sig[...]
    gate_back[...] = (back * up_pre[...] * s * (1.0 + pre * (1.0 - s))).astype(low)
    up_back[...] = (back * (pre * s)).astype(low)
    keep(gate_back, all_gate, 8)
    keep(up_back, all_up, 9)
    for j in range(width // WIDE):
        span = slice(j * WIDE, (j + 1) * WIDE)
        back = dot(gate_back[...], v_gate[span, :], NT) + dot(up_back[...], v_up[span, :], NT)
        back = back.astype(low)
        own_out[:, span] = back[spans[0]]
        back_out[:, span] = back[spans[1]]
    high = slot_grads.astype(low).astype(wide)
    rest = jnp.where(numbers == experts[0] + expert_count, slot_grads - high, 0.0)
    parts = jnp.where(numbers == experts[0], high, rest).astype(low)
    own_out[:, width:after_width] = parts[spans[0]]
    back_out[:, width:after_width] = parts[spans[1]]
    wait_all(kept)


def token_sum_kernel(k, turned_picks, *refs):
    sides, blocks, outputs, (picks, rows, out_rows, sems) = refs[:2], refs[2:6], refs[6:10], refs[10:]
    quad_rows, width = out_rows.shape
    copies = stack_copies(sides, rows, sems.at[pl.ds(0, 2)]) + [
        pltpu.make_async_copy(
            turned_picks.at[pl.ds(k * quad_rows, quad_rows), :], picks, sems.at[2]
        )
    ]
    start_all(copies)
    wait_all(copies)
    slots = rows.shape[0]
    size, first = blocks[0].shape
    for j in range(0, width, WIDE):
        span = slice(j, j + WIDE)
        out_rows[:, span] = dot(picks[:, :slots], rows[:, first + j : first + j + WIDE]).astype(low)
    copies = [
        pltpu.make_async_copy(out_rows.at[pl.ds(i * size, size), :], output, sems.at[3 + i])
        for i, output in enumerate(outputs)
    ]
    start_all(copies)
    for j in range(0, first, WIDE):
        span = slice(j, min(j + WIDE, first))
        made = dot(picks[:, :slots], rows[:, span]).astype(low)
        for i, block in enumerate(blocks):
            block[:, span] = made[i * size : (i + 1) * size]
    wait_all(copies)


def backward_kernel(head_count, core, raw, grad_attended, *refs):
    cosine, sine, query_gain, key_gain = refs[:4]
    grad_raw, query_gain_grad, key_gain_grad, key_sum, value_sum = refs[4:]
    length = raw.shape[0] // 2
    key_start = head_count * 128
    allowed = causal(core[0], length)
    scale = 128 ** (-0.5)
    turn = (cosine[...], sine[...])
    query_gain_grad[...] = jnp.zeros_like(query_gain_grad)
    key_gain_grad[...] = jnp.zeros_like(key_gain_grad)
    for s in range(2):
        span = slice(s * length, (s + 1) * length)
        key_raw = raw[span, key_start : key_start + 128]
        key_unit, key_inverse, key = head_forward(key_raw, key_gain[...], *turn)
        key = key.astype(low)
        value = raw[span, key_start + 128 : key_start + 256].astype(low)
        key_sum[...] = jnp.zeros_like(key_sum)
        value_sum[...] = jnp.zeros_like(value_sum)

        @pl.loop(0, head_count, unroll=2)
        def _(h):
            columns = lanes(h * 128, 128)
            unit, inverse, query = head_forward(raw[span, columns], query_gain[...], *turn)
            query = query.astype(low)
            weights = soft(query, key, allowed, scale)
            grad = grad_attended[span, columns]
            grad_soft = dot(grad, value, NT)
            inner = jnp.sum(weights * grad_soft, axis=-1, keepdims=True)
            grad_scores = (weights * (grad_soft - inner)).astype(low)
            value_sum[...] += dot(weights.astype(low), grad, TN)
            key_sum[...] += dot(grad_scores, query, TN) * scale
            grad_query = dot(grad_scores, key) * scale
            gain_grad, back = head_backward(grad_query, unit, inverse, query_gain[...], *turn)
            query_gain_grad[...] += gain_grad
            grad_raw[span, columns] = back.astype(low)

        gain_grad, back = head_backward(
            key_sum[...], key_unit, key_inverse, key_gain[...], *turn
        )
        key_gain_grad[...] += gain_grad
        grad_raw[span, key_start : key_start + 128] = back.astype(low)
        grad_raw[span, key_start + 128 : key_start + 256] = value_sum[...].astype(low)


def block_product_kernel(with_rest, ids, right, *refs):
    left_blocks, refs = refs[:4], refs[4:]
    rest, refs = (refs[0], refs[1:]) if with_rest else (None, refs)
    outs, (left, sems) = refs[:16], refs[16:]
    copies = stack_copies(left_blocks, left, sems)
    start_all(copies)
    wait_all(copies)
    width = right.shape[1]
    for i, out in enumerate(outs):
        part = left[:, pl.ds(spot(ids, i), 128)]
        out[:, :width] = dot(part, right[...], TN).astype(low)
        if with_rest:
            out[:, width:] = jnp.transpose(rest[:, pl.ds(spot(ids, i), 128)]).astype(low)


SMEM = pl.BlockSpec(memory_space=pltpu.SMEM)
VMEM = pl.BlockSpec(memory_space=pltpu.VMEM)
FAR = pl.BlockSpec(memory_space=pl.ANY)
HBM = pl.BlockSpec(memory_space=pltpu.HBM)


def call(kernel, name, ins, outs, scratch, flops, specs=None, aliases=None, alone=False):
    operands = [value for value, _ in ins]
    moved = sum(a.size * a.dtype.itemsize for a in operands + outs)
    placed = [value for value, spec in ins if spec is VMEM] + scratch
    placed += [out for out, spec in zip(outs, specs or [VMEM] * len(outs)) if spec is VMEM]
    held = sum(
        math.prod(a.shape) * jnp.dtype(a.dtype).itemsize
        for a in placed
        if jnp.issubdtype(a.dtype, jnp.floating)
    )
    return pl.pallas_call(
        kernel,
        out_shape=outs,
        in_specs=[spec for _, spec in ins],
        out_specs=specs or [VMEM] * len(outs),
        scratch_shapes=scratch,
        name=name,
        input_output_aliases=aliases or {},
        compiler_params=pltpu.CompilerParams(vmem_limit_bytes=WHOLE if alone else ROOM + held),
        cost_estimate=pl.CostEstimate(flops=flops, bytes_accessed=moved, transcendentals=0),
    )(*operands)


def shape(rows, columns, dtype):
    return jax.ShapeDtypeStruct((rows, columns), dtype)


def copies_sem(count):
    return pltpu.SemaphoreType.DMA((count,))


def local_sixteen(
    inputs,
    attention_gain,
    query_weight,
    key_weight,
    value_weight,
    query_gain,
    key_gain,
    out_weight,
    feedforward_gain,
    router_weight,
    gate_weight,
    up_weight,
    down_weight,
    routes,
    cotangent,
):
    tok_rows, model_width = inputs.shape
    head_width = query_gain.shape[0]
    top_count = routes.shape[1]
    expert_count = router_weight.shape[1]
    hidden_width = gate_weight.shape[2]
    capacity = tok_rows * top_count * 11 // (expert_count * 8)
    query_cols, key_cols = query_weight.shape[1] // 2, key_weight.shape[1] // 2
    raw_cols = query_cols + 2 * key_cols
    head_count = query_cols // head_width
    place = lax.axis_index("dp")
    core = lax.axis_index("tensor")
    z, y, x = place // 4, (place // 2) % 2, place % 2
    even = z % 2 == 0
    core_id = core.astype(jnp.int32)[None]
    block_ids = jnp.stack(
        [((z - k) % 4) * 4 + (y ^ dy) * 2 + (x ^ dx) for k, dy, dx in BLOCKS]
    ).astype(jnp.int32)
    weight_ids = jnp.stack(
        [(z ^ w) * 4 + (y ^ dy) * 2 + (x ^ dx) for w, dy, dx in BLOCKS]
    ).astype(jnp.int32)

    def halves(values, axis):
        first, second = jnp.split(values, 2, axis=axis)
        return jnp.where(even, first, second), jnp.where(even, second, first)

    def in_order(mine, theirs, axis):
        return jnp.where(
            even,
            jnp.concatenate([mine, theirs], axis=axis),
            jnp.concatenate([theirs, mine], axis=axis),
        )

    chain = Chain()
    numbers = jnp.arange(expert_count, dtype=jnp.int32)
    own_named = jnp.any(routes[:, :, None] == numbers, axis=1)
    splits = [halves(w, 1) for w in (query_weight, key_weight, value_weight)]
    rest = [
        router_weight,
        own_named.astype(low),
        jnp.zeros((tok_rows, 128 - 2 * expert_count), low),
    ]
    mine = jnp.concatenate([s[0] for s in splits] + rest, axis=1)
    theirs = jnp.concatenate([s[1] for s in splits] + rest, axis=1)
    held = {(0, 0, 0): mine}
    (held[1, 0, 0],) = chain.gather([(held, WEIGHT_ROUNDS[0])], [(theirs, z_pair)])
    inputs_float = inputs.astype(wide)
    normed_attention, attention_back = jax.vjp(rms_scale, inputs_float, attention_gain)
    normed = normed_attention.astype(low)
    chain.add(normed)
    chain.gather([(held, WEIGHT_ROUNDS[1])])
    chain.gather([(held, WEIGHT_ROUNDS[2])])
    far, swapped = chain.gather(
        [(held, WEIGHT_ROUNDS[3])], [(normed, z_pair), (normed, core_swap)]
    )
    out_mine, out_theirs = halves(out_weight, 0)
    out_held = {(0, 0, 0): out_mine}
    cot_held = {(0, 0, 0): cotangent}
    far_swapped, out_held[1, 0, 0] = chain.gather(
        [(held, WEIGHT_ROUNDS[4]), (out_held, SHORT_ROUNDS[0])],
        [(far, core_swap), (out_theirs, z_pair)],
    )
    sequence = [normed, swapped, far, far_swapped]
    blocks = [held[b] for b in BLOCKS]
    chain.gather([(out_held, SHORT_ROUNDS[1])])
    grad_output = cotangent.astype(wide)
    length = 2 * tok_rows
    own_places = jnp.arange(tok_rows, dtype=jnp.int32)
    places = jnp.concatenate([own_places + core * tok_rows, own_places + (1 - core) * tok_rows])
    halfway = head_width // 2
    frequency = THETA ** (-(jnp.arange(halfway, dtype=wide) * 2.0 / head_width))
    angles = places.astype(wide)[:, None] * frequency[None, :]
    cosine, sine = jnp.cos(angles), jnp.sin(angles)
    turns = [
        (jnp.concatenate([cosine, cosine], axis=1), VMEM),
        (jnp.concatenate([-sine, sine], axis=1), VMEM),
        (query_gain[None, :], VMEM),
        (key_gain[None, :], VMEM),
    ]
    both = 2 * length
    raw, router_rows, rest_rows = call(
        raw_kernel,
        "attention_raw",
        [(weight_ids, SMEM), (block_ids, SMEM)]
        + [(b, FAR) for b in sequence]
        + [(b, HBM) for b in blocks],
        [
            shape(both, raw_cols, wide),
            shape(model_width, 128, low),
            shape(model_width, 128, low),
        ],
        [
            pltpu.VMEM((model_width, raw_cols + 128), low),
            pltpu.VMEM((both, model_width), low),
            copies_sem(20),
        ],
        2 * both * model_width * raw_cols,
        alone=True,
    )
    chain.add(raw)
    chain.gather([(out_held, SHORT_ROUNDS[2])])
    (attended,) = call(
        functools.partial(forward_kernel, head_count),
        "attention_forward",
        [(core_id, SMEM), (raw, VMEM)] + turns,
        [shape(both, query_cols, low)],
        [],
        4 * both * length * query_cols,
    )
    chain.add(attended)
    chain.gather([(out_held, SHORT_ROUNDS[3])])
    out_blocks = [out_held[b] for b in BLOCKS]
    chain.gather([(cot_held, TOKEN_ROUNDS[0])])
    sent, kept = call(
        out_kernel,
        "attention_out",
        [(weight_ids, SMEM), (attended, VMEM)] + [(b, HBM) for b in out_blocks],
        [shape(length, model_width, low), shape(length, model_width, wide)],
        [pltpu.VMEM((query_cols, model_width), low), copies_sem(16)],
        2 * both * model_width * query_cols,
    )

    pair_total = kept + core_swap(sent).astype(wide)
    leaving = pair_total[tok_rows:].astype(low)
    from_pair = z_pair(leaving)
    chain.add(leaving)
    chain.gather([(cot_held, TOKEN_ROUNDS[1])])
    chain.gather([(cot_held, TOKEN_ROUNDS[2])])
    hidden = inputs_float + pair_total[:tok_rows] + from_pair.astype(wide)
    normed_experts, experts_back = jax.vjp(rms_scale, hidden, feedforward_gain)
    moe_in = normed_experts.astype(low)
    chain.add(moe_in)

    token_held = {(0, 0, 0): moe_in}
    chain.gather([(token_held, TOKEN_ROUNDS[0])])
    chain.gather([(token_held, TOKEN_ROUNDS[1])])
    slot_rows = 4 * capacity
    quad_rows = 4 * tok_rows
    rows_of = 2 * slot_rows
    all_slots = 4 * rows_of
    experts = jnp.stack([place * 2 + core, place * 2 + 1 - core]).astype(jnp.int32)
    w_gate, w_up, w_down = gate_weight[0], up_weight[0], down_weight[0]
    turned_width = -(-rows_of // 128) * 128
    picks, turned_picks = call(
        functools.partial(map_kernel, capacity, expert_count),
        "pick_maps",
        [(experts, SMEM), (rest_rows, VMEM)],
        [shape(all_slots, quad_rows, low), shape(model_width, turned_width, low)],
        [],
        2 * 128 * 128 * model_width,
    )

    logits = jnp.dot(moe_in, router_rows, preferred_element_type=wide)[:, :expert_count]
    lifted = jnp.where(own_named, logits, -1e30)
    lifted = jnp.where(own_named, jnp.exp(lifted - jnp.max(lifted, axis=1, keepdims=True)), 0.0)
    gate_dense = lifted / jnp.sum(lifted, axis=1, keepdims=True)

    full = 2 * model_width + 128

    def pick_tokens(k, *earlier):
        return call(
            functools.partial(pick_kernel, k),
            "picks",
            [(after(picks, *earlier), FAR), (rest_rows, FAR)]
            + [(token_held[k, dy, dx], FAR) for dy, dx in PLANE]
            + [(cot_held[k, dy, dx], HBM) for dy, dx in PLANE],
            [shape(slot_rows, full, low)] * 2,
            [
                pltpu.VMEM((rows_of, quad_rows), low),
                pltpu.VMEM((quad_rows, full), low),
                copies_sem(10),
            ],
            2 * rows_of * quad_rows * full,
            alone=k == 0,
        )

    stores = []

    def run_experts(k, own, back):
        ins = (
            [(experts, SMEM), (router_rows, VMEM), (own, FAR), (back, FAR)]
            + [(w, HBM) for w in (w_gate, w_up, w_down)]
        )
        made = call(
            functools.partial(expert_kernel, expert_count, k),
            "experts",
            ins + [(store, HBM) for store in stores],
            [
                shape(all_slots, model_width, low),
                shape(all_slots, hidden_width, low),
                shape(all_slots, model_width, low),
                shape(all_slots, hidden_width, low),
                shape(all_slots, hidden_width, low),
                shape(slot_rows, full, low),
                shape(slot_rows, full, low),
            ],
            [
                pltpu.VMEM((rows_of, full), low),
                pltpu.VMEM((model_width, hidden_width), low),
                pltpu.VMEM((model_width, hidden_width), low),
                pltpu.VMEM((hidden_width, model_width), low),
                pltpu.VMEM((rows_of, hidden_width), low),
                pltpu.VMEM((rows_of, model_width), low),
                pltpu.VMEM((rows_of, hidden_width), low),
                pltpu.VMEM((rows_of, hidden_width), low),
                pltpu.VMEM((rows_of, hidden_width), wide),
                pltpu.VMEM((rows_of, hidden_width), wide),
                pltpu.VMEM((rows_of, hidden_width), wide),
                copies_sem(10),
            ],
            12 * rows_of * model_width * hidden_width,
            [HBM] * 5 + [VMEM] * 2,
            {len(ins) + i: i for i in range(len(stores))},
        )
        stores[:] = made[:5]
        return made[5:]

    terms, y_terms = {b: [] for b in BLOCKS}, {}

    def sum_tokens(k, own, back):
        made = call(
            functools.partial(token_sum_kernel, k),
            "token_sums",
            [(turned_picks, FAR), (own, FAR), (back, FAR)],
            [shape(tok_rows, model_width + 128, low)] * 4 + [shape(tok_rows, model_width, low)] * 4,
            [
                pltpu.VMEM((quad_rows, turned_width), low),
                pltpu.VMEM((rows_of, full), low),
                pltpu.VMEM((quad_rows, model_width), low),
                copies_sem(7),
            ],
            2 * rows_of * quad_rows * full,
            [VMEM] * 4 + [HBM] * 4,
        )
        for i, p in enumerate(PLANE):
            terms[(k, *p)].append(made[i])
            y_terms[(k, *p)] = [made[4 + i]]
        return made[0]

    def row_product(left, right, *earlier):
        return lax.dot_general(after(left, *earlier), right, TN, preferred_element_type=wide)[None]

    own, other = pick_tokens(0)
    chain.add(other)
    (back,) = chain.gather([(token_held, TOKEN_ROUNDS[2])], [(other, core_swap)])
    own, sent = run_experts(0, own, back)
    chain.add(sent)
    (back,) = chain.gather([(token_held, TOKEN_ROUNDS[3])], [(sent, core_swap)])
    summed = sum_tokens(0, own, back)
    chain.gather([(cot_held, TOKEN_ROUNDS[3])])
    own, other = pick_tokens(1, summed)
    (back,) = chain.gather([(token_held, TOKEN_ROUNDS[4])], [(other, core_swap)])
    own, sent = run_experts(1, own, back)
    chain.add(own)
    chain.gather([(cot_held, TOKEN_ROUNDS[4])])
    own_two, other_two = pick_tokens(2, sent)
    back, back_two = chain.send([sent, other_two], [core_swap] * 2)
    sum_tokens(1, own, back)
    chain.scatter([(terms, RETURN_ROUNDS[0])])
    own, sent = run_experts(2, own_two, after(back_two, *chain.values))
    own_three, other_three = pick_tokens(3, sent)
    back, back_three = chain.send([sent, other_three], [core_swap] * 2)
    sum_tokens(2, own, back)
    chain.scatter([(terms, RETURN_ROUNDS[1])])
    own, sent = run_experts(3, own_three, back_three)
    all_rows, all_act, all_grads, all_gate, all_up = stores
    (back,) = chain.send([sent], [core_swap])
    sum_tokens(3, own, back)
    weight_grads = []
    for moves, pair in zip(
        RETURN_ROUNDS[2:], ((all_act, all_grads), (all_rows, all_gate), (all_rows, all_up))
    ):
        chain.scatter([(terms, moves)])
        weight_grads.append(row_product(*pair, *chain.values))
        chain.add(weight_grads[-1])
    grad_down, grad_gate, grad_up = weight_grads

    summed = plus(*terms[0, 0, 0])
    gate_parts = summed[:, model_width:]
    grad_gates = gate_parts[:, :expert_count] + gate_parts[:, expert_count : 2 * expert_count]
    grad_logits = gate_dense * (
        grad_gates - jnp.sum(gate_dense * grad_gates, axis=1, keepdims=True)
    )
    router_wide = router_rows[:, :expert_count].astype(wide)
    grad_moe_in = summed[:, :model_width] + jnp.einsum(
        "te,de->td", grad_logits, router_wide, precision=HIGH
    )

    grad_hidden_norm, grad_feed_gain = experts_back(grad_moe_in)
    grad_hidden = grad_output + grad_hidden_norm
    grad_own = grad_hidden.astype(low)
    chain.scatter([(y_terms, OUTPUT_ROUNDS[0])])
    chain.add(grad_own)
    far, swapped = chain.scatter(
        [(y_terms, OUTPUT_ROUNDS[1])], [(grad_own, z_pair), (grad_own, core_swap)]
    )

    grad_router = jnp.einsum(
        "td,te->ed", moe_in.astype(wide), after(grad_logits, grad_own), precision=HIGH
    )
    (far_swapped,) = chain.scatter([(y_terms, OUTPUT_ROUNDS[2])], [(far, core_swap)])
    grad_branch = [grad_own, swapped, far, far_swapped]

    def block_products(left_blocks, right, rest, name):
        width = right.shape[1] + (0 if rest is None else 128)
        return call(
            functools.partial(block_product_kernel, rest is not None),
            name,
            [(weight_ids, SMEM), (right, VMEM)]
            + [(b, FAR) for b in left_blocks]
            + ([] if rest is None else [(rest, VMEM)]),
            [shape(tok_rows, width, low)] * 16,
            [pltpu.VMEM((both, model_width), low), copies_sem(4)],
            2 * both * model_width * right.shape[1],
        )

    out_products = block_products(grad_branch, attended, None, "out_weight_grad")
    out_terms = {b: [block] for b, block in zip(BLOCKS, out_products)}
    chain.add(out_products[0])
    (router_part,) = chain.scatter(
        [(y_terms, OUTPUT_ROUNDS[3]), (out_terms, WEIGHT_RETURNS[0])],
        [(grad_router, core_swap)],
        out_products[0],
    )
    grad_router = grad_router + router_part
    (grad_attended,) = call(
        attended_grad_kernel,
        "attended_grad",
        [(weight_ids, SMEM)]
        + [(b, FAR) for b in (after(grad_branch[0], out_products[0]), *grad_branch[1:])]
        + [(b, HBM) for b in out_blocks],
        [shape(both, query_cols, low)],
        [
            pltpu.VMEM((both, model_width), low),
            pltpu.VMEM((query_cols, model_width), low),
            copies_sem(20),
        ],
        2 * both * model_width * query_cols,
    )
    chain.add(grad_attended)
    (router_part,) = chain.scatter(
        [(out_terms, WEIGHT_RETURNS[1]), (y_terms, OUTPUT_ROUNDS[4])], [(grad_router, z_pair)]
    )
    grad_rest = jnp.pad(grad_router + router_part, ((0, 128 - expert_count), (0, 0)))
    grad_raw, query_gain_grad, key_gain_grad = call(
        functools.partial(backward_kernel, head_count),
        "attention_backward",
        [(core_id, SMEM), (raw, VMEM), (after(grad_attended, *chain.values), VMEM)] + turns,
        [shape(both, raw_cols, low), shape(1, head_width, wide), shape(1, head_width, wide)],
        [pltpu.VMEM((length, head_width), wide), pltpu.VMEM((length, head_width), wide)],
        10 * both * length * query_cols,
    )
    chain.add(grad_raw)
    chain.scatter([(out_terms, WEIGHT_RETURNS[2])])
    raw_products = block_products(
        sequence, after(grad_raw, *chain.values), grad_rest, "raw_weight_grad"
    )
    raw_terms = {b: [block] for b, block in zip(BLOCKS, raw_products)}
    chain.add(raw_products[0])
    chain.scatter([(raw_terms, WEIGHT_RETURNS[0]), (y_terms, OUTPUT_ROUNDS[5])])
    sent, kept, attention_part = call(
        normed_grad_kernel,
        "normed_grad",
        [
            (weight_ids, SMEM),
            (after(grad_raw, *chain.values), VMEM),
            (attention_gain[None, :], VMEM),
        ]
        + [(b, FAR) for b in sequence]
        + [(b, HBM) for b in blocks],
        [
            shape(length, model_width, low),
            shape(length, model_width, wide),
            shape(1, model_width, wide),
        ],
        [
            pltpu.VMEM((model_width, raw_cols + 128), low),
            pltpu.VMEM((both, model_width), low),
            copies_sem(20),
        ],
        2 * both * model_width * raw_cols,
    )
    chain.add(kept)
    gains = jnp.concatenate(
        [attention_part[0], grad_feed_gain, query_gain_grad[0], key_gain_grad[0]]
    ).reshape(-1, head_width)
    gains = gains + core_swap(gains)
    (from_core,) = chain.scatter([(out_terms, WEIGHT_RETURNS[3])], [(sent, core_swap)])
    pair_total = kept + from_core.astype(wide)
    from_pair, gain_part = chain.scatter(
        [(raw_terms, WEIGHT_RETURNS[1])],
        [(pair_total[tok_rows:].astype(low), z_pair), (gains, x_swap)],
    )
    gains = gains + gain_part
    (gain_part,) = chain.scatter([(raw_terms, WEIGHT_RETURNS[2])], [(gains, y_swap)])
    grad_normed = pair_total[:tok_rows] + from_pair.astype(wide)
    grad_inputs_norm, _ = attention_back(grad_normed)
    grad_inputs = grad_hidden + grad_inputs_norm
    chain.add(grad_inputs)
    gains = gains + gain_part
    (gain_part,) = chain.scatter([(raw_terms, WEIGHT_RETURNS[3])], [(gains, z_pair)])
    gains = gains + gain_part
    theirs = jnp.concatenate([plus(*t[1, 0, 0]).astype(low) for t in (out_terms, raw_terms)], axis=1)
    theirs, gain_part = chain.scatter(
        [(raw_terms, WEIGHT_RETURNS[4]), (out_terms, WEIGHT_RETURNS[4])],
        [(theirs, z_pair), (gains, z_far)],
    )
    out_theirs, raw_theirs = theirs[:, :query_cols], theirs[:, query_cols:]
    gains = (gains + gain_part).reshape(-1)
    output = (hidden + plus(*y_terms[0, 0, 0])).astype(low)
    grad_out_weight = in_order(plus(*out_terms[0, 0, 0]), out_theirs.astype(wide), 1).T
    mine, theirs = plus(*raw_terms[0, 0, 0]), raw_theirs.astype(wide)
    spans = ((0, query_cols), (query_cols, query_cols + key_cols), (query_cols + key_cols, raw_cols))
    grad_query_weight, grad_key_weight, grad_value_weight = [
        in_order(mine[:, a:b], theirs[:, a:b], 1) for a, b in spans
    ]
    router_share = mine[:, raw_cols : raw_cols + expert_count]
    return (
        output,
        grad_inputs,
        gains[:model_width],
        grad_query_weight,
        grad_key_weight,
        grad_value_weight,
        gains[2 * model_width : 2 * model_width + head_width],
        gains[2 * model_width + head_width :],
        grad_out_weight,
        gains[model_width : 2 * model_width],
        router_share,
        grad_gate,
        grad_up,
        grad_down,
    )


def solution(mesh):
    in_specs = (
        P(("dp", "tensor"), None),
        P(),
        P("dp", "tensor"),
        P("dp", "tensor"),
        P("dp", "tensor"),
        P(),
        P(),
        P("tensor", "dp"),
        P(),
        P("dp", None),
        P(("dp", "tensor"), None, None),
        P(("dp", "tensor"), None, None),
        P(("dp", "tensor"), None, None),
        P(("dp", "tensor"), None),
        P(("dp", "tensor"), None),
    )
    out_specs = (
        P(("dp", "tensor"), None),
        P(("dp", "tensor"), None),
        P(),
        P("dp", "tensor"),
        P("dp", "tensor"),
        P("dp", "tensor"),
        P(),
        P(),
        P("tensor", "dp"),
        P(),
        P("dp", None),
        P(("dp", "tensor"), None, None),
        P(("dp", "tensor"), None, None),
        P(("dp", "tensor"), None, None),
    )
    fits = mesh.shape["dp"] == 16 and mesh.shape["tensor"] == 2
    local = local_sixteen if fits else local_any
    return jax.shard_map(local, mesh=mesh, in_specs=in_specs, out_specs=out_specs, check_vma=False)
```

```python
import functools
import math

import jax
import jax.numpy as jnp
from jax import lax
from jax.experimental import pallas as pl
from jax.experimental.pallas import tpu as pltpu
from jax.sharding import PartitionSpec as P

EPS = 1e-06
THETA = 1000000.0
HIGH = lax.Precision.HIGHEST
block_limit = 512


def rms_scale(values, scales):
    inverse = lax.rsqrt(jnp.mean(values * values, axis=-1, keepdims=True) + EPS)
    return values * inverse * scales


def rope_tables(length, columns):
    halfway = columns // 2
    frequency = THETA ** (-(jnp.arange(halfway, dtype=jnp.float32) * 2.0 / columns))
    angles = jnp.arange(length, dtype=jnp.float32)[:, None] * frequency[None, :]
    return (jnp.cos(angles), jnp.sin(angles))


def head_prep(raw_rows, scales, cosine_table, sine_table):
    length = raw_rows.shape[0]
    columns = scales.shape[0]
    shaped = rms_scale(raw_rows.reshape(length, -1, columns), scales)
    halfway = columns // 2
    leading = shaped[..., :halfway]
    second = shaped[..., halfway:]
    cos_part = cosine_table[:, None, :]
    sin_part = sine_table[:, None, :]
    turned = jnp.concatenate(
        [leading * cos_part - second * sin_part, second * cos_part + leading * sin_part], axis=-1
    )
    return turned.reshape(length, -1)


def masked_scores(offset, block_rows, queries, key_rows, score_scale):
    scores = (
        jnp.einsum("qkgd,ckd->kgqc", queries, key_rows, preferred_element_type=jnp.float32)
        * score_scale
    )
    row_places = offset + jnp.arange(block_rows, dtype=jnp.int32)
    key_places = jnp.arange(key_rows.shape[0], dtype=jnp.int32)
    allowed = key_places[None, :] <= row_places[:, None]
    return (queries, jnp.where(allowed, scores, -1e30))


def slot_layout(routes, expert_count, capacity):
    flat_routes = routes.reshape(-1)
    onehot = (flat_routes[:, None] == jnp.arange(expert_count, dtype=jnp.int32)[None, :]).astype(
        jnp.int32
    )
    position = jnp.sum((jnp.cumsum(onehot, axis=0) - onehot) * onehot, axis=1)
    return flat_routes * capacity + position


def route_rows(buffer):
    return lax.all_to_all(buffer, ("dp", "tensor"), split_axis=0, concat_axis=0, tiled=True)


def local_any(
    inputs,
    attention_gain,
    query_weight,
    key_weight,
    value_weight,
    query_gain,
    key_gain,
    out_weight,
    feedforward_gain,
    router_weight,
    gate_weight,
    up_weight,
    down_weight,
    routes,
    cotangent,
):
    tok_rows, model_width = inputs.shape
    head_width = query_gain.shape[0]
    top_count = routes.shape[1]
    expert_count = router_weight.shape[1]
    local_experts = gate_weight.shape[0]
    capacity = tok_rows * top_count * 11 // (expert_count * 8)
    full_query, full_key, full_value, full_out, full_router = (
        lax.all_gather(query_weight, "dp", axis=0, tiled=True),
        lax.all_gather(key_weight, "dp", axis=0, tiled=True),
        lax.all_gather(value_weight, "dp", axis=0, tiled=True),
        lax.all_gather(out_weight, "dp", axis=1, tiled=True),
        lax.all_gather(router_weight, "dp", axis=0, tiled=True),
    )
    inputs_float = inputs.astype(jnp.float32)
    normed_attention, attention_back = jax.vjp(rms_scale, inputs_float, attention_gain)
    sequence = lax.all_gather(normed_attention.astype(jnp.bfloat16), "tensor", axis=0, tiled=True)
    length = sequence.shape[0]
    query_raw = jnp.dot(sequence, full_query, preferred_element_type=jnp.float32)
    key_raw = jnp.dot(sequence, full_key, preferred_element_type=jnp.float32)
    value_raw = jnp.dot(sequence, full_value, preferred_element_type=jnp.float32)
    cosine_table, sine_table = rope_tables(length, head_width)

    def prepare(raw_rows, scales):
        return head_prep(raw_rows, scales, cosine_table, sine_table)

    query_ready, query_back = jax.vjp(prepare, query_raw, query_gain)
    key_ready, key_back = jax.vjp(prepare, key_raw, key_gain)
    kv_heads = key_raw.shape[1] // head_width
    group_size = query_raw.shape[1] // head_width // kv_heads
    queries = query_ready.astype(jnp.bfloat16).reshape(length, kv_heads, group_size, head_width)
    key_rows = key_ready.astype(jnp.bfloat16).reshape(length, kv_heads, head_width)
    value_rows = value_raw.astype(jnp.bfloat16).reshape(length, kv_heads, head_width)
    score_scale = head_width ** (-0.5)
    block_rows = min(block_limit, length)
    block_count = length // block_rows
    offsets = jnp.arange(block_count, dtype=jnp.int32) * block_rows

    def forward_block(offset):
        query_block, masked = masked_scores(offset, block_rows, queries, key_rows, score_scale)
        peak_value = jnp.max(masked, axis=-1, keepdims=True)
        exp_total = jnp.sum(jnp.exp(masked - peak_value), axis=-1, keepdims=True)
        log_total = peak_value + jnp.log(exp_total)
        soft_weights = jnp.exp(masked - log_total).astype(jnp.bfloat16)
        mixture = jnp.einsum(
            "kgqc,ckd->qkgd", soft_weights, value_rows, preferred_element_type=jnp.float32
        )
        return (mixture, log_total)

    mixed_blocks, log_totals = lax.map(forward_block, offsets)
    attended = mixed_blocks.reshape(length, -1).astype(jnp.bfloat16)
    branch = lax.psum_scatter(
        jnp.dot(attended, full_out, preferred_element_type=jnp.float32).astype(jnp.bfloat16),
        "tensor",
        scatter_dimension=0,
        tiled=True,
    ).astype(jnp.float32)
    hidden = inputs_float + branch
    normed_experts, experts_back = jax.vjp(rms_scale, hidden, feedforward_gain)
    moe_in = normed_experts.astype(jnp.bfloat16)
    logits = jnp.dot(moe_in, full_router, preferred_element_type=jnp.float32)
    onehot_routes = (
        routes[:, :, None] == jnp.arange(expert_count, dtype=jnp.int32)[None, None, :]
    ).astype(jnp.float32)
    chosen = jnp.einsum("tke,te->tk", onehot_routes, logits, precision=HIGH)
    gate_values = jax.nn.softmax(chosen, axis=-1)
    slots = slot_layout(routes, expert_count, capacity)
    buffer_shape = (expert_count // local_experts, local_experts, capacity, model_width)
    dispatch = (
        jnp.zeros((expert_count * capacity, model_width), jnp.bfloat16)
        .at[slots]
        .set(jnp.repeat(moe_in, top_count, axis=0))
    )
    received = route_rows(dispatch.reshape(buffer_shape))
    gate_pre = jnp.einsum(
        "secd,edf->secf", received, gate_weight, preferred_element_type=jnp.float32
    )
    up_pre = jnp.einsum("secd,edf->secf", received, up_weight, preferred_element_type=jnp.float32)
    sigmoid_gate = jax.nn.sigmoid(gate_pre)
    silu_gate = gate_pre * sigmoid_gate
    activated = (silu_gate * up_pre).astype(jnp.bfloat16)
    expert_out = jnp.einsum(
        "secf,efd->secd", activated, down_weight, preferred_element_type=jnp.float32
    ).astype(jnp.bfloat16)
    returned = route_rows(expert_out).reshape(expert_count * capacity, model_width)
    picked = returned[slots].reshape(tok_rows, top_count, model_width).astype(jnp.float32)
    mixture_out = jnp.sum(gate_values[:, :, None] * picked, axis=1)
    output = (hidden + mixture_out).astype(jnp.bfloat16)
    grad_output = cotangent.astype(jnp.float32)
    grad_gates = jnp.sum(picked * grad_output[:, None, :], axis=2)
    grad_picks = (
        (gate_values[:, :, None] * grad_output[:, None, :])
        .astype(jnp.bfloat16)
        .reshape(-1, model_width)
    )
    grad_dispatch = (
        jnp.zeros((expert_count * capacity, model_width), jnp.bfloat16).at[slots].set(grad_picks)
    )
    grad_received = route_rows(grad_dispatch.reshape(buffer_shape))
    grad_act = jnp.einsum(
        "secd,efd->secf", grad_received, down_weight, preferred_element_type=jnp.float32
    )
    grad_down = jnp.einsum(
        "secf,secd->efd", activated, grad_received, preferred_element_type=jnp.float32
    )
    grad_gate_pre = (
        grad_act * up_pre * sigmoid_gate * (1.0 + gate_pre * (1.0 - sigmoid_gate))
    ).astype(jnp.bfloat16)
    grad_up_pre = (grad_act * silu_gate).astype(jnp.bfloat16)
    grad_gate = jnp.einsum(
        "secd,secf->edf", received, grad_gate_pre, preferred_element_type=jnp.float32
    )
    grad_up = jnp.einsum(
        "secd,secf->edf", received, grad_up_pre, preferred_element_type=jnp.float32
    )
    grad_sent = jnp.einsum(
        "secf,edf->secd", grad_gate_pre, gate_weight, preferred_element_type=jnp.float32
    )
    grad_sent = (
        grad_sent
        + jnp.einsum("secf,edf->secd", grad_up_pre, up_weight, preferred_element_type=jnp.float32)
    ).astype(jnp.bfloat16)
    grad_back = route_rows(grad_sent).reshape(expert_count * capacity, model_width)
    grad_moe_in = jnp.sum(
        grad_back[slots].reshape(tok_rows, top_count, model_width).astype(jnp.float32), axis=1
    )
    grad_chosen = gate_values * (
        grad_gates - jnp.sum(gate_values * grad_gates, axis=1, keepdims=True)
    )
    grad_logits = jnp.einsum("tk,tke->te", grad_chosen, onehot_routes, precision=HIGH)
    router_float = full_router.astype(jnp.float32)
    grad_moe_in = grad_moe_in + jnp.einsum("te,de->td", grad_logits, router_float, precision=HIGH)
    grad_router = jnp.einsum("td,te->de", moe_in.astype(jnp.float32), grad_logits, precision=HIGH)
    grad_hidden_norm, grad_experts_gain = experts_back(grad_moe_in)
    grad_hidden = grad_output + grad_hidden_norm
    grad_branch = lax.all_gather(grad_hidden.astype(jnp.bfloat16), "tensor", axis=0, tiled=True)
    grad_attended = jnp.einsum(
        "td,ad->ta", grad_branch, full_out, preferred_element_type=jnp.float32
    ).astype(jnp.bfloat16)
    grad_blocks = grad_attended.reshape(block_count, block_rows, kv_heads, group_size, head_width)

    def backward_block(carry, item):
        key_sum, value_sum = carry
        offset, log_total, grad_block = item
        query_block, masked = masked_scores(offset, block_rows, queries, key_rows, score_scale)
        soft_weights = jnp.exp(masked - log_total)
        soft_low = soft_weights.astype(jnp.bfloat16)
        grad_soft = jnp.einsum(
            "qkgd,ckd->kgqc", grad_block, value_rows, preferred_element_type=jnp.float32
        )
        inner_sum = jnp.sum(soft_weights * grad_soft, axis=-1, keepdims=True)
        grad_scores = (soft_weights * (grad_soft - inner_sum)).astype(jnp.bfloat16)
        grad_query_block = (
            jnp.einsum("kgqc,ckd->qkgd", grad_scores, key_rows, preferred_element_type=jnp.float32)
            * score_scale
        )
        key_sum = (
            key_sum
            + jnp.einsum(
                "kgqc,qkgd->ckd", grad_scores, query_block, preferred_element_type=jnp.float32
            )
            * score_scale
        )
        value_sum = value_sum + jnp.einsum(
            "kgqc,qkgd->ckd", soft_low, grad_block, preferred_element_type=jnp.float32
        )
        return ((key_sum, value_sum), grad_query_block)

    zero_rows = jnp.zeros((length, kv_heads, head_width), jnp.float32)
    (key_sum, value_sum), grad_query_blocks = lax.scan(
        backward_block, (zero_rows, zero_rows), (offsets, log_totals, grad_blocks)
    )
    grad_query_raw, grad_query_gain = query_back(grad_query_blocks.reshape(length, -1))
    grad_key_raw, grad_key_gain = key_back(key_sum.reshape(length, -1))
    grad_query_low = grad_query_raw.astype(jnp.bfloat16)
    grad_key_low = grad_key_raw.astype(jnp.bfloat16)
    grad_value_low = value_sum.reshape(length, -1).astype(jnp.bfloat16)
    total = jnp.einsum("tc,dc->td", grad_query_low, full_query, preferred_element_type=jnp.float32)
    total = total + jnp.einsum(
        "tc,dc->td", grad_key_low, full_key, preferred_element_type=jnp.float32
    )
    grad_sequence = lax.psum_scatter(
        (
            total
            + jnp.einsum(
                "tc,dc->td", grad_value_low, full_value, preferred_element_type=jnp.float32
            )
        ).astype(jnp.bfloat16),
        "tensor",
        scatter_dimension=0,
        tiled=True,
    ).astype(jnp.float32)
    grad_inputs_norm, grad_attention_gain = attention_back(grad_sequence)
    grad_inputs = grad_hidden + grad_inputs_norm
    query_cols = grad_query_low.shape[1]
    key_cols = grad_key_low.shape[1]
    grad_raw_all = jnp.concatenate([grad_query_low, grad_key_low, grad_value_low], axis=1)
    inward = jnp.einsum("td,tc->dc", sequence, grad_raw_all, preferred_element_type=jnp.float32)
    outward = jnp.einsum("td,ta->da", grad_branch, attended, preferred_element_type=jnp.float32)
    owned = lax.psum_scatter(
        jnp.concatenate([inward, outward], axis=1), "dp", scatter_dimension=0, tiled=True
    )
    grad_query_weight = owned[:, :query_cols]
    grad_key_weight = owned[:, query_cols : query_cols + key_cols]
    grad_value_weight = owned[:, query_cols + key_cols : query_cols + 2 * key_cols]
    grad_out_weight = owned[:, query_cols + 2 * key_cols :].T
    router_total, attention_total, query_total, key_total, experts_total = lax.psum(
        (grad_router, grad_attention_gain, grad_query_gain, grad_key_gain, grad_experts_gain),
        ("dp", "tensor"),
    )
    router_rows = router_weight.shape[0]
    router_share = lax.dynamic_slice_in_dim(
        router_total, lax.axis_index("dp") * router_rows, router_rows, 0
    )
    return (
        output,
        grad_inputs,
        attention_total,
        grad_query_weight,
        grad_key_weight,
        grad_value_weight,
        query_total,
        key_total,
        grad_out_weight,
        experts_total,
        router_share,
        grad_gate,
        grad_up,
        grad_down,
    )


low, wide = jnp.bfloat16, jnp.float32
Z_RING = tuple((i, (i + 4) % 16) for i in range(16))
Z_PAIR = tuple((i, i ^ 4) for i in range(16))
Z_FAR = tuple((i, i ^ 8) for i in range(16))
Y_PAIR = tuple((i, i ^ 2) for i in range(16))
X_PAIR = tuple((i, i ^ 1) for i in range(16))
BLOCKS = tuple((k, dy, dx) for k in range(4) for dy in range(2) for dx in range(2))
PLANE = tuple((dy, dx) for dy in range(2) for dx in range(2))
OVER_X = (1, 2)
ROOM = 8 * 2**20
WHOLE = 60 * 2**20
TILE = 256
WIDE = 512
HIDDEN_TILE = 768
NT = (((1,), (1,)), ((), ()))
TN = (((0,), (0,)), ((), ()))


def z_next(block):
    return lax.ppermute(block, "dp", Z_RING)


def z_pair(block):
    return lax.ppermute(block, "dp", Z_PAIR)


def z_far(block):
    return lax.ppermute(block, "dp", Z_FAR)


def y_swap(block):
    return lax.ppermute(block, "dp", Y_PAIR)


def x_swap(block):
    return lax.ppermute(block, "dp", X_PAIR)


def core_swap(block):
    return lax.ppermute(block, "tensor", ((0, 1), (1, 0)))


def after(value, *earlier):
    return lax.optimization_barrier((value, *earlier))[0]


def part(term):
    return term[0][term[1]] if isinstance(term, tuple) else term


def plus(*terms):
    total = part(terms[0]).astype(wide)
    for other in terms[1:]:
        total = total + part(other).astype(wide)
    return total


TOKEN_ROUNDS = (
    (((0, 0, 0), (0, 0, 1), x_swap), ((0, 0, 0), (0, 1, 0), y_swap), ((0, 0, 0), (1, 0, 0), z_next)),
    (((1, 0, 0), (1, 0, 1), x_swap), ((0, 0, 1), (0, 1, 1), y_swap), ((1, 0, 0), (2, 0, 0), z_next)),
    (((2, 0, 0), (2, 0, 1), x_swap), ((1, 0, 0), (1, 1, 0), y_swap), ((2, 0, 0), (3, 0, 0), z_next)),
    (((3, 0, 0), (3, 0, 1), x_swap), ((2, 0, 0), (2, 1, 0), y_swap), ((0, 1, 1), (1, 1, 1), z_next)),
    (((2, 1, 0), (2, 1, 1), x_swap), ((3, 0, 1), (3, 1, 1), y_swap), ((2, 1, 0), (3, 1, 0), z_next)),
)
WEIGHT_ROUNDS = (
    (
        ((0, 0, 0), (0, 0, 1), x_swap),
        ((0, 0, 0), (0, 1, 0), y_swap),
        ((0, 0, 0), (2, 0, 0), z_far, True),
    ),
    (
        ((1, 0, 0), (1, 0, 1), x_swap),
        ((1, 0, 0), (1, 1, 0), y_swap),
        ((1, 0, 0), (3, 0, 0), z_far, True),
        ((0, 0, 1), (0, 1, 1), y_swap),
    ),
    (
        ((2, 0, 0), (2, 0, 1), x_swap),
        ((2, 0, 0), (2, 1, 0), y_swap),
        ((1, 1, 0), (1, 1, 1), x_swap),
    ),
    (
        ((3, 0, 0), (3, 1, 0), y_swap),
        ((3, 0, 0), (3, 0, 1), x_swap),
        ((2, 0, 1), (2, 1, 1), y_swap),
    ),
    (((3, 1, 0), (3, 1, 1), x_swap),),
)
SHORT_ROUNDS = (
    (*WEIGHT_ROUNDS[0][:2],),
    (((0, 0, 0), (2, 0, 0), z_far, True), *WEIGHT_ROUNDS[1][:2], WEIGHT_ROUNDS[1][3]),
    (((1, 0, 0), (3, 0, 0), z_far), *WEIGHT_ROUNDS[2]),
    (*WEIGHT_ROUNDS[3], ((1, 1, 1), (3, 1, 1), z_far)),
)
WEIGHT_RETURNS = (
    (((3, 1, 1), (3, 1, 0), x_swap),),
    (
        ((3, 1, 0), (3, 0, 0), y_swap),
        ((3, 0, 1), (3, 0, 0), x_swap),
        ((2, 1, 1), (2, 0, 1), y_swap),
    ),
    (
        ((3, 0, 0), (1, 0, 0), z_far),
        ((2, 0, 1), (2, 0, 0), x_swap),
        ((2, 1, 0), (2, 0, 0), y_swap),
        ((1, 1, 1), (1, 1, 0), x_swap),
    ),
    (
        ((2, 0, 0), (0, 0, 0), z_far),
        ((1, 1, 0), (1, 0, 0), y_swap),
        ((1, 0, 1), (1, 0, 0), x_swap),
        ((0, 1, 1), (0, 0, 1), y_swap),
    ),
    (((0, 0, 1), (0, 0, 0), x_swap), ((0, 1, 0), (0, 0, 0), y_swap)),
)


RETURN_ROUNDS = (
    (((1, 1, 1), (1, 0, 1), y_swap), ((0, 1, 1), (0, 1, 0), x_swap), ((1, 1, 0), (2, 1, 0), z_next)),
    (((1, 0, 1), (1, 0, 0), x_swap), ((2, 1, 1), (2, 0, 1), y_swap), ((2, 1, 0), (3, 1, 0), z_next)),
    (((2, 0, 1), (2, 0, 0), x_swap), ((3, 1, 1), (3, 0, 1), y_swap), ((1, 0, 0), (2, 0, 0), z_next)),
    (((3, 0, 1), (3, 0, 0), x_swap), ((3, 1, 0), (3, 0, 0), y_swap), ((2, 0, 0), (3, 0, 0), z_next)),
    (((0, 0, 1), (0, 0, 0), x_swap), ((0, 1, 0), (0, 0, 0), y_swap), ((3, 0, 0), (0, 0, 0), z_next)),
)
OUTPUT_ROUNDS = (
    (((3, 1, 1), (3, 1, 0), x_swap), ((1, 1, 1), (1, 0, 1), y_swap), ((1, 1, 0), (2, 1, 0), z_next)),
    (((1, 0, 1), (1, 0, 0), x_swap), ((2, 1, 1), (2, 0, 1), y_swap)),
    (((2, 0, 1), (2, 0, 0), x_swap), ((2, 1, 0), (2, 0, 0), y_swap), ((1, 0, 0), (2, 0, 0), z_next)),
    (((3, 0, 1), (3, 0, 0), x_swap), ((3, 1, 0), (3, 0, 0), y_swap), ((2, 0, 0), (3, 0, 0), z_next)),
    (((0, 1, 1), (0, 1, 0), x_swap),),
    (((0, 0, 1), (0, 0, 0), x_swap), ((0, 1, 0), (0, 0, 0), y_swap), ((3, 0, 0), (0, 0, 0), z_next)),
)


class Chain:
    def __init__(self):
        self.earlier = []
        self.late = []
        self.values = []

    def add(self, *values):
        self.earlier.extend(values)

    def send(self, values, ways, late=()):
        values = lax.optimization_barrier((*values, *self.earlier))[: len(values)]
        self.values = values
        results = [way(value) for value, way in zip(values, ways)]
        self.earlier = self.late + [r for i, r in enumerate(results) if i not in late]
        self.late = [results[i] for i in late]
        return results

    def round(self, values, moves, others):
        late = [i for i, move in enumerate(moves) if len(move) > 3]
        values = values + [value for value, _ in others]
        ways = [move[2] for move in moves] + [way for _, way in others]
        results = self.send(values, ways, late)
        return results[: len(moves)], results[len(moves) :]

    def gather(self, pairs, others=()):
        values = [held[move[0]] for held, moves in pairs for move in moves]
        moves = [move for _, moves in pairs for move in moves]
        results, rest = self.round(values, moves, others)
        for (held, end), result in zip([(h, m[1]) for h, ms in pairs for m in ms], results):
            held[end] = result
        return rest

    def scatter(self, pairs, others=(), later=None):
        if later is not None:
            for terms, moves in pairs:
                for move in moves:
                    last = terms[move[0]][-1]
                    held = isinstance(last, tuple)
                    gated = after(last[0] if held else last, later)
                    terms[move[0]][-1] = (gated, last[1]) if held else gated
        gathered = []
        for terms, moves in pairs:
            for move in moves:
                same = [g for g in gathered if g[0] is terms and g[1] is move[2] and len(g[2]) == 1]
                if same and terms[move[0]][0].shape[-1] < 2000:
                    same[0][2].append(move)
                else:
                    gathered.append((terms, move[2], [move]))
        groups = [[terms[move[0]] for move in moves] for terms, _, moves in gathered]
        values = totals(groups)
        results, rest = self.round(values, [moves[0] for _, _, moves in gathered], others)
        for (terms, _, moves), result in zip(gathered, results):
            for index, move in enumerate(moves):
                terms[move[1]].append((result, index) if len(moves) == 2 else result)
        return rest


def sum_kernel(groups, *refs):
    outs = refs[sum(sum(group) for group in groups) :]
    for group, out in zip(groups, outs):
        for index, count in enumerate(group):
            terms, refs = refs[:count], refs[count:]
            total = terms[0][...].astype(wide)
            for term in terms[1:]:
                total = total + term[...].astype(wide)
            if len(group) == 1:
                out[...] = total.astype(out.dtype)
            else:
                out[index] = total.astype(out.dtype)


def totals(groups):
    made = [g for g in groups if len(g) > 1 or len(g[0]) > 1 or isinstance(g[0][0], tuple)]
    if not made:
        return [g[0][0] for g in groups]
    operands, in_specs, out_shape, out_specs = [], [], [], []
    for group in made:
        for terms in group:
            for term in terms:
                array, index = term if isinstance(term, tuple) else (term, None)
                rows, columns = array.shape[-2] // 4, array.shape[-1]
                operands.append(array)
                if index is None:
                    in_specs.append(pl.BlockSpec((rows, columns), lambda i: (i, 0)))
                else:
                    in_specs.append(
                        pl.BlockSpec((None, rows, columns), lambda i, index=index: (index, i, 0))
                    )
        if len(group) == 1:
            out_shape.append(jax.ShapeDtypeStruct((4 * rows, columns), low))
            out_specs.append(pl.BlockSpec((rows, columns), lambda i: (i, 0)))
        else:
            out_shape.append(jax.ShapeDtypeStruct((2, 4 * rows, columns), low))
            out_specs.append(pl.BlockSpec((2, rows, columns), lambda i: (0, i, 0)))
    sums = pl.pallas_call(
        functools.partial(sum_kernel, [[len(terms) for terms in group] for group in made]),
        grid=(4,),
        out_shape=out_shape,
        in_specs=in_specs,
        out_specs=out_specs,
        name="sums",
        compiler_params=pltpu.CompilerParams(vmem_limit_bytes=2 * ROOM),
    )(*operands)
    sums = list(sums)
    return [sums.pop(0) if any(g is m for m in made) else g[0][0] for g in groups]


def dot(left, right, dims=None):
    if dims is None:
        return jnp.dot(left, right, preferred_element_type=wide)
    return lax.dot_general(left, right, dims, preferred_element_type=wide)


def lanes(start, size):
    return pl.ds(pl.multiple_of(start, 128), size)


def spot(ids, i):
    return pl.multiple_of(ids[i] * 128, 128)


def row_copies(ids, blocks, whole, sems):
    return [
        pltpu.make_async_copy(block, whole.at[pl.ds(spot(ids, i), 128), :], sems.at[i])
        for i, block in enumerate(blocks)
    ]


def column_copies(ids, blocks, whole, sems):
    return [
        pltpu.make_async_copy(block, whole.at[:, pl.ds(spot(ids, i), 128)], sems.at[i])
        for i, block in enumerate(blocks)
    ]


def stack_copies(blocks, whole, sems):
    rows = blocks[0].shape[0]
    return [
        pltpu.make_async_copy(block, whole.at[pl.ds(i * rows, rows), :], sems.at[i])
        for i, block in enumerate(blocks)
    ]


def start_all(copies):
    for copy in copies:
        copy.start()


def wait_all(copies):
    for copy in copies:
        copy.wait()


def head_forward(raw, gain, cosine, sine):
    inverse = lax.rsqrt(jnp.mean(raw * raw, axis=-1, keepdims=True) + EPS)
    unit = raw * inverse
    shaped = unit * gain
    return unit, inverse, shaped * cosine + pltpu.roll(shaped, 64, 1) * sine


def head_backward(grad, unit, inverse, gain, cosine, sine):
    back = grad * cosine - pltpu.roll(grad, 64, 1) * sine
    gain_grad = jnp.sum(back * unit, axis=0, keepdims=True)
    scaled = back * gain
    return gain_grad, inverse * (scaled - unit * jnp.mean(scaled * unit, axis=-1, keepdims=True))


def causal(core, length):
    half = length // 2
    rows = lax.broadcasted_iota(jnp.int32, (length, length), 0)
    columns = lax.broadcasted_iota(jnp.int32, (length, length), 1)

    def place(i):
        return jnp.where(i < half, i + core * half, i - half + (1 - core) * half)

    return place(columns) <= place(rows)


def soft(query, key, allowed, scale):
    scores = jnp.where(allowed, dot(query, key, NT) * scale, -1e30)
    raised = jnp.exp(scores - jnp.max(scores, axis=-1, keepdims=True))
    return raised / jnp.sum(raised, axis=-1, keepdims=True)


def raw_kernel(ids, block_ids, *refs):
    seq_blocks, blocks = refs[:4], refs[4:20]
    raw, router, rest, whole, seq, sems = refs[20:]
    copies = stack_copies(seq_blocks, seq, sems.at[pl.ds(16, 4)]) + row_copies(
        ids, blocks, whole, sems
    )
    start_all(copies)
    wait_all(copies)
    width = raw.shape[1]

    @pl.loop(0, width // TILE)
    def _(j):
        span = lanes(j * TILE, TILE)
        raw[:, span] = dot(seq[...], whole[:, span])

    router[...] = whole[:, width:]
    for p in range(16):
        rest[p * 128 : (p + 1) * 128, :] = whole[pl.ds(spot(block_ids, p), 128), width:]


def forward_kernel(head_count, core, raw, cosine, sine, query_gain, key_gain, attended):
    length = raw.shape[0] // 2
    key_start = head_count * 128
    allowed = causal(core[0], length)
    scale = 128 ** (-0.5)
    for s in range(2):
        span = slice(s * length, (s + 1) * length)
        turn = (cosine[...], sine[...])
        key_raw = raw[span, key_start : key_start + 128]
        key = head_forward(key_raw, key_gain[...], *turn)[2].astype(low)
        value = raw[span, key_start + 128 : key_start + 256].astype(low)

        @pl.loop(0, head_count, unroll=2)
        def _(h):
            columns = lanes(h * 128, 128)
            query = head_forward(raw[span, columns], query_gain[...], *turn)[2].astype(low)
            weights = soft(query, key, allowed, scale)
            attended[span, columns] = dot(weights.astype(low), value).astype(low)


def split_rows(product, span, sent, kept):
    rows = product.shape[0] // 4
    kept[:rows, span] = product[:rows]
    sent[:rows, span] = product[rows : 2 * rows].astype(low)
    kept[rows:, span] = product[2 * rows : 3 * rows]
    sent[rows:, span] = product[3 * rows :].astype(low)


def out_kernel(ids, attended, *refs):
    blocks, (sent, kept, whole, sems) = refs[:16], refs[16:]
    copies = column_copies(ids, blocks, whole, sems)
    start_all(copies)
    wait_all(copies)

    @pl.loop(0, whole.shape[1] // WIDE)
    def _(j):
        span = lanes(j * WIDE, WIDE)
        split_rows(dot(attended[...], whole[:, span]), span, sent, kept)


def normed_grad_kernel(ids, grad_raw, gain, *refs):
    seq_blocks, blocks = refs[:4], refs[4:20]
    sent, kept, gain_grad, whole, seq, sems = refs[20:]
    copies = row_copies(ids, blocks, whole, sems) + stack_copies(
        seq_blocks, seq, sems.at[pl.ds(16, 4)]
    )
    start_all(copies)
    wait_all(copies)
    width = grad_raw.shape[1]

    @pl.loop(0, whole.shape[0] // WIDE)
    def _(j):
        span = lanes(j * WIDE, WIDE)
        product = dot(grad_raw[...], whole[span, :width], NT)
        split_rows(product, span, sent, kept)
        unit = seq[:, span].astype(wide) / gain[:, span]
        gain_grad[:, span] = jnp.sum(product * unit, axis=0, keepdims=True)


def attended_grad_kernel(ids, *refs):
    grad_blocks, blocks = refs[:4], refs[4:20]
    grad_attended, grad_branch, whole, sems = refs[20:]
    copies = stack_copies(grad_blocks, grad_branch, sems.at[pl.ds(16, 4)]) + column_copies(
        ids, blocks, whole, sems
    )
    start_all(copies)
    wait_all(copies)

    @pl.loop(0, grad_attended.shape[1] // WIDE)
    def _(j):
        span = lanes(j * WIDE, WIDE)
        grad_attended[:, span] = dot(grad_branch[...], whole[span, :], NT).astype(low)


def map_kernel(capacity, expert_count, experts, named, picks, turned_picks):
    slot_rows = 4 * capacity
    early = lax.broadcasted_iota(jnp.int32, (128, 128), 0)
    late = lax.broadcasted_iota(jnp.int32, (128, 128), 1)
    before = jnp.where(early < late, 1.0, 0.0).astype(low)
    behind = jnp.where(late < early, 1.0, 0.0).astype(low)
    slot_numbers = lax.broadcasted_iota(jnp.int32, (slot_rows, 128), 0)
    slot_lanes = lax.broadcasted_iota(jnp.int32, (128, turned_picks.shape[1]), 1)
    for b in range(16):
        k, i = b // 4, b % 4
        block = named[b * 128 : (b + 1) * 128, :]
        turned_slots = []
        for c in range(2):
            column = experts[c] + expert_count
            own_lane = lax.broadcasted_iota(jnp.int32, (8, 128), 1) == column
            hit = dot(jnp.where(own_lane, 1.0, 0.0).astype(low), block, NT)
            slot = dot(hit.astype(low), before) + float(i * capacity)
            slot = jnp.where(hit > 0.5, slot, -1.0).astype(jnp.int32)
            first = (2 * k + c) * slot_rows
            picks[first : first + slot_rows, i * 128 : (i + 1) * 128] = jnp.where(
                slot_numbers == slot[:1], 1.0, 0.0
            ).astype(low)
            mine = jnp.where(late == column, block.astype(wide), 0.0)
            hit = jnp.sum(mine, axis=1, keepdims=True)
            slot = jnp.sum(dot(behind, mine.astype(low)), axis=1, keepdims=True)
            slot = slot + float(i * capacity + c * slot_rows)
            turned_slots.append(jnp.where(hit > 0.5, slot, -1.0).astype(jnp.int32))
        either = jnp.logical_or(slot_lanes == turned_slots[0], slot_lanes == turned_slots[1])
        turned_picks[b * 128 : (b + 1) * 128, :] = jnp.where(either, 1.0, 0.0).astype(low)


def pick_kernel(k, picks_in, named, *refs):
    tokens, cots, (own, other, picks, rows, sems) = refs[:4], refs[4:8], refs[8:]
    quad_rows, full = rows.shape
    width = tokens[0].shape[1]
    copies = (
        stack_copies(tokens, rows.at[:, pl.ds(0, width)], sems.at[pl.ds(0, 4)])
        + stack_copies(cots, rows.at[:, pl.ds(width + 128, width)], sems.at[pl.ds(4, 4)])
        + [
            pltpu.make_async_copy(
                picks_in.at[pl.ds(k * picks.shape[0], picks.shape[0]), :], picks, sems.at[8]
            ),
            pltpu.make_async_copy(
                named.at[pl.ds(k * quad_rows, quad_rows), :],
                rows.at[:, pl.ds(width, 128)],
                sems.at[9],
            ),
        ]
    )
    start_all(copies)
    wait_all(copies)
    slot_rows = own.shape[0]
    for start in range(0, full, WIDE):
        span = slice(start, min(start + WIDE, full))
        made = dot(picks[...], rows[:, span]).astype(low)
        own[:, span] = made[:slot_rows]
        other[:, span] = made[slot_rows:]


def expert_kernel(expert_count, k, experts, router, *refs):
    sides, weights = refs[:2], refs[2:5]
    refs = refs[5 + (5 if k else 0) :]
    (all_rows, all_act, all_grads, all_gate, all_up, own_out, back_out) = refs[:7]
    (rows, v_gate, v_up, v_down, act, grads, gate_back, up_back) = refs[7:15]
    (gate_pre, up_pre, sig, sems) = refs[15:]
    slot_rows = own_out.shape[0]
    width, hidden = v_gate.shape
    after_width = width + 128
    spans = [slice(c * slot_rows, (c + 1) * slot_rows) for c in range(2)]
    side_copies = stack_copies(sides, rows, sems.at[pl.ds(0, 2)])
    weight_copies = [
        pltpu.make_async_copy(a, b, sems.at[2 + i])
        for i, (a, b) in enumerate(zip(weights, (v_gate, v_up, v_down)))
    ]
    start_all(side_copies + weight_copies)
    kept = []

    def keep(source, target, sem):
        copy = pltpu.make_async_copy(
            source.at[:, pl.ds(0, target.shape[1])],
            target.at[pl.ds(k * 2 * slot_rows, 2 * slot_rows), :],
            sems.at[sem],
        )
        copy.start()
        kept.append(copy)

    wait_all(side_copies)
    keep(rows, all_rows, 5)
    logits = dot(rows[:, :width], router[...])
    numbers = lax.broadcasted_iota(jnp.int32, logits.shape, 1)
    is_named = pltpu.roll(rows[:, width:after_width].astype(wide), 128 - expert_count, 1)
    is_named = jnp.logical_and(is_named > 0.5, numbers < expert_count)
    lifted = jnp.where(is_named, logits, -1e30)
    lifted = jnp.where(
        is_named, jnp.exp(lifted - jnp.max(lifted, axis=1, keepdims=True)), 0.0
    )
    mine = jnp.sum(jnp.where(numbers == experts[0], lifted, 0.0), axis=1, keepdims=True)
    gates = mine / jnp.maximum(jnp.sum(lifted, axis=1, keepdims=True), 1e-30)
    wait_all(weight_copies[:2])
    pre = dot(rows[:, :width], v_gate[...])
    up = dot(rows[:, :width], v_up[...])
    s = jax.nn.sigmoid(pre)
    gate_pre[...] = pre
    up_pre[...] = up
    sig[...] = s
    act[...] = (pre * s * up).astype(low)
    keep(act, all_act, 6)
    wait_all(weight_copies[2:])
    slot_grads = jnp.zeros((2 * slot_rows, 1), wide)
    for j in range(width // WIDE):
        span = slice(j * WIDE, (j + 1) * WIDE)
        later = slice(after_width + j * WIDE, after_width + (j + 1) * WIDE)
        out = dot(act[...], v_down[:, span]).astype(low).astype(wide)
        cot = rows[:, later].astype(wide)
        grads[:, span] = (gates * cot).astype(low)
        scaled = (gates * out).astype(low)
        own_out[:, later] = scaled[spans[0]]
        back_out[:, later] = scaled[spans[1]]
        slot_grads = slot_grads + jnp.sum(cot * out, axis=1, keepdims=True)
    keep(grads, all_grads, 7)
    back = dot(grads[...], v_down[...], NT)
    pre, s = gate_pre[...], sig[...]
    gate_back[...] = (back * up_pre[...] * s * (1.0 + pre * (1.0 - s))).astype(low)
    up_back[...] = (back * (pre * s)).astype(low)
    keep(gate_back, all_gate, 8)
    keep(up_back, all_up, 9)
    for j in range(width // WIDE):
        span = slice(j * WIDE, (j + 1) * WIDE)
        back = dot(gate_back[...], v_gate[span, :], NT) + dot(up_back[...], v_up[span, :], NT)
        back = back.astype(low)
        own_out[:, span] = back[spans[0]]
        back_out[:, span] = back[spans[1]]
    high = slot_grads.astype(low).astype(wide)
    rest = jnp.where(numbers == experts[0] + expert_count, slot_grads - high, 0.0)
    parts = jnp.where(numbers == experts[0], high, rest).astype(low)
    own_out[:, width:after_width] = parts[spans[0]]
    back_out[:, width:after_width] = parts[spans[1]]
    wait_all(kept)


def token_sum_kernel(k, turned_picks, *refs):
    sides, blocks, outputs, (picks, rows, out_rows, sems) = refs[:2], refs[2:6], refs[6:10], refs[10:]
    quad_rows, width = out_rows.shape
    copies = stack_copies(sides, rows, sems.at[pl.ds(0, 2)]) + [
        pltpu.make_async_copy(
            turned_picks.at[pl.ds(k * quad_rows, quad_rows), :], picks, sems.at[2]
        )
    ]
    start_all(copies)
    wait_all(copies)
    slots = rows.shape[0]
    size, first = blocks[0].shape
    for j in range(0, width, WIDE):
        span = slice(j, j + WIDE)
        out_rows[:, span] = dot(picks[:, :slots], rows[:, first + j : first + j + WIDE]).astype(low)
    copies = [
        pltpu.make_async_copy(out_rows.at[pl.ds(i * size, size), :], output, sems.at[3 + i])
        for i, output in enumerate(outputs)
    ]
    start_all(copies)
    for j in range(0, first, WIDE):
        span = slice(j, min(j + WIDE, first))
        made = dot(picks[:, :slots], rows[:, span]).astype(low)
        for i, block in enumerate(blocks):
            block[:, span] = made[i * size : (i + 1) * size]
    wait_all(copies)


def backward_kernel(head_count, core, raw, grad_attended, *refs):
    cosine, sine, query_gain, key_gain = refs[:4]
    grad_raw, query_gain_grad, key_gain_grad, key_sum, value_sum = refs[4:]
    length = raw.shape[0] // 2
    key_start = head_count * 128
    allowed = causal(core[0], length)
    scale = 128 ** (-0.5)
    turn = (cosine[...], sine[...])
    query_gain_grad[...] = jnp.zeros_like(query_gain_grad)
    key_gain_grad[...] = jnp.zeros_like(key_gain_grad)
    for s in range(2):
        span = slice(s * length, (s + 1) * length)
        key_raw = raw[span, key_start : key_start + 128]
        key_unit, key_inverse, key = head_forward(key_raw, key_gain[...], *turn)
        key = key.astype(low)
        value = raw[span, key_start + 128 : key_start + 256].astype(low)
        key_sum[...] = jnp.zeros_like(key_sum)
        value_sum[...] = jnp.zeros_like(value_sum)

        @pl.loop(0, head_count, unroll=2)
        def _(h):
            columns = lanes(h * 128, 128)
            unit, inverse, query = head_forward(raw[span, columns], query_gain[...], *turn)
            query = query.astype(low)
            weights = soft(query, key, allowed, scale)
            grad = grad_attended[span, columns]
            grad_soft = dot(grad, value, NT)
            inner = jnp.sum(weights * grad_soft, axis=-1, keepdims=True)
            grad_scores = (weights * (grad_soft - inner)).astype(low)
            value_sum[...] += dot(weights.astype(low), grad, TN)
            key_sum[...] += dot(grad_scores, query, TN) * scale
            grad_query = dot(grad_scores, key) * scale
            gain_grad, back = head_backward(grad_query, unit, inverse, query_gain[...], *turn)
            query_gain_grad[...] += gain_grad
            grad_raw[span, columns] = back.astype(low)

        gain_grad, back = head_backward(
            key_sum[...], key_unit, key_inverse, key_gain[...], *turn
        )
        key_gain_grad[...] += gain_grad
        grad_raw[span, key_start : key_start + 128] = back.astype(low)
        grad_raw[span, key_start + 128 : key_start + 256] = value_sum[...].astype(low)


def block_product_kernel(with_rest, ids, right, *refs):
    left_blocks, refs = refs[:4], refs[4:]
    rest, refs = (refs[0], refs[1:]) if with_rest else (None, refs)
    outs, (left, sems) = refs[:16], refs[16:]
    copies = stack_copies(left_blocks, left, sems)
    start_all(copies)
    wait_all(copies)
    width = right.shape[1]
    for i, out in enumerate(outs):
        part = left[:, pl.ds(spot(ids, i), 128)]
        out[:, :width] = dot(part, right[...], TN).astype(low)
        if with_rest:
            out[:, width:] = jnp.transpose(rest[:, pl.ds(spot(ids, i), 128)]).astype(low)


SMEM = pl.BlockSpec(memory_space=pltpu.SMEM)
VMEM = pl.BlockSpec(memory_space=pltpu.VMEM)
FAR = pl.BlockSpec(memory_space=pl.ANY)
HBM = pl.BlockSpec(memory_space=pltpu.HBM)


def call(kernel, name, ins, outs, scratch, flops, specs=None, aliases=None, alone=False):
    operands = [value for value, _ in ins]
    moved = sum(a.size * a.dtype.itemsize for a in operands + outs)
    placed = [value for value, spec in ins if spec is VMEM] + scratch
    placed += [out for out, spec in zip(outs, specs or [VMEM] * len(outs)) if spec is VMEM]
    held = sum(
        math.prod(a.shape) * jnp.dtype(a.dtype).itemsize
        for a in placed
        if jnp.issubdtype(a.dtype, jnp.floating)
    )
    return pl.pallas_call(
        kernel,
        out_shape=outs,
        in_specs=[spec for _, spec in ins],
        out_specs=specs or [VMEM] * len(outs),
        scratch_shapes=scratch,
        name=name,
        input_output_aliases=aliases or {},
        compiler_params=pltpu.CompilerParams(vmem_limit_bytes=WHOLE if alone else ROOM + held),
        cost_estimate=pl.CostEstimate(flops=flops, bytes_accessed=moved, transcendentals=0),
    )(*operands)


def shape(rows, columns, dtype):
    return jax.ShapeDtypeStruct((rows, columns), dtype)


def copies_sem(count):
    return pltpu.SemaphoreType.DMA((count,))


def local_sixteen(
    inputs,
    attention_gain,
    query_weight,
    key_weight,
    value_weight,
    query_gain,
    key_gain,
    out_weight,
    feedforward_gain,
    router_weight,
    gate_weight,
    up_weight,
    down_weight,
    routes,
    cotangent,
):
    tok_rows, model_width = inputs.shape
    head_width = query_gain.shape[0]
    top_count = routes.shape[1]
    expert_count = router_weight.shape[1]
    hidden_width = gate_weight.shape[2]
    capacity = tok_rows * top_count * 11 // (expert_count * 8)
    query_cols, key_cols = query_weight.shape[1] // 2, key_weight.shape[1] // 2
    raw_cols = query_cols + 2 * key_cols
    head_count = query_cols // head_width
    place = lax.axis_index("dp")
    core = lax.axis_index("tensor")
    z, y, x = place // 4, (place // 2) % 2, place % 2
    even = z % 2 == 0
    core_id = core.astype(jnp.int32)[None]
    block_ids = jnp.stack(
        [((z - k) % 4) * 4 + (y ^ dy) * 2 + (x ^ dx) for k, dy, dx in BLOCKS]
    ).astype(jnp.int32)
    weight_ids = jnp.stack(
        [(z ^ w) * 4 + (y ^ dy) * 2 + (x ^ dx) for w, dy, dx in BLOCKS]
    ).astype(jnp.int32)

    def halves(values, axis):
        first, second = jnp.split(values, 2, axis=axis)
        return jnp.where(even, first, second), jnp.where(even, second, first)

    def in_order(mine, theirs, axis):
        return jnp.where(
            even,
            jnp.concatenate([mine, theirs], axis=axis),
            jnp.concatenate([theirs, mine], axis=axis),
        )

    chain = Chain()
    numbers = jnp.arange(expert_count, dtype=jnp.int32)
    own_named = jnp.any(routes[:, :, None] == numbers, axis=1)
    splits = [halves(w, 1) for w in (query_weight, key_weight, value_weight)]
    rest = [
        router_weight,
        own_named.astype(low),
        jnp.zeros((tok_rows, 128 - 2 * expert_count), low),
    ]
    mine = jnp.concatenate([s[0] for s in splits] + rest, axis=1)
    theirs = jnp.concatenate([s[1] for s in splits] + rest, axis=1)
    held = {(0, 0, 0): mine}
    (held[1, 0, 0],) = chain.gather([(held, WEIGHT_ROUNDS[0])], [(theirs, z_pair)])
    inputs_float = inputs.astype(wide)
    normed_attention, attention_back = jax.vjp(rms_scale, inputs_float, attention_gain)
    normed = normed_attention.astype(low)
    chain.add(normed)
    chain.gather([(held, WEIGHT_ROUNDS[1])])
    chain.gather([(held, WEIGHT_ROUNDS[2])])
    far, swapped = chain.gather(
        [(held, WEIGHT_ROUNDS[3])], [(normed, z_pair), (normed, core_swap)]
    )
    out_mine, out_theirs = halves(out_weight, 0)
    out_held = {(0, 0, 0): out_mine}
    cot_held = {(0, 0, 0): cotangent}
    far_swapped, out_held[1, 0, 0] = chain.gather(
        [(held, WEIGHT_ROUNDS[4]), (out_held, SHORT_ROUNDS[0])],
        [(far, core_swap), (out_theirs, z_pair)],
    )
    sequence = [normed, swapped, far, far_swapped]
    blocks = [held[b] for b in BLOCKS]
    chain.gather([(out_held, SHORT_ROUNDS[1])])
    grad_output = cotangent.astype(wide)
    length = 2 * tok_rows
    own_places = jnp.arange(tok_rows, dtype=jnp.int32)
    places = jnp.concatenate([own_places + core * tok_rows, own_places + (1 - core) * tok_rows])
    halfway = head_width // 2
    frequency = THETA ** (-(jnp.arange(halfway, dtype=wide) * 2.0 / head_width))
    angles = places.astype(wide)[:, None] * frequency[None, :]
    cosine, sine = jnp.cos(angles), jnp.sin(angles)
    turns = [
        (jnp.concatenate([cosine, cosine], axis=1), VMEM),
        (jnp.concatenate([-sine, sine], axis=1), VMEM),
        (query_gain[None, :], VMEM),
        (key_gain[None, :], VMEM),
    ]
    both = 2 * length
    raw, router_rows, rest_rows = call(
        raw_kernel,
        "attention_raw",
        [(weight_ids, SMEM), (block_ids, SMEM)]
        + [(b, FAR) for b in sequence]
        + [(b, HBM) for b in blocks],
        [
            shape(both, raw_cols, wide),
            shape(model_width, 128, low),
            shape(model_width, 128, low),
        ],
        [
            pltpu.VMEM((model_width, raw_cols + 128), low),
            pltpu.VMEM((both, model_width), low),
            copies_sem(20),
        ],
        2 * both * model_width * raw_cols,
        alone=True,
    )
    chain.add(raw)
    chain.gather([(out_held, SHORT_ROUNDS[2])])
    (attended,) = call(
        functools.partial(forward_kernel, head_count),
        "attention_forward",
        [(core_id, SMEM), (raw, VMEM)] + turns,
        [shape(both, query_cols, low)],
        [],
        4 * both * length * query_cols,
    )
    chain.add(attended)
    chain.gather([(out_held, SHORT_ROUNDS[3])])
    out_blocks = [out_held[b] for b in BLOCKS]
    chain.gather([(cot_held, TOKEN_ROUNDS[0])])
    sent, kept = call(
        out_kernel,
        "attention_out",
        [(weight_ids, SMEM), (attended, VMEM)] + [(b, HBM) for b in out_blocks],
        [shape(length, model_width, low), shape(length, model_width, wide)],
        [pltpu.VMEM((query_cols, model_width), low), copies_sem(16)],
        2 * both * model_width * query_cols,
    )

    pair_total = kept + core_swap(sent).astype(wide)
    leaving = pair_total[tok_rows:].astype(low)
    from_pair = z_pair(leaving)
    chain.add(leaving)
    chain.gather([(cot_held, TOKEN_ROUNDS[1])])
    chain.gather([(cot_held, TOKEN_ROUNDS[2])])
    hidden = inputs_float + pair_total[:tok_rows] + from_pair.astype(wide)
    normed_experts, experts_back = jax.vjp(rms_scale, hidden, feedforward_gain)
    moe_in = normed_experts.astype(low)
    chain.add(moe_in)

    token_held = {(0, 0, 0): moe_in}
    chain.gather([(token_held, TOKEN_ROUNDS[0])])
    chain.gather([(token_held, TOKEN_ROUNDS[1])])
    slot_rows = 4 * capacity
    quad_rows = 4 * tok_rows
    rows_of = 2 * slot_rows
    all_slots = 4 * rows_of
    experts = jnp.stack([place * 2 + core, place * 2 + 1 - core]).astype(jnp.int32)
    w_gate, w_up, w_down = gate_weight[0], up_weight[0], down_weight[0]
    turned_width = -(-rows_of // 128) * 128
    picks, turned_picks = call(
        functools.partial(map_kernel, capacity, expert_count),
        "pick_maps",
        [(experts, SMEM), (rest_rows, VMEM)],
        [shape(all_slots, quad_rows, low), shape(model_width, turned_width, low)],
        [],
        2 * 128 * 128 * model_width,
    )

    logits = jnp.dot(moe_in, router_rows, preferred_element_type=wide)[:, :expert_count]
    lifted = jnp.where(own_named, logits, -1e30)
    lifted = jnp.where(own_named, jnp.exp(lifted - jnp.max(lifted, axis=1, keepdims=True)), 0.0)
    gate_dense = lifted / jnp.sum(lifted, axis=1, keepdims=True)

    full = 2 * model_width + 128

    def pick_tokens(k, *earlier):
        return call(
            functools.partial(pick_kernel, k),
            "picks",
            [(after(picks, *earlier), FAR), (rest_rows, FAR)]
            + [(token_held[k, dy, dx], FAR) for dy, dx in PLANE]
            + [(cot_held[k, dy, dx], HBM) for dy, dx in PLANE],
            [shape(slot_rows, full, low)] * 2,
            [
                pltpu.VMEM((rows_of, quad_rows), low),
                pltpu.VMEM((quad_rows, full), low),
                copies_sem(10),
            ],
            2 * rows_of * quad_rows * full,
            alone=k == 0,
        )

    stores = []

    def run_experts(k, own, back):
        ins = (
            [(experts, SMEM), (router_rows, VMEM), (own, FAR), (back, FAR)]
            + [(w, HBM) for w in (w_gate, w_up, w_down)]
        )
        made = call(
            functools.partial(expert_kernel, expert_count, k),
            "experts",
            ins + [(store, HBM) for store in stores],
            [
                shape(all_slots, model_width, low),
                shape(all_slots, hidden_width, low),
                shape(all_slots, model_width, low),
                shape(all_slots, hidden_width, low),
                shape(all_slots, hidden_width, low),
                shape(slot_rows, full, low),
                shape(slot_rows, full, low),
            ],
            [
                pltpu.VMEM((rows_of, full), low),
                pltpu.VMEM((model_width, hidden_width), low),
                pltpu.VMEM((model_width, hidden_width), low),
                pltpu.VMEM((hidden_width, model_width), low),
                pltpu.VMEM((rows_of, hidden_width), low),
                pltpu.VMEM((rows_of, model_width), low),
                pltpu.VMEM((rows_of, hidden_width), low),
                pltpu.VMEM((rows_of, hidden_width), low),
                pltpu.VMEM((rows_of, hidden_width), wide),
                pltpu.VMEM((rows_of, hidden_width), wide),
                pltpu.VMEM((rows_of, hidden_width), wide),
                copies_sem(10),
            ],
            12 * rows_of * model_width * hidden_width,
            [HBM] * 5 + [VMEM] * 2,
            {len(ins) + i: i for i in range(len(stores))},
        )
        stores[:] = made[:5]
        return made[5:]

    terms, y_terms = {b: [] for b in BLOCKS}, {}

    def sum_tokens(k, own, back):
        made = call(
            functools.partial(token_sum_kernel, k),
            "token_sums",
            [(turned_picks, FAR), (own, FAR), (back, FAR)],
            [shape(tok_rows, model_width + 128, low)] * 4 + [shape(tok_rows, model_width, low)] * 4,
            [
                pltpu.VMEM((quad_rows, turned_width), low),
                pltpu.VMEM((rows_of, full), low),
                pltpu.VMEM((quad_rows, model_width), low),
                copies_sem(7),
            ],
            2 * rows_of * quad_rows * full,
            [VMEM] * 4 + [HBM] * 4,
        )
        for i, p in enumerate(PLANE):
            terms[(k, *p)].append(made[i])
            y_terms[(k, *p)] = [made[4 + i]]
        return made[0]

    def row_product(left, right, *earlier):
        return lax.dot_general(after(left, *earlier), right, TN, preferred_element_type=wide)[None]

    own, other = pick_tokens(0)
    chain.add(other)
    (back,) = chain.gather([(token_held, TOKEN_ROUNDS[2])], [(other, core_swap)])
    own, sent = run_experts(0, own, back)
    chain.add(sent)
    (back,) = chain.gather([(token_held, TOKEN_ROUNDS[3])], [(sent, core_swap)])
    summed = sum_tokens(0, own, back)
    chain.gather([(cot_held, TOKEN_ROUNDS[3])])
    own, other = pick_tokens(1, summed)
    (back,) = chain.gather([(token_held, TOKEN_ROUNDS[4])], [(other, core_swap)])
    own, sent = run_experts(1, own, back)
    chain.add(own)
    chain.gather([(cot_held, TOKEN_ROUNDS[4])])
    own_two, other_two = pick_tokens(2, sent)
    back, back_two = chain.send([sent, other_two], [core_swap] * 2)
    sum_tokens(1, own, back)
    chain.scatter([(terms, RETURN_ROUNDS[0])])
    own, sent = run_experts(2, own_two, after(back_two, *chain.values))
    own_three, other_three = pick_tokens(3, sent)
    back, back_three = chain.send([sent, other_three], [core_swap] * 2)
    sum_tokens(2, own, back)
    chain.scatter([(terms, RETURN_ROUNDS[1])])
    own, sent = run_experts(3, own_three, back_three)
    all_rows, all_act, all_grads, all_gate, all_up = stores
    (back,) = chain.send([sent], [core_swap])
    sum_tokens(3, own, back)
    weight_grads = []
    for moves, pair in zip(
        RETURN_ROUNDS[2:], ((all_act, all_grads), (all_rows, all_gate), (all_rows, all_up))
    ):
        chain.scatter([(terms, moves)])
        weight_grads.append(row_product(*pair, *chain.values))
        chain.add(weight_grads[-1])
    grad_down, grad_gate, grad_up = weight_grads

    summed = plus(*terms[0, 0, 0])
    gate_parts = summed[:, model_width:]
    grad_gates = gate_parts[:, :expert_count] + gate_parts[:, expert_count : 2 * expert_count]
    grad_logits = gate_dense * (
        grad_gates - jnp.sum(gate_dense * grad_gates, axis=1, keepdims=True)
    )
    router_wide = router_rows[:, :expert_count].astype(wide)
    grad_moe_in = summed[:, :model_width] + jnp.einsum(
        "te,de->td", grad_logits, router_wide, precision=HIGH
    )

    grad_hidden_norm, grad_feed_gain = experts_back(grad_moe_in)
    grad_hidden = grad_output + grad_hidden_norm
    grad_own = grad_hidden.astype(low)
    chain.scatter([(y_terms, OUTPUT_ROUNDS[0])])
    chain.add(grad_own)
    far, swapped = chain.scatter(
        [(y_terms, OUTPUT_ROUNDS[1])], [(grad_own, z_pair), (grad_own, core_swap)]
    )

    grad_router = jnp.einsum(
        "td,te->ed", moe_in.astype(wide), after(grad_logits, grad_own), precision=HIGH
    )
    (far_swapped,) = chain.scatter([(y_terms, OUTPUT_ROUNDS[2])], [(far, core_swap)])
    grad_branch = [grad_own, swapped, far, far_swapped]

    def block_products(left_blocks, right, rest, name):
        width = right.shape[1] + (0 if rest is None else 128)
        return call(
            functools.partial(block_product_kernel, rest is not None),
            name,
            [(weight_ids, SMEM), (right, VMEM)]
            + [(b, FAR) for b in left_blocks]
            + ([] if rest is None else [(rest, VMEM)]),
            [shape(tok_rows, width, low)] * 16,
            [pltpu.VMEM((both, model_width), low), copies_sem(4)],
            2 * both * model_width * right.shape[1],
        )

    out_products = block_products(grad_branch, attended, None, "out_weight_grad")
    out_terms = {b: [block] for b, block in zip(BLOCKS, out_products)}
    chain.add(out_products[0])
    (router_part,) = chain.scatter(
        [(y_terms, OUTPUT_ROUNDS[3]), (out_terms, WEIGHT_RETURNS[0])],
        [(grad_router, core_swap)],
        out_products[0],
    )
    grad_router = grad_router + router_part
    (grad_attended,) = call(
        attended_grad_kernel,
        "attended_grad",
        [(weight_ids, SMEM)]
        + [(b, FAR) for b in (after(grad_branch[0], out_products[0]), *grad_branch[1:])]
        + [(b, HBM) for b in out_blocks],
        [shape(both, query_cols, low)],
        [
            pltpu.VMEM((both, model_width), low),
            pltpu.VMEM((query_cols, model_width), low),
            copies_sem(20),
        ],
        2 * both * model_width * query_cols,
    )
    chain.add(grad_attended)
    (router_part,) = chain.scatter(
        [(out_terms, WEIGHT_RETURNS[1]), (y_terms, OUTPUT_ROUNDS[4])], [(grad_router, z_pair)]
    )
    grad_rest = jnp.pad(grad_router + router_part, ((0, 128 - expert_count), (0, 0)))
    grad_raw, query_gain_grad, key_gain_grad = call(
        functools.partial(backward_kernel, head_count),
        "attention_backward",
        [(core_id, SMEM), (raw, VMEM), (after(grad_attended, *chain.values), VMEM)] + turns,
        [shape(both, raw_cols, low), shape(1, head_width, wide), shape(1, head_width, wide)],
        [pltpu.VMEM((length, head_width), wide), pltpu.VMEM((length, head_width), wide)],
        10 * both * length * query_cols,
    )
    chain.add(grad_raw)
    chain.scatter([(out_terms, WEIGHT_RETURNS[2])])
    raw_products = block_products(
        sequence, after(grad_raw, *chain.values), grad_rest, "raw_weight_grad"
    )
    raw_terms = {b: [block] for b, block in zip(BLOCKS, raw_products)}
    chain.add(raw_products[0])
    chain.scatter([(raw_terms, WEIGHT_RETURNS[0]), (y_terms, OUTPUT_ROUNDS[5])])
    sent, kept, attention_part = call(
        normed_grad_kernel,
        "normed_grad",
        [
            (weight_ids, SMEM),
            (after(grad_raw, *chain.values), VMEM),
            (attention_gain[None, :], VMEM),
        ]
        + [(b, FAR) for b in sequence]
        + [(b, HBM) for b in blocks],
        [
            shape(length, model_width, low),
            shape(length, model_width, wide),
            shape(1, model_width, wide),
        ],
        [
            pltpu.VMEM((model_width, raw_cols + 128), low),
            pltpu.VMEM((both, model_width), low),
            copies_sem(20),
        ],
        2 * both * model_width * raw_cols,
    )
    chain.add(kept)
    gains = jnp.concatenate(
        [attention_part[0], grad_feed_gain, query_gain_grad[0], key_gain_grad[0]]
    ).reshape(-1, head_width)
    gains = gains + core_swap(gains)
    (from_core,) = chain.scatter([(out_terms, WEIGHT_RETURNS[3])], [(sent, core_swap)])
    pair_total = kept + from_core.astype(wide)
    from_pair, gain_part = chain.scatter(
        [(raw_terms, WEIGHT_RETURNS[1])],
        [(pair_total[tok_rows:].astype(low), z_pair), (gains, x_swap)],
    )
    gains = gains + gain_part
    (gain_part,) = chain.scatter([(raw_terms, WEIGHT_RETURNS[2])], [(gains, y_swap)])
    grad_normed = pair_total[:tok_rows] + from_pair.astype(wide)
    grad_inputs_norm, _ = attention_back(grad_normed)
    grad_inputs = grad_hidden + grad_inputs_norm
    chain.add(grad_inputs)
    gains = gains + gain_part
    (gain_part,) = chain.scatter([(raw_terms, WEIGHT_RETURNS[3])], [(gains, z_pair)])
    gains = gains + gain_part
    theirs = jnp.concatenate([plus(*t[1, 0, 0]).astype(low) for t in (out_terms, raw_terms)], axis=1)
    theirs, gain_part = chain.scatter(
        [(raw_terms, WEIGHT_RETURNS[4]), (out_terms, WEIGHT_RETURNS[4])],
        [(theirs, z_pair), (gains, z_far)],
    )
    out_theirs, raw_theirs = theirs[:, :query_cols], theirs[:, query_cols:]
    gains = (gains + gain_part).reshape(-1)
    output = (hidden + plus(*y_terms[0, 0, 0])).astype(low)
    grad_out_weight = in_order(plus(*out_terms[0, 0, 0]), out_theirs.astype(wide), 1).T
    mine, theirs = plus(*raw_terms[0, 0, 0]), raw_theirs.astype(wide)
    spans = ((0, query_cols), (query_cols, query_cols + key_cols), (query_cols + key_cols, raw_cols))
    grad_query_weight, grad_key_weight, grad_value_weight = [
        in_order(mine[:, a:b], theirs[:, a:b], 1) for a, b in spans
    ]
    router_share = mine[:, raw_cols : raw_cols + expert_count]
    return (
        output,
        grad_inputs,
        gains[:model_width],
        grad_query_weight,
        grad_key_weight,
        grad_value_weight,
        gains[2 * model_width : 2 * model_width + head_width],
        gains[2 * model_width + head_width :],
        grad_out_weight,
        gains[model_width : 2 * model_width],
        router_share,
        grad_gate,
        grad_up,
        grad_down,
    )


def solution(mesh):
    in_specs = (
        P(("dp", "tensor"), None),
        P(),
        P("dp", "tensor"),
        P("dp", "tensor"),
        P("dp", "tensor"),
        P(),
        P(),
        P("tensor", "dp"),
        P(),
        P("dp", None),
        P(("dp", "tensor"), None, None),
        P(("dp", "tensor"), None, None),
        P(("dp", "tensor"), None, None),
        P(("dp", "tensor"), None),
        P(("dp", "tensor"), None),
    )
    out_specs = (
        P(("dp", "tensor"), None),
        P(("dp", "tensor"), None),
        P(),
        P("dp", "tensor"),
        P("dp", "tensor"),
        P("dp", "tensor"),
        P(),
        P(),
        P("tensor", "dp"),
        P(),
        P("dp", None),
        P(("dp", "tensor"), None, None),
        P(("dp", "tensor"), None, None),
        P(("dp", "tensor"), None, None),
    )
    fits = mesh.shape["dp"] == 16 and mesh.shape["tensor"] == 2
    local = local_sixteen if fits else local_any
    return jax.shard_map(local, mesh=mesh, in_specs=in_specs, out_specs=out_specs, check_vma=False)
```

```python
import functools
import math

import jax
import jax.numpy as jnp
from jax import lax
from jax.experimental import pallas as pl
from jax.experimental.pallas import tpu as pltpu
from jax.sharding import PartitionSpec as P

EPS = 1e-06
THETA = 1000000.0
HIGH = lax.Precision.HIGHEST
block_limit = 512


def rms_scale(values, scales):
    inverse = lax.rsqrt(jnp.mean(values * values, axis=-1, keepdims=True) + EPS)
    return values * inverse * scales


def rope_tables(length, columns):
    halfway = columns // 2
    frequency = THETA ** (-(jnp.arange(halfway, dtype=jnp.float32) * 2.0 / columns))
    angles = jnp.arange(length, dtype=jnp.float32)[:, None] * frequency[None, :]
    return (jnp.cos(angles), jnp.sin(angles))


def head_prep(raw_rows, scales, cosine_table, sine_table):
    length = raw_rows.shape[0]
    columns = scales.shape[0]
    shaped = rms_scale(raw_rows.reshape(length, -1, columns), scales)
    halfway = columns // 2
    leading = shaped[..., :halfway]
    second = shaped[..., halfway:]
    cos_part = cosine_table[:, None, :]
    sin_part = sine_table[:, None, :]
    turned = jnp.concatenate(
        [leading * cos_part - second * sin_part, second * cos_part + leading * sin_part], axis=-1
    )
    return turned.reshape(length, -1)


def masked_scores(offset, block_rows, queries, key_rows, score_scale):
    scores = (
        jnp.einsum("qkgd,ckd->kgqc", queries, key_rows, preferred_element_type=jnp.float32)
        * score_scale
    )
    row_places = offset + jnp.arange(block_rows, dtype=jnp.int32)
    key_places = jnp.arange(key_rows.shape[0], dtype=jnp.int32)
    allowed = key_places[None, :] <= row_places[:, None]
    return (queries, jnp.where(allowed, scores, -1e30))


def slot_layout(routes, expert_count, capacity):
    flat_routes = routes.reshape(-1)
    onehot = (flat_routes[:, None] == jnp.arange(expert_count, dtype=jnp.int32)[None, :]).astype(
        jnp.int32
    )
    position = jnp.sum((jnp.cumsum(onehot, axis=0) - onehot) * onehot, axis=1)
    return flat_routes * capacity + position


def route_rows(buffer):
    return lax.all_to_all(buffer, ("dp", "tensor"), split_axis=0, concat_axis=0, tiled=True)


def local_any(
    inputs,
    attention_gain,
    query_weight,
    key_weight,
    value_weight,
    query_gain,
    key_gain,
    out_weight,
    feedforward_gain,
    router_weight,
    gate_weight,
    up_weight,
    down_weight,
    routes,
    cotangent,
):
    tok_rows, model_width = inputs.shape
    head_width = query_gain.shape[0]
    top_count = routes.shape[1]
    expert_count = router_weight.shape[1]
    local_experts = gate_weight.shape[0]
    capacity = tok_rows * top_count * 11 // (expert_count * 8)
    full_query, full_key, full_value, full_out, full_router = (
        lax.all_gather(query_weight, "dp", axis=0, tiled=True),
        lax.all_gather(key_weight, "dp", axis=0, tiled=True),
        lax.all_gather(value_weight, "dp", axis=0, tiled=True),
        lax.all_gather(out_weight, "dp", axis=1, tiled=True),
        lax.all_gather(router_weight, "dp", axis=0, tiled=True),
    )
    inputs_float = inputs.astype(jnp.float32)
    normed_attention, attention_back = jax.vjp(rms_scale, inputs_float, attention_gain)
    sequence = lax.all_gather(normed_attention.astype(jnp.bfloat16), "tensor", axis=0, tiled=True)
    length = sequence.shape[0]
    query_raw = jnp.dot(sequence, full_query, preferred_element_type=jnp.float32)
    key_raw = jnp.dot(sequence, full_key, preferred_element_type=jnp.float32)
    value_raw = jnp.dot(sequence, full_value, preferred_element_type=jnp.float32)
    cosine_table, sine_table = rope_tables(length, head_width)

    def prepare(raw_rows, scales):
        return head_prep(raw_rows, scales, cosine_table, sine_table)

    query_ready, query_back = jax.vjp(prepare, query_raw, query_gain)
    key_ready, key_back = jax.vjp(prepare, key_raw, key_gain)
    kv_heads = key_raw.shape[1] // head_width
    group_size = query_raw.shape[1] // head_width // kv_heads
    queries = query_ready.astype(jnp.bfloat16).reshape(length, kv_heads, group_size, head_width)
    key_rows = key_ready.astype(jnp.bfloat16).reshape(length, kv_heads, head_width)
    value_rows = value_raw.astype(jnp.bfloat16).reshape(length, kv_heads, head_width)
    score_scale = head_width ** (-0.5)
    block_rows = min(block_limit, length)
    block_count = length // block_rows
    offsets = jnp.arange(block_count, dtype=jnp.int32) * block_rows

    def forward_block(offset):
        query_block, masked = masked_scores(offset, block_rows, queries, key_rows, score_scale)
        peak_value = jnp.max(masked, axis=-1, keepdims=True)
        exp_total = jnp.sum(jnp.exp(masked - peak_value), axis=-1, keepdims=True)
        log_total = peak_value + jnp.log(exp_total)
        soft_weights = jnp.exp(masked - log_total).astype(jnp.bfloat16)
        mixture = jnp.einsum(
            "kgqc,ckd->qkgd", soft_weights, value_rows, preferred_element_type=jnp.float32
        )
        return (mixture, log_total)

    mixed_blocks, log_totals = lax.map(forward_block, offsets)
    attended = mixed_blocks.reshape(length, -1).astype(jnp.bfloat16)
    branch = lax.psum_scatter(
        jnp.dot(attended, full_out, preferred_element_type=jnp.float32).astype(jnp.bfloat16),
        "tensor",
        scatter_dimension=0,
        tiled=True,
    ).astype(jnp.float32)
    hidden = inputs_float + branch
    normed_experts, experts_back = jax.vjp(rms_scale, hidden, feedforward_gain)
    moe_in = normed_experts.astype(jnp.bfloat16)
    logits = jnp.dot(moe_in, full_router, preferred_element_type=jnp.float32)
    onehot_routes = (
        routes[:, :, None] == jnp.arange(expert_count, dtype=jnp.int32)[None, None, :]
    ).astype(jnp.float32)
    chosen = jnp.einsum("tke,te->tk", onehot_routes, logits, precision=HIGH)
    gate_values = jax.nn.softmax(chosen, axis=-1)
    slots = slot_layout(routes, expert_count, capacity)
    buffer_shape = (expert_count // local_experts, local_experts, capacity, model_width)
    dispatch = (
        jnp.zeros((expert_count * capacity, model_width), jnp.bfloat16)
        .at[slots]
        .set(jnp.repeat(moe_in, top_count, axis=0))
    )
    received = route_rows(dispatch.reshape(buffer_shape))
    gate_pre = jnp.einsum(
        "secd,edf->secf", received, gate_weight, preferred_element_type=jnp.float32
    )
    up_pre = jnp.einsum("secd,edf->secf", received, up_weight, preferred_element_type=jnp.float32)
    sigmoid_gate = jax.nn.sigmoid(gate_pre)
    silu_gate = gate_pre * sigmoid_gate
    activated = (silu_gate * up_pre).astype(jnp.bfloat16)
    expert_out = jnp.einsum(
        "secf,efd->secd", activated, down_weight, preferred_element_type=jnp.float32
    ).astype(jnp.bfloat16)
    returned = route_rows(expert_out).reshape(expert_count * capacity, model_width)
    picked = returned[slots].reshape(tok_rows, top_count, model_width).astype(jnp.float32)
    mixture_out = jnp.sum(gate_values[:, :, None] * picked, axis=1)
    output = (hidden + mixture_out).astype(jnp.bfloat16)
    grad_output = cotangent.astype(jnp.float32)
    grad_gates = jnp.sum(picked * grad_output[:, None, :], axis=2)
    grad_picks = (
        (gate_values[:, :, None] * grad_output[:, None, :])
        .astype(jnp.bfloat16)
        .reshape(-1, model_width)
    )
    grad_dispatch = (
        jnp.zeros((expert_count * capacity, model_width), jnp.bfloat16).at[slots].set(grad_picks)
    )
    grad_received = route_rows(grad_dispatch.reshape(buffer_shape))
    grad_act = jnp.einsum(
        "secd,efd->secf", grad_received, down_weight, preferred_element_type=jnp.float32
    )
    grad_down = jnp.einsum(
        "secf,secd->efd", activated, grad_received, preferred_element_type=jnp.float32
    )
    grad_gate_pre = (
        grad_act * up_pre * sigmoid_gate * (1.0 + gate_pre * (1.0 - sigmoid_gate))
    ).astype(jnp.bfloat16)
    grad_up_pre = (grad_act * silu_gate).astype(jnp.bfloat16)
    grad_gate = jnp.einsum(
        "secd,secf->edf", received, grad_gate_pre, preferred_element_type=jnp.float32
    )
    grad_up = jnp.einsum(
        "secd,secf->edf", received, grad_up_pre, preferred_element_type=jnp.float32
    )
    grad_sent = jnp.einsum(
        "secf,edf->secd", grad_gate_pre, gate_weight, preferred_element_type=jnp.float32
    )
    grad_sent = (
        grad_sent
        + jnp.einsum("secf,edf->secd", grad_up_pre, up_weight, preferred_element_type=jnp.float32)
    ).astype(jnp.bfloat16)
    grad_back = route_rows(grad_sent).reshape(expert_count * capacity, model_width)
    grad_moe_in = jnp.sum(
        grad_back[slots].reshape(tok_rows, top_count, model_width).astype(jnp.float32), axis=1
    )
    grad_chosen = gate_values * (
        grad_gates - jnp.sum(gate_values * grad_gates, axis=1, keepdims=True)
    )
    grad_logits = jnp.einsum("tk,tke->te", grad_chosen, onehot_routes, precision=HIGH)
    router_float = full_router.astype(jnp.float32)
    grad_moe_in = grad_moe_in + jnp.einsum("te,de->td", grad_logits, router_float, precision=HIGH)
    grad_router = jnp.einsum("td,te->de", moe_in.astype(jnp.float32), grad_logits, precision=HIGH)
    grad_hidden_norm, grad_experts_gain = experts_back(grad_moe_in)
    grad_hidden = grad_output + grad_hidden_norm
    grad_branch = lax.all_gather(grad_hidden.astype(jnp.bfloat16), "tensor", axis=0, tiled=True)
    grad_attended = jnp.einsum(
        "td,ad->ta", grad_branch, full_out, preferred_element_type=jnp.float32
    ).astype(jnp.bfloat16)
    grad_blocks = grad_attended.reshape(block_count, block_rows, kv_heads, group_size, head_width)

    def backward_block(carry, item):
        key_sum, value_sum = carry
        offset, log_total, grad_block = item
        query_block, masked = masked_scores(offset, block_rows, queries, key_rows, score_scale)
        soft_weights = jnp.exp(masked - log_total)
        soft_low = soft_weights.astype(jnp.bfloat16)
        grad_soft = jnp.einsum(
            "qkgd,ckd->kgqc", grad_block, value_rows, preferred_element_type=jnp.float32
        )
        inner_sum = jnp.sum(soft_weights * grad_soft, axis=-1, keepdims=True)
        grad_scores = (soft_weights * (grad_soft - inner_sum)).astype(jnp.bfloat16)
        grad_query_block = (
            jnp.einsum("kgqc,ckd->qkgd", grad_scores, key_rows, preferred_element_type=jnp.float32)
            * score_scale
        )
        key_sum = (
            key_sum
            + jnp.einsum(
                "kgqc,qkgd->ckd", grad_scores, query_block, preferred_element_type=jnp.float32
            )
            * score_scale
        )
        value_sum = value_sum + jnp.einsum(
            "kgqc,qkgd->ckd", soft_low, grad_block, preferred_element_type=jnp.float32
        )
        return ((key_sum, value_sum), grad_query_block)

    zero_rows = jnp.zeros((length, kv_heads, head_width), jnp.float32)
    (key_sum, value_sum), grad_query_blocks = lax.scan(
        backward_block, (zero_rows, zero_rows), (offsets, log_totals, grad_blocks)
    )
    grad_query_raw, grad_query_gain = query_back(grad_query_blocks.reshape(length, -1))
    grad_key_raw, grad_key_gain = key_back(key_sum.reshape(length, -1))
    grad_query_low = grad_query_raw.astype(jnp.bfloat16)
    grad_key_low = grad_key_raw.astype(jnp.bfloat16)
    grad_value_low = value_sum.reshape(length, -1).astype(jnp.bfloat16)
    total = jnp.einsum("tc,dc->td", grad_query_low, full_query, preferred_element_type=jnp.float32)
    total = total + jnp.einsum(
        "tc,dc->td", grad_key_low, full_key, preferred_element_type=jnp.float32
    )
    grad_sequence = lax.psum_scatter(
        (
            total
            + jnp.einsum(
                "tc,dc->td", grad_value_low, full_value, preferred_element_type=jnp.float32
            )
        ).astype(jnp.bfloat16),
        "tensor",
        scatter_dimension=0,
        tiled=True,
    ).astype(jnp.float32)
    grad_inputs_norm, grad_attention_gain = attention_back(grad_sequence)
    grad_inputs = grad_hidden + grad_inputs_norm
    query_cols = grad_query_low.shape[1]
    key_cols = grad_key_low.shape[1]
    grad_raw_all = jnp.concatenate([grad_query_low, grad_key_low, grad_value_low], axis=1)
    inward = jnp.einsum("td,tc->dc", sequence, grad_raw_all, preferred_element_type=jnp.float32)
    outward = jnp.einsum("td,ta->da", grad_branch, attended, preferred_element_type=jnp.float32)
    owned = lax.psum_scatter(
        jnp.concatenate([inward, outward], axis=1), "dp", scatter_dimension=0, tiled=True
    )
    grad_query_weight = owned[:, :query_cols]
    grad_key_weight = owned[:, query_cols : query_cols + key_cols]
    grad_value_weight = owned[:, query_cols + key_cols : query_cols + 2 * key_cols]
    grad_out_weight = owned[:, query_cols + 2 * key_cols :].T
    router_total, attention_total, query_total, key_total, experts_total = lax.psum(
        (grad_router, grad_attention_gain, grad_query_gain, grad_key_gain, grad_experts_gain),
        ("dp", "tensor"),
    )
    router_rows = router_weight.shape[0]
    router_share = lax.dynamic_slice_in_dim(
        router_total, lax.axis_index("dp") * router_rows, router_rows, 0
    )
    return (
        output,
        grad_inputs,
        attention_total,
        grad_query_weight,
        grad_key_weight,
        grad_value_weight,
        query_total,
        key_total,
        grad_out_weight,
        experts_total,
        router_share,
        grad_gate,
        grad_up,
        grad_down,
    )


low, wide = jnp.bfloat16, jnp.float32
Z_RING = tuple((i, (i + 4) % 16) for i in range(16))
Z_PAIR = tuple((i, i ^ 4) for i in range(16))
Z_FAR = tuple((i, i ^ 8) for i in range(16))
Y_PAIR = tuple((i, i ^ 2) for i in range(16))
X_PAIR = tuple((i, i ^ 1) for i in range(16))
BLOCKS = tuple((k, dy, dx) for k in range(4) for dy in range(2) for dx in range(2))
PLANE = tuple((dy, dx) for dy in range(2) for dx in range(2))
OVER_X = (1, 2)
ROOM = 8 * 2**20
WHOLE = 60 * 2**20
TILE = 256
WIDE = 512
HIDDEN_TILE = 768
NT = (((1,), (1,)), ((), ()))
TN = (((0,), (0,)), ((), ()))


def z_next(block):
    return lax.ppermute(block, "dp", Z_RING)


def z_pair(block):
    return lax.ppermute(block, "dp", Z_PAIR)


def z_far(block):
    return lax.ppermute(block, "dp", Z_FAR)


def y_swap(block):
    return lax.ppermute(block, "dp", Y_PAIR)


def x_swap(block):
    return lax.ppermute(block, "dp", X_PAIR)


def core_swap(block):
    return lax.ppermute(block, "tensor", ((0, 1), (1, 0)))


def after(value, *earlier):
    return lax.optimization_barrier((value, *earlier))[0]


def part(term):
    return term[0][term[1]] if isinstance(term, tuple) else term


def plus(*terms):
    total = part(terms[0]).astype(wide)
    for other in terms[1:]:
        total = total + part(other).astype(wide)
    return total


TOKEN_ROUNDS = (
    (((0, 0, 0), (0, 0, 1), x_swap), ((0, 0, 0), (0, 1, 0), y_swap), ((0, 0, 0), (1, 0, 0), z_next)),
    (((1, 0, 0), (1, 0, 1), x_swap), ((0, 0, 1), (0, 1, 1), y_swap), ((1, 0, 0), (2, 0, 0), z_next)),
    (((2, 0, 0), (2, 0, 1), x_swap), ((1, 0, 0), (1, 1, 0), y_swap), ((2, 0, 0), (3, 0, 0), z_next)),
    (((3, 0, 0), (3, 0, 1), x_swap), ((2, 0, 0), (2, 1, 0), y_swap), ((0, 1, 1), (1, 1, 1), z_next)),
    (((2, 1, 0), (2, 1, 1), x_swap), ((3, 0, 1), (3, 1, 1), y_swap), ((2, 1, 0), (3, 1, 0), z_next)),
)
WEIGHT_ROUNDS = (
    (
        ((0, 0, 0), (0, 0, 1), x_swap),
        ((0, 0, 0), (0, 1, 0), y_swap),
        ((0, 0, 0), (2, 0, 0), z_far, True),
    ),
    (
        ((1, 0, 0), (1, 0, 1), x_swap),
        ((1, 0, 0), (1, 1, 0), y_swap),
        ((1, 0, 0), (3, 0, 0), z_far, True),
        ((0, 0, 1), (0, 1, 1), y_swap),
    ),
    (
        ((2, 0, 0), (2, 0, 1), x_swap),
        ((2, 0, 0), (2, 1, 0), y_swap),
        ((1, 1, 0), (1, 1, 1), x_swap),
    ),
    (
        ((3, 0, 0), (3, 1, 0), y_swap),
        ((3, 0, 0), (3, 0, 1), x_swap),
        ((2, 0, 1), (2, 1, 1), y_swap),
    ),
    (((3, 1, 0), (3, 1, 1), x_swap),),
)
SHORT_ROUNDS = (
    (*WEIGHT_ROUNDS[0][:2],),
    (((0, 0, 0), (2, 0, 0), z_far, True), *WEIGHT_ROUNDS[1][:2], WEIGHT_ROUNDS[1][3]),
    (((1, 0, 0), (3, 0, 0), z_far), *WEIGHT_ROUNDS[2]),
    (*WEIGHT_ROUNDS[3], ((1, 1, 1), (3, 1, 1), z_far)),
)
WEIGHT_RETURNS = (
    (((3, 1, 1), (3, 1, 0), x_swap),),
    (
        ((3, 1, 0), (3, 0, 0), y_swap),
        ((3, 0, 1), (3, 0, 0), x_swap),
        ((2, 1, 1), (2, 0, 1), y_swap),
    ),
    (
        ((3, 0, 0), (1, 0, 0), z_far),
        ((2, 0, 1), (2, 0, 0), x_swap),
        ((2, 1, 0), (2, 0, 0), y_swap),
        ((1, 1, 1), (1, 1, 0), x_swap),
    ),
    (
        ((2, 0, 0), (0, 0, 0), z_far),
        ((1, 1, 0), (1, 0, 0), y_swap),
        ((1, 0, 1), (1, 0, 0), x_swap),
        ((0, 1, 1), (0, 0, 1), y_swap),
    ),
    (((0, 0, 1), (0, 0, 0), x_swap), ((0, 1, 0), (0, 0, 0), y_swap)),
)


RETURN_ROUNDS = (
    (((1, 1, 1), (1, 0, 1), y_swap), ((0, 1, 1), (0, 1, 0), x_swap), ((1, 1, 0), (2, 1, 0), z_next)),
    (((1, 0, 1), (1, 0, 0), x_swap), ((2, 1, 1), (2, 0, 1), y_swap), ((2, 1, 0), (3, 1, 0), z_next)),
    (((2, 0, 1), (2, 0, 0), x_swap), ((3, 1, 1), (3, 0, 1), y_swap), ((1, 0, 0), (2, 0, 0), z_next)),
    (((3, 0, 1), (3, 0, 0), x_swap), ((3, 1, 0), (3, 0, 0), y_swap), ((2, 0, 0), (3, 0, 0), z_next)),
    (((0, 0, 1), (0, 0, 0), x_swap), ((0, 1, 0), (0, 0, 0), y_swap), ((3, 0, 0), (0, 0, 0), z_next)),
)
OUTPUT_ROUNDS = (
    (((3, 1, 1), (3, 1, 0), x_swap), ((1, 1, 1), (1, 0, 1), y_swap), ((1, 1, 0), (2, 1, 0), z_next)),
    (((1, 0, 1), (1, 0, 0), x_swap), ((2, 1, 1), (2, 0, 1), y_swap)),
    (((2, 0, 1), (2, 0, 0), x_swap), ((2, 1, 0), (2, 0, 0), y_swap), ((1, 0, 0), (2, 0, 0), z_next)),
    (((3, 0, 1), (3, 0, 0), x_swap), ((3, 1, 0), (3, 0, 0), y_swap), ((2, 0, 0), (3, 0, 0), z_next)),
    (((0, 1, 1), (0, 1, 0), x_swap),),
    (((0, 0, 1), (0, 0, 0), x_swap), ((0, 1, 0), (0, 0, 0), y_swap), ((3, 0, 0), (0, 0, 0), z_next)),
)


class Chain:
    def __init__(self):
        self.earlier = []
        self.late = []
        self.values = []

    def add(self, *values):
        self.earlier.extend(values)

    def send(self, values, ways, late=()):
        values = lax.optimization_barrier((*values, *self.earlier))[: len(values)]
        self.values = values
        results = [way(value) for value, way in zip(values, ways)]
        self.earlier = self.late + [r for i, r in enumerate(results) if i not in late]
        self.late = [results[i] for i in late]
        return results

    def round(self, values, moves, others):
        late = [i for i, move in enumerate(moves) if len(move) > 3]
        values = values + [value for value, _ in others]
        ways = [move[2] for move in moves] + [way for _, way in others]
        results = self.send(values, ways, late)
        return results[: len(moves)], results[len(moves) :]

    def gather(self, pairs, others=()):
        values = [held[move[0]] for held, moves in pairs for move in moves]
        moves = [move for _, moves in pairs for move in moves]
        results, rest = self.round(values, moves, others)
        for (held, end), result in zip([(h, m[1]) for h, ms in pairs for m in ms], results):
            held[end] = result
        return rest

    def scatter(self, pairs, others=(), later=None):
        if later is not None:
            for terms, moves in pairs:
                for move in moves:
                    last = terms[move[0]][-1]
                    held = isinstance(last, tuple)
                    gated = after(last[0] if held else last, later)
                    terms[move[0]][-1] = (gated, last[1]) if held else gated
        gathered = []
        for terms, moves in pairs:
            for move in moves:
                same = [g for g in gathered if g[0] is terms and g[1] is move[2] and len(g[2]) == 1]
                if same and terms[move[0]][0].shape[-1] < 2000:
                    same[0][2].append(move)
                else:
                    gathered.append((terms, move[2], [move]))
        groups = [[terms[move[0]] for move in moves] for terms, _, moves in gathered]
        values = totals(groups)
        results, rest = self.round(values, [moves[0] for _, _, moves in gathered], others)
        for (terms, _, moves), result in zip(gathered, results):
            for index, move in enumerate(moves):
                terms[move[1]].append((result, index) if len(moves) == 2 else result)
        return rest


def sum_kernel(groups, *refs):
    outs = refs[sum(sum(group) for group in groups) :]
    for group, out in zip(groups, outs):
        for index, count in enumerate(group):
            terms, refs = refs[:count], refs[count:]
            total = terms[0][...].astype(wide)
            for term in terms[1:]:
                total = total + term[...].astype(wide)
            if len(group) == 1:
                out[...] = total.astype(out.dtype)
            else:
                out[index] = total.astype(out.dtype)


def totals(groups):
    made = [g for g in groups if len(g) > 1 or len(g[0]) > 1 or isinstance(g[0][0], tuple)]
    if not made:
        return [g[0][0] for g in groups]
    operands, in_specs, out_shape, out_specs = [], [], [], []
    for group in made:
        for terms in group:
            for term in terms:
                array, index = term if isinstance(term, tuple) else (term, None)
                rows, columns = array.shape[-2] // 4, array.shape[-1]
                operands.append(array)
                if index is None:
                    in_specs.append(pl.BlockSpec((rows, columns), lambda i: (i, 0)))
                else:
                    in_specs.append(
                        pl.BlockSpec((None, rows, columns), lambda i, index=index: (index, i, 0))
                    )
        if len(group) == 1:
            out_shape.append(jax.ShapeDtypeStruct((4 * rows, columns), low))
            out_specs.append(pl.BlockSpec((rows, columns), lambda i: (i, 0)))
        else:
            out_shape.append(jax.ShapeDtypeStruct((2, 4 * rows, columns), low))
            out_specs.append(pl.BlockSpec((2, rows, columns), lambda i: (0, i, 0)))
    sums = pl.pallas_call(
        functools.partial(sum_kernel, [[len(terms) for terms in group] for group in made]),
        grid=(4,),
        out_shape=out_shape,
        in_specs=in_specs,
        out_specs=out_specs,
        name="sums",
        compiler_params=pltpu.CompilerParams(vmem_limit_bytes=2 * ROOM),
    )(*operands)
    sums = list(sums)
    return [sums.pop(0) if any(g is m for m in made) else g[0][0] for g in groups]


def dot(left, right, dims=None):
    if dims is None:
        return jnp.dot(left, right, preferred_element_type=wide)
    return lax.dot_general(left, right, dims, preferred_element_type=wide)


def lanes(start, size):
    return pl.ds(pl.multiple_of(start, 128), size)


def spot(ids, i):
    return pl.multiple_of(ids[i] * 128, 128)


def row_copies(ids, blocks, whole, sems):
    return [
        pltpu.make_async_copy(block, whole.at[pl.ds(spot(ids, i), 128), :], sems.at[i])
        for i, block in enumerate(blocks)
    ]


def column_copies(ids, blocks, whole, sems):
    return [
        pltpu.make_async_copy(block, whole.at[:, pl.ds(spot(ids, i), 128)], sems.at[i])
        for i, block in enumerate(blocks)
    ]


def stack_copies(blocks, whole, sems):
    rows = blocks[0].shape[0]
    return [
        pltpu.make_async_copy(block, whole.at[pl.ds(i * rows, rows), :], sems.at[i])
        for i, block in enumerate(blocks)
    ]


def start_all(copies):
    for copy in copies:
        copy.start()


def wait_all(copies):
    for copy in copies:
        copy.wait()


def head_forward(raw, gain, cosine, sine):
    inverse = lax.rsqrt(jnp.mean(raw * raw, axis=-1, keepdims=True) + EPS)
    unit = raw * inverse
    shaped = unit * gain
    return unit, inverse, shaped * cosine + pltpu.roll(shaped, 64, 1) * sine


def head_backward(grad, unit, inverse, gain, cosine, sine):
    back = grad * cosine - pltpu.roll(grad, 64, 1) * sine
    gain_grad = jnp.sum(back * unit, axis=0, keepdims=True)
    scaled = back * gain
    return gain_grad, inverse * (scaled - unit * jnp.mean(scaled * unit, axis=-1, keepdims=True))


def causal(core, length):
    half = length // 2
    rows = lax.broadcasted_iota(jnp.int32, (length, length), 0)
    columns = lax.broadcasted_iota(jnp.int32, (length, length), 1)

    def place(i):
        return jnp.where(i < half, i + core * half, i - half + (1 - core) * half)

    return place(columns) <= place(rows)


def soft(query, key, allowed, scale):
    scores = jnp.where(allowed, dot(query, key, NT) * scale, -1e30)
    raised = jnp.exp(scores - jnp.max(scores, axis=-1, keepdims=True))
    return raised / jnp.sum(raised, axis=-1, keepdims=True)


def first_blocks_kernel(odd, routes, query, key, value, router, mine, theirs, rest):
    count = router.shape[1]
    columns = lax.broadcasted_iota(jnp.int32, rest.shape, 1)
    named = columns == routes[:, :1] + count
    for j in range(1, routes.shape[1]):
        named = jnp.logical_or(named, columns == routes[:, j : j + 1] + count)
    rest[...] = jnp.where(named, 1.0, 0.0)
    rest[:, :count] = router[...].astype(wide)
    for out, side in ((mine, odd[0]), (theirs, 1 - odd[0])):
        first = 0
        for weight in (query, key, value):
            size = weight.shape[1] // 2
            out[:, first : first + size] = weight[:, lanes(side * size, size)]
            first += size
        out[:, first:] = rest[...].astype(low)


def raw_kernel(ids, block_ids, *refs):
    seq_blocks, blocks = refs[:4], refs[4:20]
    raw, router, rest, whole, seq, sems = refs[20:]
    copies = stack_copies(seq_blocks, seq, sems.at[pl.ds(16, 4)]) + row_copies(
        ids, blocks, whole, sems
    )
    start_all(copies)
    wait_all(copies)
    width = raw.shape[1]

    @pl.loop(0, width // TILE)
    def _(j):
        span = lanes(j * TILE, TILE)
        raw[:, span] = dot(seq[...], whole[:, span])

    router[...] = whole[:, width:]
    for p in range(16):
        rest[p * 128 : (p + 1) * 128, :] = whole[pl.ds(spot(block_ids, p), 128), width:]


def forward_kernel(head_count, core, raw, cosine, sine, query_gain, key_gain, attended):
    length = raw.shape[0] // 2
    key_start = head_count * 128
    allowed = causal(core[0], length)
    scale = 128 ** (-0.5)
    for s in range(2):
        span = slice(s * length, (s + 1) * length)
        turn = (cosine[...], sine[...])
        key_raw = raw[span, key_start : key_start + 128]
        key = head_forward(key_raw, key_gain[...], *turn)[2].astype(low)
        value = raw[span, key_start + 128 : key_start + 256].astype(low)

        @pl.loop(0, head_count, unroll=2)
        def _(h):
            columns = lanes(h * 128, 128)
            query = head_forward(raw[span, columns], query_gain[...], *turn)[2].astype(low)
            weights = soft(query, key, allowed, scale)
            attended[span, columns] = dot(weights.astype(low), value).astype(low)


def split_rows(product, span, sent, kept):
    rows = product.shape[0] // 4
    kept[:rows, span] = product[:rows]
    sent[:rows, span] = product[rows : 2 * rows].astype(low)
    kept[rows:, span] = product[2 * rows : 3 * rows]
    sent[rows:, span] = product[3 * rows :].astype(low)


def out_kernel(ids, attended, *refs):
    blocks, (sent, kept, whole, sems) = refs[:16], refs[16:]
    copies = column_copies(ids, blocks, whole, sems)
    start_all(copies)
    wait_all(copies)

    @pl.loop(0, whole.shape[1] // WIDE)
    def _(j):
        span = lanes(j * WIDE, WIDE)
        split_rows(dot(attended[...], whole[:, span]), span, sent, kept)


def normed_grad_kernel(ids, grad_raw, gain, *refs):
    seq_blocks, blocks = refs[:4], refs[4:20]
    sent, kept, gain_grad, whole, seq, sems = refs[20:]
    copies = row_copies(ids, blocks, whole, sems) + stack_copies(
        seq_blocks, seq, sems.at[pl.ds(16, 4)]
    )
    start_all(copies)
    wait_all(copies)
    width = grad_raw.shape[1]

    @pl.loop(0, whole.shape[0] // WIDE)
    def _(j):
        span = lanes(j * WIDE, WIDE)
        product = dot(grad_raw[...], whole[span, :width], NT)
        split_rows(product, span, sent, kept)
        unit = seq[:, span].astype(wide) / gain[:, span]
        gain_grad[:, span] = jnp.sum(product * unit, axis=0, keepdims=True)


def attended_grad_kernel(ids, *refs):
    grad_blocks, blocks = refs[:4], refs[4:20]
    grad_attended, grad_branch, whole, sems = refs[20:]
    copies = stack_copies(grad_blocks, grad_branch, sems.at[pl.ds(16, 4)]) + column_copies(
        ids, blocks, whole, sems
    )
    start_all(copies)
    wait_all(copies)

    @pl.loop(0, grad_attended.shape[1] // WIDE)
    def _(j):
        span = lanes(j * WIDE, WIDE)
        grad_attended[:, span] = dot(grad_branch[...], whole[span, :], NT).astype(low)


def map_kernel(capacity, expert_count, experts, named, picks, turned_picks):
    slot_rows = 4 * capacity
    early = lax.broadcasted_iota(jnp.int32, (128, 128), 0)
    late = lax.broadcasted_iota(jnp.int32, (128, 128), 1)
    before = jnp.where(early < late, 1.0, 0.0).astype(low)
    behind = jnp.where(late < early, 1.0, 0.0).astype(low)
    slot_numbers = lax.broadcasted_iota(jnp.int32, (slot_rows, 128), 0)
    slot_lanes = lax.broadcasted_iota(jnp.int32, (128, turned_picks.shape[1]), 1)
    for b in range(16):
        k, i = b // 4, b % 4
        block = named[b * 128 : (b + 1) * 128, :]
        turned_slots = []
        for c in range(2):
            column = experts[c] + expert_count
            own_lane = lax.broadcasted_iota(jnp.int32, (8, 128), 1) == column
            hit = dot(jnp.where(own_lane, 1.0, 0.0).astype(low), block, NT)
            slot = dot(hit.astype(low), before) + float(i * capacity)
            slot = jnp.where(hit > 0.5, slot, -1.0).astype(jnp.int32)
            first = (2 * k + c) * slot_rows
            picks[first : first + slot_rows, i * 128 : (i + 1) * 128] = jnp.where(
                slot_numbers == slot[:1], 1.0, 0.0
            ).astype(low)
            mine = jnp.where(late == column, block.astype(wide), 0.0)
            hit = jnp.sum(mine, axis=1, keepdims=True)
            slot = jnp.sum(dot(behind, mine.astype(low)), axis=1, keepdims=True)
            slot = slot + float(i * capacity + c * slot_rows)
            turned_slots.append(jnp.where(hit > 0.5, slot, -1.0).astype(jnp.int32))
        either = jnp.logical_or(slot_lanes == turned_slots[0], slot_lanes == turned_slots[1])
        turned_picks[b * 128 : (b + 1) * 128, :] = jnp.where(either, 1.0, 0.0).astype(low)


def pick_kernel(k, picks_in, named, *refs):
    tokens, cots, (own, other, picks, rows, sems) = refs[:4], refs[4:8], refs[8:]
    quad_rows, full = rows.shape
    width = tokens[0].shape[1]
    copies = (
        stack_copies(tokens, rows.at[:, pl.ds(0, width)], sems.at[pl.ds(0, 4)])
        + stack_copies(cots, rows.at[:, pl.ds(width + 128, width)], sems.at[pl.ds(4, 4)])
        + [
            pltpu.make_async_copy(
                picks_in.at[pl.ds(k * picks.shape[0], picks.shape[0]), :], picks, sems.at[8]
            ),
            pltpu.make_async_copy(
                named.at[pl.ds(k * quad_rows, quad_rows), :],
                rows.at[:, pl.ds(width, 128)],
                sems.at[9],
            ),
        ]
    )
    start_all(copies)
    wait_all(copies)
    slot_rows = own.shape[0]
    for start in range(0, full, WIDE):
        span = slice(start, min(start + WIDE, full))
        made = dot(picks[...], rows[:, span]).astype(low)
        own[:, span] = made[:slot_rows]
        other[:, span] = made[slot_rows:]


def expert_kernel(expert_count, k, experts, router, *refs):
    sides, weights = refs[:2], refs[2:5]
    refs = refs[5 + (5 if k else 0) :]
    (all_rows, all_act, all_grads, all_gate, all_up, own_out, back_out) = refs[:7]
    (rows, v_gate, v_up, v_down, act, grads, gate_back, up_back) = refs[7:15]
    (gate_pre, up_pre, sig, sems) = refs[15:]
    slot_rows = own_out.shape[0]
    width, hidden = v_gate.shape
    after_width = width + 128
    spans = [slice(c * slot_rows, (c + 1) * slot_rows) for c in range(2)]
    side_copies = stack_copies(sides, rows, sems.at[pl.ds(0, 2)])
    weight_copies = [
        pltpu.make_async_copy(a, b, sems.at[2 + i])
        for i, (a, b) in enumerate(zip(weights, (v_gate, v_up, v_down)))
    ]
    start_all(side_copies + weight_copies)
    kept = []

    def keep(source, target, sem):
        copy = pltpu.make_async_copy(
            source.at[:, pl.ds(0, target.shape[1])],
            target.at[pl.ds(k * 2 * slot_rows, 2 * slot_rows), :],
            sems.at[sem],
        )
        copy.start()
        kept.append(copy)

    wait_all(side_copies)
    keep(rows, all_rows, 5)
    logits = dot(rows[:, :width], router[...])
    numbers = lax.broadcasted_iota(jnp.int32, logits.shape, 1)
    is_named = pltpu.roll(rows[:, width:after_width].astype(wide), 128 - expert_count, 1)
    is_named = jnp.logical_and(is_named > 0.5, numbers < expert_count)
    lifted = jnp.where(is_named, logits, -1e30)
    lifted = jnp.where(
        is_named, jnp.exp(lifted - jnp.max(lifted, axis=1, keepdims=True)), 0.0
    )
    mine = jnp.sum(jnp.where(numbers == experts[0], lifted, 0.0), axis=1, keepdims=True)
    gates = mine / jnp.maximum(jnp.sum(lifted, axis=1, keepdims=True), 1e-30)
    wait_all(weight_copies[:2])
    pre = dot(rows[:, :width], v_gate[...])
    up = dot(rows[:, :width], v_up[...])
    s = jax.nn.sigmoid(pre)
    gate_pre[...] = pre
    up_pre[...] = up
    sig[...] = s
    act[...] = (pre * s * up).astype(low)
    keep(act, all_act, 6)
    wait_all(weight_copies[2:])
    slot_grads = jnp.zeros((2 * slot_rows, 1), wide)
    for j in range(width // WIDE):
        span = slice(j * WIDE, (j + 1) * WIDE)
        later = slice(after_width + j * WIDE, after_width + (j + 1) * WIDE)
        out = dot(act[...], v_down[:, span]).astype(low).astype(wide)
        cot = rows[:, later].astype(wide)
        grads[:, span] = (gates * cot).astype(low)
        scaled = (gates * out).astype(low)
        own_out[:, later] = scaled[spans[0]]
        back_out[:, later] = scaled[spans[1]]
        slot_grads = slot_grads + jnp.sum(cot * out, axis=1, keepdims=True)
    keep(grads, all_grads, 7)
    back = dot(grads[...], v_down[...], NT)
    pre, s = gate_pre[...], sig[...]
    gate_back[...] = (back * up_pre[...] * s * (1.0 + pre * (1.0 - s))).astype(low)
    up_back[...] = (back * (pre * s)).astype(low)
    keep(gate_back, all_gate, 8)
    keep(up_back, all_up, 9)
    for j in range(width // WIDE):
        span = slice(j * WIDE, (j + 1) * WIDE)
        back = dot(gate_back[...], v_gate[span, :], NT) + dot(up_back[...], v_up[span, :], NT)
        back = back.astype(low)
        own_out[:, span] = back[spans[0]]
        back_out[:, span] = back[spans[1]]
    high = slot_grads.astype(low).astype(wide)
    rest = jnp.where(numbers == experts[0] + expert_count, slot_grads - high, 0.0)
    parts = jnp.where(numbers == experts[0], high, rest).astype(low)
    own_out[:, width:after_width] = parts[spans[0]]
    back_out[:, width:after_width] = parts[spans[1]]
    wait_all(kept)


def token_sum_kernel(k, turned_picks, *refs):
    sides, blocks, outputs, (picks, rows, out_rows, sems) = refs[:2], refs[2:6], refs[6:10], refs[10:]
    quad_rows, width = out_rows.shape
    copies = stack_copies(sides, rows, sems.at[pl.ds(0, 2)]) + [
        pltpu.make_async_copy(
            turned_picks.at[pl.ds(k * quad_rows, quad_rows), :], picks, sems.at[2]
        )
    ]
    start_all(copies)
    wait_all(copies)
    slots = rows.shape[0]
    size, first = blocks[0].shape
    for j in range(0, width, WIDE):
        span = slice(j, j + WIDE)
        out_rows[:, span] = dot(picks[:, :slots], rows[:, first + j : first + j + WIDE]).astype(low)
    copies = [
        pltpu.make_async_copy(out_rows.at[pl.ds(i * size, size), :], output, sems.at[3 + i])
        for i, output in enumerate(outputs)
    ]
    start_all(copies)
    for j in range(0, first, WIDE):
        span = slice(j, min(j + WIDE, first))
        made = dot(picks[:, :slots], rows[:, span]).astype(low)
        for i, block in enumerate(blocks):
            block[:, span] = made[i * size : (i + 1) * size]
    wait_all(copies)


def backward_kernel(head_count, core, raw, grad_attended, *refs):
    cosine, sine, query_gain, key_gain = refs[:4]
    grad_raw, query_gain_grad, key_gain_grad, key_sum, value_sum = refs[4:]
    length = raw.shape[0] // 2
    key_start = head_count * 128
    allowed = causal(core[0], length)
    scale = 128 ** (-0.5)
    turn = (cosine[...], sine[...])
    query_gain_grad[...] = jnp.zeros_like(query_gain_grad)
    key_gain_grad[...] = jnp.zeros_like(key_gain_grad)
    for s in range(2):
        span = slice(s * length, (s + 1) * length)
        key_raw = raw[span, key_start : key_start + 128]
        key_unit, key_inverse, key = head_forward(key_raw, key_gain[...], *turn)
        key = key.astype(low)
        value = raw[span, key_start + 128 : key_start + 256].astype(low)
        key_sum[...] = jnp.zeros_like(key_sum)
        value_sum[...] = jnp.zeros_like(value_sum)

        @pl.loop(0, head_count, unroll=2)
        def _(h):
            columns = lanes(h * 128, 128)
            unit, inverse, query = head_forward(raw[span, columns], query_gain[...], *turn)
            query = query.astype(low)
            weights = soft(query, key, allowed, scale)
            grad = grad_attended[span, columns]
            grad_soft = dot(grad, value, NT)
            inner = jnp.sum(weights * grad_soft, axis=-1, keepdims=True)
            grad_scores = (weights * (grad_soft - inner)).astype(low)
            value_sum[...] += dot(weights.astype(low), grad, TN)
            key_sum[...] += dot(grad_scores, query, TN) * scale
            grad_query = dot(grad_scores, key) * scale
            gain_grad, back = head_backward(grad_query, unit, inverse, query_gain[...], *turn)
            query_gain_grad[...] += gain_grad
            grad_raw[span, columns] = back.astype(low)

        gain_grad, back = head_backward(
            key_sum[...], key_unit, key_inverse, key_gain[...], *turn
        )
        key_gain_grad[...] += gain_grad
        grad_raw[span, key_start : key_start + 128] = back.astype(low)
        grad_raw[span, key_start + 128 : key_start + 256] = value_sum[...].astype(low)


def block_product_kernel(with_rest, ids, right, *refs):
    left_blocks, refs = refs[:4], refs[4:]
    rest, refs = (refs[0], refs[1:]) if with_rest else (None, refs)
    outs, (left, sems) = refs[:16], refs[16:]
    copies = stack_copies(left_blocks, left, sems)
    start_all(copies)
    wait_all(copies)
    width = right.shape[1]
    for i, out in enumerate(outs):
        part = left[:, pl.ds(spot(ids, i), 128)]
        out[:, :width] = dot(part, right[...], TN).astype(low)
        if with_rest:
            out[:, width:] = jnp.transpose(rest[:, pl.ds(spot(ids, i), 128)]).astype(low)


SMEM = pl.BlockSpec(memory_space=pltpu.SMEM)
VMEM = pl.BlockSpec(memory_space=pltpu.VMEM)
FAR = pl.BlockSpec(memory_space=pl.ANY)
HBM = pl.BlockSpec(memory_space=pltpu.HBM)


def call(kernel, name, ins, outs, scratch, flops, specs=None, aliases=None, alone=False):
    operands = [value for value, _ in ins]
    moved = sum(a.size * a.dtype.itemsize for a in operands + outs)
    placed = [value for value, spec in ins if spec is VMEM] + scratch
    placed += [out for out, spec in zip(outs, specs or [VMEM] * len(outs)) if spec is VMEM]
    held = sum(
        math.prod(a.shape) * jnp.dtype(a.dtype).itemsize
        for a in placed
        if jnp.issubdtype(a.dtype, jnp.floating)
    )
    return pl.pallas_call(
        kernel,
        out_shape=outs,
        in_specs=[spec for _, spec in ins],
        out_specs=specs or [VMEM] * len(outs),
        scratch_shapes=scratch,
        name=name,
        input_output_aliases=aliases or {},
        compiler_params=pltpu.CompilerParams(vmem_limit_bytes=WHOLE if alone else ROOM + held),
        cost_estimate=pl.CostEstimate(flops=flops, bytes_accessed=moved, transcendentals=0),
    )(*operands)


def shape(rows, columns, dtype):
    return jax.ShapeDtypeStruct((rows, columns), dtype)


def copies_sem(count):
    return pltpu.SemaphoreType.DMA((count,))


def local_sixteen(
    inputs,
    attention_gain,
    query_weight,
    key_weight,
    value_weight,
    query_gain,
    key_gain,
    out_weight,
    feedforward_gain,
    router_weight,
    gate_weight,
    up_weight,
    down_weight,
    routes,
    cotangent,
):
    tok_rows, model_width = inputs.shape
    head_width = query_gain.shape[0]
    top_count = routes.shape[1]
    expert_count = router_weight.shape[1]
    hidden_width = gate_weight.shape[2]
    capacity = tok_rows * top_count * 11 // (expert_count * 8)
    query_cols, key_cols = query_weight.shape[1] // 2, key_weight.shape[1] // 2
    raw_cols = query_cols + 2 * key_cols
    head_count = query_cols // head_width
    place = lax.axis_index("dp")
    core = lax.axis_index("tensor")
    z, y, x = place // 4, (place // 2) % 2, place % 2
    even = z % 2 == 0
    core_id = core.astype(jnp.int32)[None]
    block_ids = jnp.stack(
        [((z - k) % 4) * 4 + (y ^ dy) * 2 + (x ^ dx) for k, dy, dx in BLOCKS]
    ).astype(jnp.int32)
    weight_ids = jnp.stack(
        [(z ^ w) * 4 + (y ^ dy) * 2 + (x ^ dx) for w, dy, dx in BLOCKS]
    ).astype(jnp.int32)

    def halves(values, axis):
        first, second = jnp.split(values, 2, axis=axis)
        return jnp.where(even, first, second), jnp.where(even, second, first)

    def in_order(mine, theirs, axis):
        return jnp.where(
            even,
            jnp.concatenate([mine, theirs], axis=axis),
            jnp.concatenate([theirs, mine], axis=axis),
        )

    chain = Chain()
    numbers = jnp.arange(expert_count, dtype=jnp.int32)
    own_named = jnp.any(routes[:, :, None] == numbers, axis=1)
    mine, theirs = call(
        first_blocks_kernel,
        "first_blocks",
        [((z % 2).astype(jnp.int32)[None], SMEM)]
        + [(a, VMEM) for a in (routes, query_weight, key_weight, value_weight, router_weight)],
        [shape(tok_rows, raw_cols + 128, low)] * 2,
        [pltpu.VMEM((tok_rows, 128), wide)],
        0,
    )
    held = {(0, 0, 0): mine}
    (held[1, 0, 0],) = chain.gather([(held, WEIGHT_ROUNDS[0])], [(theirs, z_pair)])
    inputs_float = inputs.astype(wide)
    normed_attention, attention_back = jax.vjp(rms_scale, inputs_float, attention_gain)
    normed = normed_attention.astype(low)
    chain.add(normed)
    chain.gather([(held, WEIGHT_ROUNDS[1])])
    chain.gather([(held, WEIGHT_ROUNDS[2])])
    far, swapped = chain.gather(
        [(held, WEIGHT_ROUNDS[3])], [(normed, z_pair), (normed, core_swap)]
    )
    out_mine, out_theirs = halves(out_weight, 0)
    out_held = {(0, 0, 0): out_mine}
    cot_held = {(0, 0, 0): cotangent}
    far_swapped, out_held[1, 0, 0] = chain.gather(
        [(held, WEIGHT_ROUNDS[4]), (out_held, SHORT_ROUNDS[0])],
        [(far, core_swap), (out_theirs, z_pair)],
    )
    sequence = [normed, swapped, far, far_swapped]
    blocks = [held[b] for b in BLOCKS]
    chain.gather([(out_held, SHORT_ROUNDS[1])])
    grad_output = cotangent.astype(wide)
    length = 2 * tok_rows
    own_places = jnp.arange(tok_rows, dtype=jnp.int32)
    places = jnp.concatenate([own_places + core * tok_rows, own_places + (1 - core) * tok_rows])
    halfway = head_width // 2
    frequency = THETA ** (-(jnp.arange(halfway, dtype=wide) * 2.0 / head_width))
    angles = places.astype(wide)[:, None] * frequency[None, :]
    cosine, sine = jnp.cos(angles), jnp.sin(angles)
    turns = [
        (jnp.concatenate([cosine, cosine], axis=1), VMEM),
        (jnp.concatenate([-sine, sine], axis=1), VMEM),
        (query_gain[None, :], VMEM),
        (key_gain[None, :], VMEM),
    ]
    both = 2 * length
    raw, router_rows, rest_rows = call(
        raw_kernel,
        "attention_raw",
        [(weight_ids, SMEM), (block_ids, SMEM)]
        + [(b, FAR) for b in sequence]
        + [(b, HBM) for b in blocks],
        [
            shape(both, raw_cols, wide),
            shape(model_width, 128, low),
            shape(model_width, 128, low),
        ],
        [
            pltpu.VMEM((model_width, raw_cols + 128), low),
            pltpu.VMEM((both, model_width), low),
            copies_sem(20),
        ],
        2 * both * model_width * raw_cols,
        alone=True,
    )
    chain.add(raw)
    chain.gather([(out_held, SHORT_ROUNDS[2])])
    (attended,) = call(
        functools.partial(forward_kernel, head_count),
        "attention_forward",
        [(core_id, SMEM), (raw, VMEM)] + turns,
        [shape(both, query_cols, low)],
        [],
        4 * both * length * query_cols,
    )
    chain.add(attended)
    chain.gather([(out_held, SHORT_ROUNDS[3])])
    out_blocks = [out_held[b] for b in BLOCKS]
    chain.gather([(cot_held, TOKEN_ROUNDS[0])])
    sent, kept = call(
        out_kernel,
        "attention_out",
        [(weight_ids, SMEM), (attended, VMEM)] + [(b, HBM) for b in out_blocks],
        [shape(length, model_width, low), shape(length, model_width, wide)],
        [pltpu.VMEM((query_cols, model_width), low), copies_sem(16)],
        2 * both * model_width * query_cols,
    )

    pair_total = kept + core_swap(sent).astype(wide)
    leaving = pair_total[tok_rows:].astype(low)
    from_pair = z_pair(leaving)
    chain.add(leaving)
    chain.gather([(cot_held, TOKEN_ROUNDS[1])])
    chain.gather([(cot_held, TOKEN_ROUNDS[2])])
    hidden = inputs_float + pair_total[:tok_rows] + from_pair.astype(wide)
    normed_experts, experts_back = jax.vjp(rms_scale, hidden, feedforward_gain)
    moe_in = normed_experts.astype(low)
    chain.add(moe_in)

    token_held = {(0, 0, 0): moe_in}
    chain.gather([(token_held, TOKEN_ROUNDS[0])])
    chain.gather([(token_held, TOKEN_ROUNDS[1])])
    slot_rows = 4 * capacity
    quad_rows = 4 * tok_rows
    rows_of = 2 * slot_rows
    all_slots = 4 * rows_of
    experts = jnp.stack([place * 2 + core, place * 2 + 1 - core]).astype(jnp.int32)
    w_gate, w_up, w_down = gate_weight[0], up_weight[0], down_weight[0]
    turned_width = -(-rows_of // 128) * 128
    picks, turned_picks = call(
        functools.partial(map_kernel, capacity, expert_count),
        "pick_maps",
        [(experts, SMEM), (rest_rows, VMEM)],
        [shape(all_slots, quad_rows, low), shape(model_width, turned_width, low)],
        [],
        2 * 128 * 128 * model_width,
    )

    logits = jnp.dot(moe_in, router_rows, preferred_element_type=wide)[:, :expert_count]
    lifted = jnp.where(own_named, logits, -1e30)
    lifted = jnp.where(own_named, jnp.exp(lifted - jnp.max(lifted, axis=1, keepdims=True)), 0.0)
    gate_dense = lifted / jnp.sum(lifted, axis=1, keepdims=True)

    full = 2 * model_width + 128

    def pick_tokens(k, *earlier):
        return call(
            functools.partial(pick_kernel, k),
            "picks",
            [(after(picks, *earlier), FAR), (rest_rows, FAR)]
            + [(token_held[k, dy, dx], FAR) for dy, dx in PLANE]
            + [(cot_held[k, dy, dx], HBM) for dy, dx in PLANE],
            [shape(slot_rows, full, low)] * 2,
            [
                pltpu.VMEM((rows_of, quad_rows), low),
                pltpu.VMEM((quad_rows, full), low),
                copies_sem(10),
            ],
            2 * rows_of * quad_rows * full,
            alone=k == 0,
        )

    stores = []

    def run_experts(k, own, back):
        ins = (
            [(experts, SMEM), (router_rows, VMEM), (own, FAR), (back, FAR)]
            + [(w, HBM) for w in (w_gate, w_up, w_down)]
        )
        made = call(
            functools.partial(expert_kernel, expert_count, k),
            "experts",
            ins + [(store, HBM) for store in stores],
            [
                shape(all_slots, model_width, low),
                shape(all_slots, hidden_width, low),
                shape(all_slots, model_width, low),
                shape(all_slots, hidden_width, low),
                shape(all_slots, hidden_width, low),
                shape(slot_rows, full, low),
                shape(slot_rows, full, low),
            ],
            [
                pltpu.VMEM((rows_of, full), low),
                pltpu.VMEM((model_width, hidden_width), low),
                pltpu.VMEM((model_width, hidden_width), low),
                pltpu.VMEM((hidden_width, model_width), low),
                pltpu.VMEM((rows_of, hidden_width), low),
                pltpu.VMEM((rows_of, model_width), low),
                pltpu.VMEM((rows_of, hidden_width), low),
                pltpu.VMEM((rows_of, hidden_width), low),
                pltpu.VMEM((rows_of, hidden_width), wide),
                pltpu.VMEM((rows_of, hidden_width), wide),
                pltpu.VMEM((rows_of, hidden_width), wide),
                copies_sem(10),
            ],
            12 * rows_of * model_width * hidden_width,
            [HBM] * 5 + [VMEM] * 2,
            {len(ins) + i: i for i in range(len(stores))},
        )
        stores[:] = made[:5]
        return made[5:]

    terms, y_terms = {b: [] for b in BLOCKS}, {}

    def sum_tokens(k, own, back):
        made = call(
            functools.partial(token_sum_kernel, k),
            "token_sums",
            [(turned_picks, FAR), (own, FAR), (back, FAR)],
            [shape(tok_rows, model_width + 128, low)] * 4 + [shape(tok_rows, model_width, low)] * 4,
            [
                pltpu.VMEM((quad_rows, turned_width), low),
                pltpu.VMEM((rows_of, full), low),
                pltpu.VMEM((quad_rows, model_width), low),
                copies_sem(7),
            ],
            2 * rows_of * quad_rows * full,
            [VMEM] * 4 + [HBM] * 4,
        )
        for i, p in enumerate(PLANE):
            terms[(k, *p)].append(made[i])
            y_terms[(k, *p)] = [made[4 + i]]
        return made[0]

    def row_product(left, right, *earlier):
        return lax.dot_general(after(left, *earlier), right, TN, preferred_element_type=wide)[None]

    own, other = pick_tokens(0)
    chain.add(other)
    (back,) = chain.gather([(token_held, TOKEN_ROUNDS[2])], [(other, core_swap)])
    own, sent = run_experts(0, own, back)
    chain.add(sent)
    (back,) = chain.gather([(token_held, TOKEN_ROUNDS[3])], [(sent, core_swap)])
    summed = sum_tokens(0, own, back)
    chain.gather([(cot_held, TOKEN_ROUNDS[3])])
    own, other = pick_tokens(1, summed)
    (back,) = chain.gather([(token_held, TOKEN_ROUNDS[4])], [(other, core_swap)])
    own, sent = run_experts(1, own, back)
    chain.add(own)
    chain.gather([(cot_held, TOKEN_ROUNDS[4])])
    own_two, other_two = pick_tokens(2, sent)
    back, back_two = chain.send([sent, other_two], [core_swap] * 2)
    sum_tokens(1, own, back)
    chain.scatter([(terms, RETURN_ROUNDS[0])])
    own, sent = run_experts(2, own_two, after(back_two, *chain.values))
    own_three, other_three = pick_tokens(3, sent)
    back, back_three = chain.send([sent, other_three], [core_swap] * 2)
    sum_tokens(2, own, back)
    chain.scatter([(terms, RETURN_ROUNDS[1])])
    own, sent = run_experts(3, own_three, back_three)
    all_rows, all_act, all_grads, all_gate, all_up = stores
    (back,) = chain.send([sent], [core_swap])
    sum_tokens(3, own, back)
    weight_grads = []
    for moves, pair in zip(
        RETURN_ROUNDS[2:], ((all_act, all_grads), (all_rows, all_gate), (all_rows, all_up))
    ):
        chain.scatter([(terms, moves)])
        weight_grads.append(row_product(*pair, *chain.values))
        chain.add(weight_grads[-1])
    grad_down, grad_gate, grad_up = weight_grads

    summed = plus(*terms[0, 0, 0])
    gate_parts = summed[:, model_width:]
    grad_gates = gate_parts[:, :expert_count] + gate_parts[:, expert_count : 2 * expert_count]
    grad_logits = gate_dense * (
        grad_gates - jnp.sum(gate_dense * grad_gates, axis=1, keepdims=True)
    )
    router_wide = router_rows[:, :expert_count].astype(wide)
    grad_moe_in = summed[:, :model_width] + jnp.einsum(
        "te,de->td", grad_logits, router_wide, precision=HIGH
    )

    grad_hidden_norm, grad_feed_gain = experts_back(grad_moe_in)
    grad_hidden = grad_output + grad_hidden_norm
    grad_own = grad_hidden.astype(low)
    chain.scatter([(y_terms, OUTPUT_ROUNDS[0])])
    chain.add(grad_own)
    far, swapped = chain.scatter(
        [(y_terms, OUTPUT_ROUNDS[1])], [(grad_own, z_pair), (grad_own, core_swap)]
    )

    grad_router = jnp.einsum(
        "td,te->ed", moe_in.astype(wide), after(grad_logits, grad_own), precision=HIGH
    )
    (far_swapped,) = chain.scatter([(y_terms, OUTPUT_ROUNDS[2])], [(far, core_swap)])
    grad_branch = [grad_own, swapped, far, far_swapped]

    def block_products(left_blocks, right, rest, name):
        width = right.shape[1] + (0 if rest is None else 128)
        return call(
            functools.partial(block_product_kernel, rest is not None),
            name,
            [(weight_ids, SMEM), (right, VMEM)]
            + [(b, FAR) for b in left_blocks]
            + ([] if rest is None else [(rest, VMEM)]),
            [shape(tok_rows, width, low)] * 16,
            [pltpu.VMEM((both, model_width), low), copies_sem(4)],
            2 * both * model_width * right.shape[1],
        )

    out_products = block_products(grad_branch, attended, None, "out_weight_grad")
    out_terms = {b: [block] for b, block in zip(BLOCKS, out_products)}
    chain.add(out_products[0])
    (router_part,) = chain.scatter(
        [(y_terms, OUTPUT_ROUNDS[3]), (out_terms, WEIGHT_RETURNS[0])],
        [(grad_router, core_swap)],
        out_products[0],
    )
    grad_router = grad_router + router_part
    (grad_attended,) = call(
        attended_grad_kernel,
        "attended_grad",
        [(weight_ids, SMEM)]
        + [(b, FAR) for b in (after(grad_branch[0], out_products[0]), *grad_branch[1:])]
        + [(b, HBM) for b in out_blocks],
        [shape(both, query_cols, low)],
        [
            pltpu.VMEM((both, model_width), low),
            pltpu.VMEM((query_cols, model_width), low),
            copies_sem(20),
        ],
        2 * both * model_width * query_cols,
    )
    chain.add(grad_attended)
    (router_part,) = chain.scatter(
        [(out_terms, WEIGHT_RETURNS[1]), (y_terms, OUTPUT_ROUNDS[4])], [(grad_router, z_pair)]
    )
    grad_rest = jnp.pad(grad_router + router_part, ((0, 128 - expert_count), (0, 0)))
    grad_raw, query_gain_grad, key_gain_grad = call(
        functools.partial(backward_kernel, head_count),
        "attention_backward",
        [(core_id, SMEM), (raw, VMEM), (after(grad_attended, *chain.values), VMEM)] + turns,
        [shape(both, raw_cols, low), shape(1, head_width, wide), shape(1, head_width, wide)],
        [pltpu.VMEM((length, head_width), wide), pltpu.VMEM((length, head_width), wide)],
        10 * both * length * query_cols,
    )
    chain.add(grad_raw)
    chain.scatter([(out_terms, WEIGHT_RETURNS[2])])
    raw_products = block_products(
        sequence, after(grad_raw, *chain.values), grad_rest, "raw_weight_grad"
    )
    raw_terms = {b: [block] for b, block in zip(BLOCKS, raw_products)}
    chain.add(raw_products[0])
    chain.scatter([(raw_terms, WEIGHT_RETURNS[0]), (y_terms, OUTPUT_ROUNDS[5])])
    sent, kept, attention_part = call(
        normed_grad_kernel,
        "normed_grad",
        [
            (weight_ids, SMEM),
            (after(grad_raw, *chain.values), VMEM),
            (attention_gain[None, :], VMEM),
        ]
        + [(b, FAR) for b in sequence]
        + [(b, HBM) for b in blocks],
        [
            shape(length, model_width, low),
            shape(length, model_width, wide),
            shape(1, model_width, wide),
        ],
        [
            pltpu.VMEM((model_width, raw_cols + 128), low),
            pltpu.VMEM((both, model_width), low),
            copies_sem(20),
        ],
        2 * both * model_width * raw_cols,
    )
    chain.add(kept)
    gains = jnp.concatenate(
        [attention_part[0], grad_feed_gain, query_gain_grad[0], key_gain_grad[0]]
    ).reshape(-1, head_width)
    gains = gains + core_swap(gains)
    (from_core,) = chain.scatter([(out_terms, WEIGHT_RETURNS[3])], [(sent, core_swap)])
    pair_total = kept + from_core.astype(wide)
    from_pair, gain_part = chain.scatter(
        [(raw_terms, WEIGHT_RETURNS[1])],
        [(pair_total[tok_rows:].astype(low), z_pair), (gains, x_swap)],
    )
    gains = gains + gain_part
    (gain_part,) = chain.scatter([(raw_terms, WEIGHT_RETURNS[2])], [(gains, y_swap)])
    grad_normed = pair_total[:tok_rows] + from_pair.astype(wide)
    grad_inputs_norm, _ = attention_back(grad_normed)
    grad_inputs = grad_hidden + grad_inputs_norm
    chain.add(grad_inputs)
    gains = gains + gain_part
    (gain_part,) = chain.scatter([(raw_terms, WEIGHT_RETURNS[3])], [(gains, z_pair)])
    gains = gains + gain_part
    theirs = jnp.concatenate([plus(*t[1, 0, 0]).astype(low) for t in (out_terms, raw_terms)], axis=1)
    theirs, gain_part = chain.scatter(
        [(raw_terms, WEIGHT_RETURNS[4]), (out_terms, WEIGHT_RETURNS[4])],
        [(theirs, z_pair), (gains, z_far)],
    )
    out_theirs, raw_theirs = theirs[:, :query_cols], theirs[:, query_cols:]
    gains = (gains + gain_part).reshape(-1)
    output = (hidden + plus(*y_terms[0, 0, 0])).astype(low)
    grad_out_weight = in_order(plus(*out_terms[0, 0, 0]), out_theirs.astype(wide), 1).T
    mine, theirs = plus(*raw_terms[0, 0, 0]), raw_theirs.astype(wide)
    spans = ((0, query_cols), (query_cols, query_cols + key_cols), (query_cols + key_cols, raw_cols))
    grad_query_weight, grad_key_weight, grad_value_weight = [
        in_order(mine[:, a:b], theirs[:, a:b], 1) for a, b in spans
    ]
    router_share = mine[:, raw_cols : raw_cols + expert_count]
    return (
        output,
        grad_inputs,
        gains[:model_width],
        grad_query_weight,
        grad_key_weight,
        grad_value_weight,
        gains[2 * model_width : 2 * model_width + head_width],
        gains[2 * model_width + head_width :],
        grad_out_weight,
        gains[model_width : 2 * model_width],
        router_share,
        grad_gate,
        grad_up,
        grad_down,
    )


def solution(mesh):
    in_specs = (
        P(("dp", "tensor"), None),
        P(),
        P("dp", "tensor"),
        P("dp", "tensor"),
        P("dp", "tensor"),
        P(),
        P(),
        P("tensor", "dp"),
        P(),
        P("dp", None),
        P(("dp", "tensor"), None, None),
        P(("dp", "tensor"), None, None),
        P(("dp", "tensor"), None, None),
        P(("dp", "tensor"), None),
        P(("dp", "tensor"), None),
    )
    out_specs = (
        P(("dp", "tensor"), None),
        P(("dp", "tensor"), None),
        P(),
        P("dp", "tensor"),
        P("dp", "tensor"),
        P("dp", "tensor"),
        P(),
        P(),
        P("tensor", "dp"),
        P(),
        P("dp", None),
        P(("dp", "tensor"), None, None),
        P(("dp", "tensor"), None, None),
        P(("dp", "tensor"), None, None),
    )
    fits = mesh.shape["dp"] == 16 and mesh.shape["tensor"] == 2
    local = local_sixteen if fits else local_any
    return jax.shard_map(local, mesh=mesh, in_specs=in_specs, out_specs=out_specs, check_vma=False)
```
